256 devices in a mesh: grp: 16 (over y_hi, z), tp: 16 (over y_lo, x, core).
Axes of the slice: x: 4, y: 4 (y_hi: 2, y_lo: 2; y = y_hi * 2 + y_lo), z: 8, core: 2. Of those that a mesh axis runs over, the one named last changes fastest.
Arguments:
- attention_output: bfloat16 [8192, 8192], P('grp', 'tp'), parts along dimension 0, may hold values from -6 to 6
- output_projection_weight: bfloat16 [8192, 8192], P('tp'), may hold values from -0.0625 to 0.0625
- residual: bfloat16 [512, 131072], P('tp', 'grp'), parts along dimension 1, may hold values from -6 to 6
- resident_down_maps: bfloat16 [8192, 16384], P('tp', 'grp'), parts along dimension 1, may hold values from -0.0625 to 0.0625
- resident_up_maps: bfloat16 [16384, 8192], P('grp', 'tp'), parts along dimension 0, may hold values from -0.75 to 0.75
- fresh_adapter_bundle: bfloat16 [256, 4096, 128], P(('grp', 'tp')), parts along dimension 0, as said below
- fresh_slot_targets: int32 [256], P('grp'), parts along dimension 0, may hold values from 0 to 15, each once
- request_adapter_slot: int32 [8192], P('grp'), parts along dimension 0, may hold values from 0 to 15
Outputs:
- hidden: bfloat16 [512, 131072], P('tp', 'grp'), parts along dimension 1
The draws below stay inside these ranges and needn't reach their ends.
There are 16 independent parts, one for each index of `grp`. The reference program is written for one: setup_inputs(seed, part) draws one part's arguments, and reference() takes and returns one part's arrays. A program takes and returns all parts, laid end to end along the dimension named above; an argument that names none is the same for every part. Nothing has to cross between parts.
Inputs may be any that keep to these rules, and one draw needn't show every extreme that they name: `fresh_adapter_bundle`: entries 2k hold down maps of deviation about 8192 ** -0.5, entries 2k + 1 up maps of deviation about 64 ** -0.5.
All inputs are finite; a program needn't handle non-finite values.
Results may differ from the reference program's by a relative error of at most 0.0055.
Values may be sent and summed in bfloat16 or wider, within the bound.
No kernel may reach another device: no remote copies, remote signals or barrier semaphores. Data moves between devices by JAX's collectives and lax.ppermute only.
A program may use at most 128 MiB of HBM per device.

```python
import jax
import jax.numpy as jnp

MODEL_WIDTH = 8192
ADAPTER_RANK = 64
GROUP_SLOTS = 16
ROWS = 512
NEW = 8


def draw_fresh_adapter_bundle(key, part):
    key = jax.random.fold_in(key, 11)
    values = jax.random.normal(key, (2 * NEW, MODEL_WIDTH // 2, 2 * ADAPTER_RANK), jnp.float32)
    parity = jnp.arange(2 * NEW, dtype=jnp.int32) % 2
    factor = jnp.where(parity == 0, MODEL_WIDTH ** (-0.5), ADAPTER_RANK ** (-0.5)).astype(jnp.float32)
    return (values * factor[:, None, None]).astype(jnp.bfloat16)


def set_ends(result, rng, least, high):
    longest = result.shape.index(max(result.shape))
    spots = []
    for shift in (0, 1):
        where = [jax.random.randint(jax.random.fold_in(rng, axis), (), 0, length) for axis, length in enumerate(result.shape)]
        where[longest] = (where[longest] + shift) % result.shape[longest]
        spots.append(tuple(where))
    return result.at[spots[0]].set(least).at[spots[1]].set(high)


def block_scale(rng, shape, shards, smallest, top_value):
    loudness, own = 1.0, jax.random.fold_in(rng, 6)
    for dim, parts in shards:
        steps = jnp.exp(jax.random.uniform(jax.random.fold_in(own, dim), (parts,), jnp.float32, smallest / len(shards), top_value / len(shards)))
        loudness = loudness * jnp.repeat(steps, shape[dim] // parts).reshape([-1 if axis == dim else 1 for axis in range(len(shape))])
    return loudness


def noise(stream_key, dims, width, most, split=(), held_as=jnp.bfloat16):
    gain = block_scale(stream_key, dims, split, -0.22, 0.18) if split else 1.0
    result = jax.random.normal(stream_key, dims, jnp.float32) * width * gain
    return jnp.minimum(jnp.maximum(result, -most), most).astype(held_as)


def setup_inputs(seed: int = 0, part: int = 0) -> dict:
    splits = jax.random.split(jax.random.key(seed), 9)
    own_keys = jax.random.split(jax.random.fold_in(splits[8], part), 9)
    return {
        "attention_output": noise(own_keys[0], (ROWS, MODEL_WIDTH), 1.0, 6.0, ((1, 16),)),
        "output_projection_weight": noise(splits[1], (MODEL_WIDTH, MODEL_WIDTH), MODEL_WIDTH ** -0.5, 0.0625, ((0, 16),)),
        "residual": noise(own_keys[2], (ROWS, MODEL_WIDTH), 1.0, 6.0, ((0, 16),)),
        "resident_down_maps": noise(own_keys[3], (MODEL_WIDTH, GROUP_SLOTS * ADAPTER_RANK), MODEL_WIDTH ** -0.5, 0.0625, ((0, 16),)),
        "resident_up_maps": noise(own_keys[4], (GROUP_SLOTS * ADAPTER_RANK, MODEL_WIDTH), ADAPTER_RANK ** -0.5, 0.75, ((1, 16),)),
        "fresh_adapter_bundle": draw_fresh_adapter_bundle(jax.random.fold_in(jax.random.fold_in(splits[8], part), 71), part),
        "fresh_slot_targets": jax.random.permutation(own_keys[6], GROUP_SLOTS).astype(jnp.int32),
        "request_adapter_slot": set_ends(jax.random.randint(own_keys[7], (ROWS,), 0, GROUP_SLOTS), jax.random.fold_in(own_keys[7], 1), 0, GROUP_SLOTS - 1).astype(jnp.int32),
    }


adapter_scale = 0.5


def reference(attention_output, output_projection_weight, residual, resident_down_maps, resident_up_maps, fresh_adapter_bundle, fresh_slot_targets, request_adapter_slot):
    adapter_matrices = fresh_adapter_bundle.reshape(2 * NEW, MODEL_WIDTH, ADAPTER_RANK)
    picked_adapters = fresh_slot_targets[:NEW]
    down_map_table = resident_down_maps.reshape(MODEL_WIDTH, GROUP_SLOTS, ADAPTER_RANK).at[:, picked_adapters, :].set(jnp.transpose(adapter_matrices[0::2], (1, 0, 2)))
    up_map_table = resident_up_maps.reshape(GROUP_SLOTS, ADAPTER_RANK, MODEL_WIDTH).at[picked_adapters].set(jnp.transpose(adapter_matrices[1::2], (0, 2, 1)))
    shrink_wide = jnp.dot(attention_output, down_map_table.reshape(MODEL_WIDTH, GROUP_SLOTS * ADAPTER_RANK), preferred_element_type=jnp.float32)
    onehot = (request_adapter_slot[:, None] == jnp.arange(GROUP_SLOTS, dtype=jnp.int32)[None, :]).astype(jnp.float32)
    shrink = jnp.sum(shrink_wide.reshape(ROWS, GROUP_SLOTS, ADAPTER_RANK) * onehot[:, :, None], axis=1).astype(jnp.bfloat16)
    raised_features = (shrink[:, None, :] * onehot.astype(jnp.bfloat16)[:, :, None]).reshape(ROWS, GROUP_SLOTS * ADAPTER_RANK)
    adapter_update = adapter_scale * jnp.dot(raised_features, up_map_table.reshape(GROUP_SLOTS * ADAPTER_RANK, MODEL_WIDTH), preferred_element_type=jnp.float32)
    base_part = jnp.dot(attention_output, output_projection_weight, preferred_element_type=jnp.float32)
    return (residual.astype(jnp.float32) + base_part + adapter_update).astype(jnp.bfloat16)
```

```python
import jax
import jax.numpy as jnp
from jax import lax
from jax.experimental import pallas as pl
from jax.experimental.pallas import tpu as pltpu
from jax.sharding import PartitionSpec as P

RANK = 64
SLOTS = 16
CHIPS = 8
SCALE = 0.5
F32 = jnp.float32
BF16 = jnp.bfloat16
WIDE = 4608
TILE = 512
VMEM_LIMIT = 40 * 1024 * 1024


def place(y, x, core):
    return ((y % 2) * 4 + x % 4) * 2 + core % 2


def route(yy, xx, cc):
    return [
        (place(y, x, c), place(y + yy, x + xx, c + cc))
        for y in range(2)
        for x in range(4)
        for c in range(2)
    ]


def send(array, yy, xx, cc):
    return lax.ppermute(array, "tp", route(yy, xx, cc))


def spot():
    t = lax.axis_index("tp")
    return t // 8, lax.rem(t // 2, 4), lax.rem(t, 2)


def partner(yy, xx, cc):
    y, x, c = spot()
    return (lax.rem(y + yy, 2) * 4 + lax.rem(x + xx, 4)) * 2 + lax.rem(c + cc, 2)


def rows_at(index, size):
    return pl.ds(pl.multiple_of(index * size, size), size)


def whole(shape, dtype):
    return jax.ShapeDtypeStruct(shape, dtype)


def params():
    return pltpu.CompilerParams(vmem_limit_bytes=VMEM_LIMIT)


OFFSETS = [(yy, xx, cc) for yy in range(2) for xx in range(4) for cc in range(2)]


def cut_kernel(bundle_ref, *out_refs):
    for offset, out in zip(OFFSETS, out_refs):
        out[...] = bundle_ref[0, rows_at(partner(*offset), 256), :]


def cut_bundle(bundle):
    return pl.pallas_call(
        cut_kernel,
        out_shape=[whole((256, 128), BF16)] * 16,
        compiler_params=params(),
        name="cut_bundle",
    )(bundle)


def product_kernel(order, cc, x_ref, w_ref, out_ref, rows_ref):
    @pl.when(pl.program_id(0) == 0)
    def _():
        for i, (yy, xx) in enumerate(order):
            rows_ref[i * 32 : (i + 1) * 32, :] = x_ref[rows_at(partner(yy, xx, cc), 32), :]

    out_ref[...] = jnp.dot(rows_ref[...], w_ref[...], preferred_element_type=F32).astype(BF16)


X_MAJOR = [(yy, xx) for xx in range(4) for yy in range(2)]
Y_MAJOR = [(yy, xx) for yy in range(2) for xx in range(4)]


def product(x, w, order, cc, first, width):
    def body(*refs):
        product_kernel(order, cc, *refs)

    return pl.pallas_call(
        body,
        grid=(width // TILE,),
        in_specs=[
            pl.BlockSpec((512, 512), lambda j: (0, 0)),
            pl.BlockSpec((512, TILE), lambda j: (0, first // TILE + j)),
        ],
        out_specs=pl.BlockSpec((256, TILE), lambda j: (0, j)),
        out_shape=whole((256, width), BF16),
        scratch_shapes=[pltpu.VMEM((256, 512), BF16)],
        compiler_params=params(),
        cost_estimate=pl.CostEstimate(
            flops=2 * 256 * 512 * width, bytes_accessed=(512 + 256) * width * 2, transcendentals=0
        ),
        name="product",
    )(x, w)


def lanes(rows):
    return lax.broadcasted_iota(jnp.int32, (rows, 128), 1)


def resident_slot(slot, target_ref):
    for k in range(CHIPS):
        slot = jnp.where(slot == target_ref[k], -1, slot)
    return slot


def shrink_resident_kernel(x_ref, down_ref, slot_ref, target_ref, acc_ref, split_ref):
    x = x_ref[...]
    row = lax.broadcasted_iota(jnp.int32, (512, 512), 0)
    col = lax.broadcasted_iota(jnp.int32, (512, 512), 1)
    source = jnp.where(col < 256, 2 * col, 2 * (col - 256) + 1)
    chooser = jnp.where(row == source, 1.0, 0.0).astype(BF16)
    split_ref[...] = jnp.dot(x, chooser, preferred_element_type=F32).astype(BF16)
    slot = jnp.broadcast_to(resident_slot(slot_ref[...], target_ref), (512, 128))
    high = (lanes(512) >= RANK).astype(jnp.int32)
    acc = jnp.zeros((512, 128), F32)
    for j in range(CHIPS):
        part = jnp.dot(x, down_ref[:, j * 128 : (j + 1) * 128], preferred_element_type=F32)
        acc += jnp.where(slot == 2 * j + high, part, 0.0)
    acc_ref[...] = acc


def shrink_resident(x, down, slot, target):
    vm = pl.BlockSpec(memory_space=pltpu.VMEM)
    return pl.pallas_call(
        shrink_resident_kernel,
        in_specs=[vm, vm, vm, pl.BlockSpec(memory_space=pltpu.SMEM)],
        out_shape=[whole((512, 128), F32), whole((512, 512), BF16)],
        compiler_params=params(),
        name="shrink_resident",
    )(x, down, slot, target)


CHIP_OFFSETS = [(yy, xx) for yy in range(2) for xx in range(4)]


def source_chip(yy, xx):
    y, x, _ = spot()
    return lax.rem(y + 2 - yy, 2) * 4 + lax.rem(x + 4 - xx, 4)


def shrink_fresh_kernel(split_ref, acc_ref, slot_ref, target_ref, *refs):
    same, cross, out_ref = refs[:8], refs[8:16], refs[16]
    _, _, core = spot()
    even, odd = split_ref[:, :256], split_ref[:, 256:]
    slot = jnp.broadcast_to(slot_ref[...], (512, 128))
    low = lanes(512) < RANK
    acc = acc_ref[...]
    for i, offset in enumerate(CHIP_OFFSETS):
        maps = jnp.where(core == 0, same[i][...], cross[i][...])
        part = jnp.where(
            low,
            jnp.dot(even, maps, preferred_element_type=F32),
            jnp.dot(odd, maps, preferred_element_type=F32),
        )
        acc += jnp.where(slot == target_ref[source_chip(*offset)], part, 0.0)
    acc = acc + pltpu.roll(acc, RANK, 1)
    out_ref[...] = jnp.where(lanes(256) < RANK, acc[:256], acc[256:]).astype(BF16)


def shrink_fresh(split, acc, slot, target, same, cross):
    vm = pl.BlockSpec(memory_space=pltpu.VMEM)
    return pl.pallas_call(
        shrink_fresh_kernel,
        in_specs=[vm, vm, vm, pl.BlockSpec(memory_space=pltpu.SMEM)] + [vm] * 16,
        out_shape=whole((256, 128), BF16),
        compiler_params=params(),
        name="shrink_fresh",
    )(split, acc, slot, target, *same, *cross)


def raise_kernel(mine_ref, other_ref, up_ref, slot_ref, target_ref, *refs):
    same, cross, outs = refs[:8], refs[8:16], refs[16:]
    _, _, core = spot()
    packed = (mine_ref[...].astype(F32) + other_ref[...].astype(F32)).astype(BF16).astype(F32)
    turned = pltpu.roll(packed, RANK, 1)
    left = lanes(256) < RANK
    both = jnp.concatenate(
        [jnp.where(left, packed, turned), jnp.where(left, turned, packed)], axis=0
    )
    slot = jnp.broadcast_to(slot_ref[...], (512, 128))
    kept = resident_slot(slot, target_ref)
    high = (lanes(512) >= RANK).astype(jnp.int32)
    total = jnp.zeros((512, 512), F32)
    for j in range(CHIPS):
        raised = jnp.where(kept == 2 * j + high, both, 0.0).astype(BF16)
        total += jnp.dot(raised, up_ref[j * 128 : (j + 1) * 128, :], preferred_element_type=F32)
    even = jnp.zeros((512, 256), F32)
    odd = jnp.zeros((512, 256), F32)
    turn = (((1,), (1,)), ((), ()))
    for i, offset in enumerate(CHIP_OFFSETS):
        maps = jnp.where(core == 0, cross[i][...], same[i][...])
        fresh = jnp.where(slot == target_ref[source_chip(*offset)], both, 0.0)
        even += lax.dot_general(
            jnp.where(high == 0, fresh, 0.0).astype(BF16), maps, turn, preferred_element_type=F32
        )
        odd += lax.dot_general(
            jnp.where(high == 1, fresh, 0.0).astype(BF16), maps, turn, preferred_element_type=F32
        )
    row = lax.broadcasted_iota(jnp.int32, (256, 512), 0)
    col = lax.broadcasted_iota(jnp.int32, (256, 512), 1)
    to_even = jnp.where(col == 2 * row, 1.0, 0.0).astype(BF16)
    to_odd = jnp.where(col == 2 * row + 1, 1.0, 0.0).astype(BF16)
    total += jnp.dot(even.astype(BF16), to_even, preferred_element_type=F32)
    total += jnp.dot(odd.astype(BF16), to_odd, preferred_element_type=F32)
    scaled = (SCALE * total).astype(BF16)
    outs[16][...] = scaled
    for offset, out in zip(OFFSETS, outs[:16]):
        out[...] = outs[16][rows_at(partner(*offset), 32), :]


def raise_features(mine, other, up, slot, target, same, cross):
    vm = pl.BlockSpec(memory_space=pltpu.VMEM)

    def body(*refs):
        raise_kernel(*refs)

    return pl.pallas_call(
        body,
        in_specs=[vm, vm, vm, vm, pl.BlockSpec(memory_space=pltpu.SMEM)] + [vm] * 16,
        out_shape=[whole((32, 512), BF16)] * 16,
        scratch_shapes=[pltpu.VMEM((512, 512), BF16)],
        compiler_params=params(),
        name="raise_features",
    )(mine, other, up, slot, target, *same, *cross)


def finish_kernel(residual_ref, wide_ref, narrow_ref, *refs):
    deltas, out_ref, held_ref = refs[:16], refs[16], refs[17]
    for offset, delta in zip(OFFSETS, deltas):
        yy, xx, cc = offset
        held_ref[partner(2 - yy, 4 - xx, 2 - cc)] = delta[...]
    for t in range(16):
        cols = slice(t * 512, (t + 1) * 512)
        if (t + 1) * 512 <= WIDE:
            base = wide_ref[:, cols]
        else:
            base = narrow_ref[:, t * 512 - WIDE : (t + 1) * 512 - WIDE]
        out_ref[:, cols] = (
            residual_ref[:, cols].astype(F32) + base + held_ref[t].astype(F32)
        ).astype(BF16)


def finish(residual, wide, narrow, deltas):
    return pl.pallas_call(
        finish_kernel,
        out_shape=whole((32, 8192), BF16),
        scratch_shapes=[pltpu.VMEM((16, 32, 512), BF16)],
        compiler_params=params(),
        name="finish",
    )(residual, wide, narrow, *deltas)


def plus(a, *others):
    total = a.astype(F32)
    for other in others:
        total = total + other.astype(F32)
    return total


def along_x(blocks, rows):
    half = blocks.shape[1] // 2

    def block(d, side):
        return blocks[d * rows : (d + 1) * rows, side * half : (side + 1) * half]

    far_right = send(block(2, 0), 0, 1, 0)
    far_left = send(block(2, 1), 0, 3, 0)
    near_right = send(block(1, 1), 0, 1, 0)
    near_left = send(block(3, 0), 0, 3, 0)
    sum_right = send(plus(block(1, 0), far_right).astype(BF16), 0, 1, 0)
    sum_left = send(plus(block(3, 1), far_left).astype(BF16), 0, 3, 0)
    return jnp.concatenate(
        [plus(block(0, 0), near_left, sum_right), plus(block(0, 1), near_right, sum_left)], axis=1
    )


def local(
    attention_output,
    output_projection_weight,
    residual,
    resident_down_maps,
    resident_up_maps,
    fresh_adapter_bundle,
    fresh_slot_targets,
    request_adapter_slot,
):
    x, w = attention_output, output_projection_weight
    slot = request_adapter_slot.reshape(512, 1)
    target = fresh_slot_targets

    pieces = dict(zip(OFFSETS, cut_bundle(fresh_adapter_bundle)))
    landed = {o: (pieces[o] if o == (0, 0, 0) else send(pieces[o], *o)) for o in OFFSETS}
    same = [landed[(yy, xx, 0)] for yy, xx in CHIP_OFFSETS]
    cross = [landed[(yy, xx, 1)] for yy, xx in CHIP_OFFSETS]

    narrow = x.shape[0] * 16 - WIDE
    wide_away = send(product(x, w, X_MAJOR, 1, 0, WIDE), 0, 0, 1)
    narrow_away = send(product(x, w, Y_MAJOR, 1, WIDE, narrow), 0, 0, 1)
    wide_own = product(x, w, X_MAJOR, 0, 0, WIDE)
    narrow_own = product(x, w, Y_MAJOR, 0, WIDE, narrow)
    acc, split = shrink_resident(x, resident_down_maps, slot, target)

    wide_chip = plus(wide_own, wide_away).astype(BF16)
    narrow_chip = plus(narrow_own, narrow_away).astype(BF16)

    narrow_row = plus(narrow_chip[:128], send(narrow_chip[128:], 1, 0, 0)).astype(BF16)
    wide_col = along_x(wide_chip, 64)
    wide_sum = wide_col[:32] + send(wide_col[32:].astype(BF16), 1, 0, 0).astype(F32)
    narrow_sum = along_x(narrow_row, 32)

    part = shrink_fresh(split, acc, slot, target, same, cross)
    part = plus(part, send(part, 0, 0, 1)).astype(BF16)
    part = plus(
        part, send(part, 0, 1, 0), send(part, 0, 2, 0), send(part, 0, 3, 0)
    ).astype(BF16)
    raised = raise_features(
        part, send(part, 1, 0, 0), resident_up_maps, slot, target, same, cross
    )
    raised = dict(zip(OFFSETS, raised))
    deltas = [raised[o] if o == (0, 0, 0) else send(raised[o], *o) for o in OFFSETS]
    return finish(residual, wide_sum, narrow_sum, deltas)


def solution(mesh):
    return jax.shard_map(
        local,
        mesh=mesh,
        in_specs=(
            P("grp", "tp"),
            P("tp", None),
            P("tp", "grp"),
            P("tp", "grp"),
            P("grp", "tp"),
            P(("grp", "tp"), None, None),
            P("grp"),
            P("grp"),
        ),
        out_specs=P("tp", "grp"),
        check_vma=False,
    )
```

```python
import jax
import jax.numpy as jnp
from jax import lax
from jax.experimental import pallas as pl
from jax.experimental.pallas import tpu as pltpu
from jax.sharding import PartitionSpec as P

RANK = 64
SLOTS = 16
CHIPS = 8
SCALE = 0.5
F32 = jnp.float32
BF16 = jnp.bfloat16
WIDE = 4608
VMEM_LIMIT = 40 * 1024 * 1024
PRODUCT_LIMIT = 56 * 1024 * 1024


def place(y, x, core):
    return ((y % 2) * 4 + x % 4) * 2 + core % 2


def route(yy, xx, cc):
    return [
        (place(y, x, c), place(y + yy, x + xx, c + cc))
        for y in range(2)
        for x in range(4)
        for c in range(2)
    ]


def send(array, yy, xx, cc):
    return lax.ppermute(array, "tp", route(yy, xx, cc))


def spot():
    t = lax.axis_index("tp")
    return t // 8, lax.rem(t // 2, 4), lax.rem(t, 2)


def partner(yy, xx, cc):
    y, x, c = spot()
    return (lax.rem(y + yy, 2) * 4 + lax.rem(x + xx, 4)) * 2 + lax.rem(c + cc, 2)


def rows_at(index, size):
    return pl.ds(pl.multiple_of(index * size, size), size)


def whole(shape, dtype):
    return jax.ShapeDtypeStruct(shape, dtype)


def plus(a, *others):
    total = a.astype(F32)
    for other in others:
        total = total + other.astype(F32)
    return total


VM = pl.BlockSpec(memory_space=pltpu.VMEM)
SM = pl.BlockSpec(memory_space=pltpu.SMEM)
LATER = pl.BlockSpec(memory_space=pl.ANY)


def call(kernel, name, out_shape, args, specs=None, after=(), limit=VMEM_LIMIT, **options):
    count = len(args)

    def body(*refs):
        kernel(*refs[:count], *refs[count + len(after) :])

    return pl.pallas_call(
        body,
        in_specs=list(specs or [VM] * count) + [LATER] * len(after),
        out_shape=out_shape,
        compiler_params=pltpu.CompilerParams(vmem_limit_bytes=limit),
        name=name,
        **options,
    )(*args, *after)


X_MAJOR = [(yy, xx) for xx in range(4) for yy in range(2)]
Y_MAJOR = [(yy, xx) for yy in range(2) for xx in range(4)]


def product(x, w, order, cc, first, width, tile, after=()):
    def kernel(x_ref, w_ref, out_ref, rows_ref):
        @pl.when(pl.program_id(0) == 0)
        def _():
            for i, (yy, xx) in enumerate(order):
                rows_ref[i * 32 : (i + 1) * 32, :] = x_ref[rows_at(partner(yy, xx, cc), 32), :]

        out_ref[...] = jnp.dot(
            rows_ref[...], w_ref[...], preferred_element_type=F32
        ).astype(BF16)

    return call(
        kernel,
        "product",
        whole((256, width), BF16),
        (x, w),
        [
            pl.BlockSpec((512, 512), lambda j: (0, 0)),
            pl.BlockSpec(
                (pl.Element(512), pl.Element(tile)),
                lambda j: (0, (first // 128 + j * (tile // 128)) * 128),
            ),
        ],
        after,
        limit=PRODUCT_LIMIT,
        grid=(width // tile,),
        out_specs=pl.BlockSpec((256, tile), lambda j: (0, j)),
        scratch_shapes=[pltpu.VMEM((256, 512), BF16)],
    )


def chip_narrow(own, away, after=()):
    width = own.shape[1]
    tile = width // 4

    def kernel(own_ref, away_ref, keep_ref, send_ref):
        total = plus(own_ref[...], away_ref[...]).astype(BF16)
        keep_ref[...] = total[:128]
        send_ref[...] = total[128:]

    piece = pl.BlockSpec((256, tile), lambda j: (0, j))
    half = pl.BlockSpec((128, tile), lambda j: (0, j))
    return call(
        kernel,
        "chip_narrow",
        [whole((128, width), BF16)] * 2,
        (own, away),
        [piece, piece],
        after,
        grid=(4,),
        out_specs=[half, half],
    )


def chip_wide(own, away, after=()):
    width = own.shape[1]
    tile = width // 4

    def kernel(own_ref, away_ref, here_ref, right_ref, left_ref, far_right_ref, far_left_ref):
        j = pl.program_id(0)
        total = plus(own_ref[...], away_ref[...]).astype(BF16)
        here_ref[...] = total[:64]
        right_ref[...] = total[64:128]
        left_ref[...] = total[192:]

        @pl.when(j < 2)
        def _():
            far_right_ref[...] = total[128:192]

        @pl.when(j >= 2)
        def _():
            far_left_ref[...] = total[128:192]

    piece = pl.BlockSpec((256, tile), lambda j: (0, j))
    block = pl.BlockSpec((64, tile), lambda j: (0, j))
    return call(
        kernel,
        "chip_wide",
        [whole((64, width), BF16)] * 3 + [whole((64, width // 2), BF16)] * 2,
        (own, away),
        [piece, piece],
        after,
        grid=(4,),
        out_specs=[block] * 3
        + [
            pl.BlockSpec((64, tile), lambda j: (0, jnp.minimum(j, 1))),
            pl.BlockSpec((64, tile), lambda j: (0, jnp.maximum(j - 2, 0))),
        ],
    )


def turn_narrow(keep, landed, after=()):
    width = keep.shape[1]
    half = width // 2

    def kernel(keep_ref, landed_ref, here_ref, right_ref, left_ref, far_right_ref, far_left_ref):
        total = plus(keep_ref[...], landed_ref[...]).astype(BF16)
        here_ref[...] = total[:32]
        right_ref[...] = total[32:64]
        left_ref[...] = total[96:]
        far_right_ref[...] = total[64:96, :half]
        far_left_ref[...] = total[64:96, half:]

    return call(
        kernel,
        "turn_narrow",
        [whole((32, width), BF16)] * 3 + [whole((32, half), BF16)] * 2,
        (keep, landed),
        after=after,
    )


def near(right, left, far_right, far_left, after=()):
    half = right.shape[1] // 2

    def kernel(right_ref, left_ref, far_right_ref, far_left_ref, to_right_ref, to_left_ref):
        to_right_ref[:, :half] = plus(right_ref[:, :half], far_right_ref[...]).astype(BF16)
        to_right_ref[:, half:] = right_ref[:, half:]
        to_left_ref[:, :half] = left_ref[:, :half]
        to_left_ref[:, half:] = plus(left_ref[:, half:], far_left_ref[...]).astype(BF16)

    return call(
        kernel, "near", [whole(right.shape, BF16)] * 2, (right, left, far_right, far_left), after=after
    )


def turn_wide(here, from_left, from_right, after=()):
    width = here.shape[1]

    def kernel(here_ref, from_left_ref, from_right_ref, keep_ref, send_ref):
        total = plus(here_ref[...], from_left_ref[...], from_right_ref[...])
        keep_ref[...] = total[:32]
        send_ref[...] = total[32:].astype(BF16)

    return call(
        kernel,
        "turn_wide",
        [whole((32, width), F32), whole((32, width), BF16)],
        (here, from_left, from_right),
        after=after,
    )


def add_parts(parts, after=()):
    def kernel(*refs):
        refs[-1][...] = plus(*[ref[...] for ref in refs[:-1]]).astype(BF16)

    return call(kernel, "add_parts", whole(parts[0].shape, BF16), parts, after=after)


def lanes(rows):
    return lax.broadcasted_iota(jnp.int32, (rows, 128), 1)


def resident_slot(slot, target_ref):
    for k in range(CHIPS):
        slot = jnp.where(slot == target_ref[k], -1, slot)
    return slot


def shrink_resident_kernel(x_ref, down_ref, slot_ref, target_ref, acc_ref, split_ref):
    x = x_ref[...]
    row = lax.broadcasted_iota(jnp.int32, (512, 512), 0)
    col = lax.broadcasted_iota(jnp.int32, (512, 512), 1)
    source = jnp.where(col < 256, 2 * col, 2 * (col - 256) + 1)
    chooser = jnp.where(row == source, 1.0, 0.0).astype(BF16)
    split_ref[...] = jnp.dot(x, chooser, preferred_element_type=F32).astype(BF16)
    slot = jnp.broadcast_to(resident_slot(slot_ref[...], target_ref), (512, 128))
    high = (lanes(512) >= RANK).astype(jnp.int32)
    acc = jnp.zeros((512, 128), F32)
    for j in range(CHIPS):
        part = jnp.dot(x, down_ref[:, j * 128 : (j + 1) * 128], preferred_element_type=F32)
        acc += jnp.where(slot == 2 * j + high, part, 0.0)
    acc_ref[...] = acc


def shrink_resident(x, down, slot, target, after=()):
    return call(
        shrink_resident_kernel,
        "shrink_resident",
        [whole((512, 128), F32), whole((512, 512), BF16)],
        (x, down, slot, target),
        [VM, VM, VM, SM],
        after,
    )


def shrink_fresh_kernel(split_ref, acc_ref, slot_ref, target_ref, maps_ref, out_ref):
    even, odd = split_ref[:, :256], split_ref[:, 256:]
    slot = jnp.broadcast_to(slot_ref[...], (512, 128))
    low = lanes(512) < RANK
    acc = acc_ref[...]
    for k in range(CHIPS):
        maps = maps_ref[2 * k]
        part = jnp.where(
            low,
            jnp.dot(even, maps, preferred_element_type=F32),
            jnp.dot(odd, maps, preferred_element_type=F32),
        )
        acc += jnp.where(slot == target_ref[k], part, 0.0)
    acc = acc + pltpu.roll(acc, RANK, 1)
    out_ref[...] = jnp.where(lanes(256) < RANK, acc[:256], acc[256:]).astype(BF16)


def shrink_fresh(split, acc, slot, target, maps, after=()):
    return call(
        shrink_fresh_kernel,
        "shrink_fresh",
        whole((256, 128), BF16),
        (split, acc, slot, target, maps),
        [VM, VM, VM, SM, VM],
        after,
    )


def raise_kernel(mine_ref, other_ref, up_ref, slot_ref, target_ref, maps_ref, out_ref):
    packed = (mine_ref[...].astype(F32) + other_ref[...].astype(F32)).astype(BF16).astype(F32)
    turned = pltpu.roll(packed, RANK, 1)
    left = lanes(256) < RANK
    both = jnp.concatenate(
        [jnp.where(left, packed, turned), jnp.where(left, turned, packed)], axis=0
    )
    slot = jnp.broadcast_to(slot_ref[...], (512, 128))
    kept = resident_slot(slot, target_ref)
    high = (lanes(512) >= RANK).astype(jnp.int32)
    total = jnp.zeros((512, 512), F32)
    for j in range(CHIPS):
        raised = jnp.where(kept == 2 * j + high, both, 0.0).astype(BF16)
        total += jnp.dot(raised, up_ref[j * 128 : (j + 1) * 128, :], preferred_element_type=F32)
    even = jnp.zeros((512, 256), F32)
    odd = jnp.zeros((512, 256), F32)
    turn = (((1,), (1,)), ((), ()))
    for k in range(CHIPS):
        maps = maps_ref[2 * k + 1]
        fresh = jnp.where(slot == target_ref[k], both, 0.0)
        even += lax.dot_general(
            jnp.where(high == 0, fresh, 0.0).astype(BF16), maps, turn, preferred_element_type=F32
        )
        odd += lax.dot_general(
            jnp.where(high == 1, fresh, 0.0).astype(BF16), maps, turn, preferred_element_type=F32
        )
    row = lax.broadcasted_iota(jnp.int32, (256, 512), 0)
    col = lax.broadcasted_iota(jnp.int32, (256, 512), 1)
    to_even = jnp.where(col == 2 * row, 1.0, 0.0).astype(BF16)
    to_odd = jnp.where(col == 2 * row + 1, 1.0, 0.0).astype(BF16)
    total += jnp.dot(even.astype(BF16), to_even, preferred_element_type=F32)
    total += jnp.dot(odd.astype(BF16), to_odd, preferred_element_type=F32)
    out_ref[...] = (SCALE * total).astype(BF16).reshape(16, 32, 512)


def raise_features(mine, other, up, slot, target, maps, after=()):
    return call(
        raise_kernel,
        "raise_features",
        whole((16, 32, 512), BF16),
        (mine, other, up, slot, target, maps),
        [VM, VM, VM, VM, SM, VM],
        after,
    )


def finish_kernel(
    residual_ref, wide_ref, wide_y_ref, narrow_ref, narrow_left_ref, narrow_right_ref, delta_ref, out_ref
):
    for t in range(16):
        cols = slice(t * 512, (t + 1) * 512)
        if (t + 1) * 512 <= WIDE:
            base = wide_ref[:, cols] + wide_y_ref[:, cols].astype(F32)
        else:
            part = slice(t * 512 - WIDE, (t + 1) * 512 - WIDE)
            base = plus(narrow_ref[:, part], narrow_left_ref[:, part], narrow_right_ref[:, part])
        out_ref[:, cols] = (
            residual_ref[:, cols].astype(F32) + base + delta_ref[t].astype(F32)
        ).astype(BF16)


def local(
    attention_output,
    output_projection_weight,
    residual,
    resident_down_maps,
    resident_up_maps,
    fresh_adapter_bundle,
    fresh_slot_targets,
    request_adapter_slot,
):
    x, w = attention_output, output_projection_weight
    slot = request_adapter_slot.reshape(512, 1)
    target = fresh_slot_targets

    maps = lax.all_to_all(
        fresh_adapter_bundle.reshape(16, 256, 128), "tp", split_axis=0, concat_axis=0, tiled=True
    )
    narrow = x.shape[0] * 16 - WIDE
    narrow_away = product(x, w, Y_MAJOR, 1, WIDE, narrow, 1792)
    narrow_in = send(narrow_away, 0, 0, 1)
    wide_away = product(x, w, X_MAJOR, 1, 0, WIDE, 1536, [narrow_away])
    wide_in = send(wide_away, 0, 0, 1)
    narrow_own = product(x, w, Y_MAJOR, 0, WIDE, narrow, 1792, [wide_away])
    wide_own = product(x, w, X_MAJOR, 0, 0, WIDE, 1536, [narrow_own])

    keep, away = chip_narrow(narrow_own, narrow_in, [wide_own])
    narrow_y = send(away, 1, 0, 0)
    here, right, left, far_right, far_left = chip_wide(wide_own, wide_in, [away])
    far_right, far_left = send(far_right, 0, 1, 0), send(far_left, 0, 3, 0)
    acc, split = shrink_resident(x, resident_down_maps, slot, target, [here])

    right, left = near(right, left, far_right, far_left, [acc])
    from_left, from_right = send(right, 0, 1, 0), send(left, 0, 3, 0)

    part = shrink_fresh(split, acc, slot, target, maps, [right])
    part = add_parts([part, send(part, 0, 0, 1)])
    rest = [send(part, 0, 1, 0), send(part, 0, 2, 0), send(part, 0, 3, 0)]

    low_here, low_right, low_left, low_far_right, low_far_left = turn_narrow(keep, narrow_y, [part])
    low_far_right, low_far_left = send(low_far_right, 0, 1, 0), send(low_far_left, 0, 3, 0)

    part = add_parts([part, *rest], [low_here])
    other = send(part, 1, 0, 0)

    low_right, low_left = near(low_right, low_left, low_far_right, low_far_left, [part])
    low_from_left, low_from_right = send(low_right, 0, 1, 0), send(low_left, 0, 3, 0)

    raised = raise_features(part, other, resident_up_maps, slot, target, maps, [low_right])
    delta = lax.all_to_all(raised, "tp", split_axis=0, concat_axis=0, tiled=True)

    wide_keep, wide_send = turn_wide(here, from_left, from_right, [raised])
    wide_y = send(wide_send, 1, 0, 0)
    return call(
        finish_kernel,
        "finish",
        whole((32, 8192), BF16),
        (residual, wide_keep, wide_y, low_here, low_from_left, low_from_right, delta),
    )


def solution(mesh):
    return jax.shard_map(
        local,
        mesh=mesh,
        in_specs=(
            P("grp", "tp"),
            P("tp", None),
            P("tp", "grp"),
            P("tp", "grp"),
            P("grp", "tp"),
            P(("grp", "tp"), None, None),
            P("grp"),
            P("grp"),
        ),
        out_specs=P("tp", "grp"),
        check_vma=False,
    )
```

```python
import jax
import jax.numpy as jnp
from jax import lax
from jax.experimental import pallas as pl
from jax.experimental.pallas import tpu as pltpu
from jax.sharding import PartitionSpec as P

RANK = 64
SLOTS = 16
CHIPS = 8
SCALE = 0.5
F32 = jnp.float32
BF16 = jnp.bfloat16
WIDE = 4608
VMEM_LIMIT = 16 * 1024 * 1024
PRODUCT_LIMIT = 56 * 1024 * 1024
CHUNK = 512


def place(y, x, core):
    return ((y % 2) * 4 + x % 4) * 2 + core % 2


def route(yy, xx, cc):
    return [
        (place(y, x, c), place(y + yy, x + xx, c + cc))
        for y in range(2)
        for x in range(4)
        for c in range(2)
    ]


def send(array, yy, xx, cc):
    return lax.ppermute(array, "tp", route(yy, xx, cc))


def spot():
    t = lax.axis_index("tp")
    return t // 8, lax.rem(t // 2, 4), lax.rem(t, 2)


def partner(yy, xx, cc):
    y, x, c = spot()
    return (lax.rem(y + yy, 2) * 4 + lax.rem(x + xx, 4)) * 2 + lax.rem(c + cc, 2)


def rows_at(index, size):
    return pl.ds(pl.multiple_of(index * size, size), size)


def whole(shape, dtype):
    return jax.ShapeDtypeStruct(shape, dtype)


def plus(a, *others):
    total = a.astype(F32)
    for other in others:
        total = total + other.astype(F32)
    return total


VM = pl.BlockSpec(memory_space=pltpu.VMEM)
SM = pl.BlockSpec(memory_space=pltpu.SMEM)
LATER = pl.BlockSpec(memory_space=pl.ANY)


def call(kernel, name, out_shape, args, specs=None, after=(), limit=VMEM_LIMIT, **options):
    count = len(args)

    def body(*refs):
        kernel(*refs[:count], *refs[count + len(after) :])

    return pl.pallas_call(
        body,
        in_specs=list(specs or [VM] * count) + [LATER] * len(after),
        out_shape=out_shape,
        compiler_params=pltpu.CompilerParams(vmem_limit_bytes=limit),
        cost_estimate=pl.CostEstimate(flops=1024, bytes_accessed=1024, transcendentals=0),
        name=name,
        **options,
    )(*args, *after)


X_MAJOR = [(yy, xx) for xx in range(4) for yy in range(2)]
Y_MAJOR = [(yy, xx) for yy in range(2) for xx in range(4)]


def product(x, w, order, first, width, after=()):
    chunks = width // CHUNK

    def kernel(x_ref, w_ref, away_ref, own_ref, rows_ref, held_ref, sems):
        def copy(i):
            cols = pl.ds(pl.multiple_of(first + i * CHUNK, CHUNK), CHUNK)
            return pltpu.make_async_copy(w_ref.at[:, cols], held_ref.at[i], sems.at[i])

        @pl.loop(0, chunks)
        def _(i):
            copy(i).start()

        for i, (yy, xx) in enumerate(order):
            for cc, top in ((1, 0), (0, 256)):
                rows_ref[top + i * 32 : top + (i + 1) * 32, :] = x_ref[
                    rows_at(partner(yy, xx, cc), 32), :
                ]

        @pl.loop(0, chunks)
        def _(i):
            copy(i).wait()
            part = jnp.dot(rows_ref[...], held_ref[i], preferred_element_type=F32).astype(BF16)
            cols = pl.ds(pl.multiple_of(i * CHUNK, CHUNK), CHUNK)
            away_ref[:, cols] = part[:256]
            own_ref[:, cols] = part[256:]

    return call(
        kernel,
        "product",
        [whole((256, width), BF16)] * 2,
        (x, w),
        [VM, pl.BlockSpec(memory_space=pltpu.HBM)],
        after,
        limit=PRODUCT_LIMIT,
        scratch_shapes=[
            pltpu.VMEM((512, 512), BF16),
            pltpu.VMEM((chunks, 512, CHUNK), BF16),
            pltpu.SemaphoreType.DMA((chunks,)),
        ],
    )


def chip_narrow(own, away, after=()):
    width = own.shape[1]

    def kernel(own_ref, away_ref, keep_ref, send_ref):
        @pl.loop(0, width // CHUNK)
        def _(j):
            cols = pl.ds(pl.multiple_of(j * CHUNK, CHUNK), CHUNK)
            total = plus(own_ref[:, cols], away_ref[:, cols]).astype(BF16)
            keep_ref[:, cols] = total[:128]
            send_ref[:, cols] = total[128:]

    return call(
        kernel, "chip_narrow", [whole((128, width), BF16)] * 2, (own, away), after=after
    )


def chip_wide(own, away, after=()):
    width = own.shape[1]
    half = width // 2
    step = 256

    def kernel(own_ref, away_ref, here_ref, right_ref, left_ref, far_right_ref, far_left_ref):
        for side, far_ref in enumerate((far_right_ref, far_left_ref)):

            @pl.loop(0, half // step)
            def _(j):
                cols = pl.ds(pl.multiple_of(side * half + j * step, step), step)
                total = plus(own_ref[:, cols], away_ref[:, cols]).astype(BF16)
                here_ref[:, cols] = total[:64]
                right_ref[:, cols] = total[64:128]
                far_ref[:, pl.ds(pl.multiple_of(j * step, step), step)] = total[128:192]
                left_ref[:, cols] = total[192:]

    return call(
        kernel,
        "chip_wide",
        [whole((64, width), BF16)] * 3 + [whole((64, half), BF16)] * 2,
        (own, away),
        after=after,
    )


def turn_narrow(keep, landed, after=()):
    width = keep.shape[1]
    half = width // 2

    def kernel(keep_ref, landed_ref, here_ref, right_ref, left_ref, far_right_ref, far_left_ref):
        total = plus(keep_ref[...], landed_ref[...]).astype(BF16)
        here_ref[...] = total[:32]
        right_ref[...] = total[32:64]
        left_ref[...] = total[96:]
        far_right_ref[...] = total[64:96, :half]
        far_left_ref[...] = total[64:96, half:]

    return call(
        kernel,
        "turn_narrow",
        [whole((32, width), BF16)] * 3 + [whole((32, half), BF16)] * 2,
        (keep, landed),
        after=after,
    )


def near(right, left, far_right, far_left, after=()):
    half = right.shape[1] // 2

    def kernel(right_ref, left_ref, far_right_ref, far_left_ref, to_right_ref, to_left_ref):
        to_right_ref[:, :half] = plus(right_ref[:, :half], far_right_ref[...]).astype(BF16)
        to_right_ref[:, half:] = right_ref[:, half:]
        to_left_ref[:, :half] = left_ref[:, :half]
        to_left_ref[:, half:] = plus(left_ref[:, half:], far_left_ref[...]).astype(BF16)

    return call(
        kernel, "near", [whole(right.shape, BF16)] * 2, (right, left, far_right, far_left), after=after
    )


def turn_wide(here, from_left, from_right, after=()):
    width = here.shape[1]

    def kernel(here_ref, from_left_ref, from_right_ref, keep_ref, send_ref):
        total = plus(here_ref[...], from_left_ref[...], from_right_ref[...])
        keep_ref[...] = total[:32]
        send_ref[...] = total[32:].astype(BF16)

    return call(
        kernel,
        "turn_wide",
        [whole((32, width), F32), whole((32, width), BF16)],
        (here, from_left, from_right),
        after=after,
    )


def add_parts(parts, after=()):
    def kernel(*refs):
        refs[-1][...] = plus(*[ref[...] for ref in refs[:-1]]).astype(BF16)

    return call(kernel, "add_parts", whole(parts[0].shape, BF16), parts, after=after)


def lanes(rows):
    return lax.broadcasted_iota(jnp.int32, (rows, 128), 1)


def resident_slot(slot, target_ref):
    for k in range(CHIPS):
        slot = jnp.where(slot == target_ref[k], -1, slot)
    return slot


def shrink_resident_kernel(x_ref, down_ref, slot_ref, target_ref, acc_ref, split_ref):
    x = x_ref[...]
    row = lax.broadcasted_iota(jnp.int32, (512, 512), 0)
    col = lax.broadcasted_iota(jnp.int32, (512, 512), 1)
    source = jnp.where(col < 256, 2 * col, 2 * (col - 256) + 1)
    chooser = jnp.where(row == source, 1.0, 0.0).astype(BF16)
    split_ref[...] = jnp.dot(x, chooser, preferred_element_type=F32).astype(BF16)
    slot = jnp.broadcast_to(resident_slot(slot_ref[...], target_ref), (512, 128))
    high = (lanes(512) >= RANK).astype(jnp.int32)
    acc = jnp.zeros((512, 128), F32)
    for j in range(CHIPS):
        part = jnp.dot(x, down_ref[:, j * 128 : (j + 1) * 128], preferred_element_type=F32)
        acc += jnp.where(slot == 2 * j + high, part, 0.0)
    acc_ref[...] = acc


def shrink_resident(x, down, slot, target, after=()):
    return call(
        shrink_resident_kernel,
        "shrink_resident",
        [whole((512, 128), F32), whole((512, 512), BF16)],
        (x, down, slot, target),
        [VM, VM, VM, SM],
        after,
    )


def shrink_fresh_kernel(split_ref, acc_ref, slot_ref, target_ref, maps_ref, out_ref):
    even, odd = split_ref[:, :256], split_ref[:, 256:]
    slot = jnp.broadcast_to(slot_ref[...], (512, 128))
    low = lanes(512) < RANK
    acc = acc_ref[...]
    for k in range(CHIPS):
        maps = maps_ref[2 * k]
        part = jnp.where(
            low,
            jnp.dot(even, maps, preferred_element_type=F32),
            jnp.dot(odd, maps, preferred_element_type=F32),
        )
        acc += jnp.where(slot == target_ref[k], part, 0.0)
    acc = acc + pltpu.roll(acc, RANK, 1)
    out_ref[...] = jnp.where(lanes(256) < RANK, acc[:256], acc[256:]).astype(BF16)


def shrink_fresh(split, acc, slot, target, maps, after=()):
    return call(
        shrink_fresh_kernel,
        "shrink_fresh",
        whole((256, 128), BF16),
        (split, acc, slot, target, maps),
        [VM, VM, VM, SM, VM],
        after,
    )


def up_table_kernel(up_ref, target_ref, maps_ref, table_ref):
    table_ref[...] = up_ref[...]
    row = lax.broadcasted_iota(jnp.int32, (256, 512), 0)
    col = lax.broadcasted_iota(jnp.int32, (256, 512), 1)
    to_even = jnp.where(col == 2 * row, 1.0, 0.0).astype(BF16)
    to_odd = jnp.where(col == 2 * row + 1, 1.0, 0.0).astype(BF16)
    turn = (((0,), (0,)), ((), ()))
    for k in range(CHIPS):
        maps = maps_ref[2 * k + 1]
        even = lax.dot_general(maps, to_even, turn, preferred_element_type=F32)
        odd = lax.dot_general(maps, to_odd, turn, preferred_element_type=F32)
        table_ref[rows_at(target_ref[k], RANK), :] = (even[:RANK] + odd[RANK:]).astype(BF16)


def up_table(up, target, maps, after=()):
    return call(
        up_table_kernel, "up_table", whole((1024, 512), BF16), (up, target, maps), [VM, SM, VM], after
    )


def raise_kernel(mine_ref, other_ref, table_ref, slot_ref, out_ref):
    packed = (mine_ref[...].astype(F32) + other_ref[...].astype(F32)).astype(BF16).astype(F32)
    turned = pltpu.roll(packed, RANK, 1)
    left = lanes(256) < RANK
    both = jnp.concatenate(
        [jnp.where(left, packed, turned), jnp.where(left, turned, packed)], axis=0
    )
    slot = jnp.broadcast_to(slot_ref[...], (512, 128))
    high = (lanes(512) >= RANK).astype(jnp.int32)
    raised = jnp.concatenate(
        [jnp.where(slot == 2 * j + high, both, 0.0).astype(BF16) for j in range(CHIPS)], axis=1
    )
    total = jnp.dot(raised, table_ref[...], preferred_element_type=F32)
    out_ref[...] = (SCALE * total).astype(BF16).reshape(16, 32, 512)


def raise_features(mine, other, table, slot, after=()):
    return call(
        raise_kernel,
        "raise_features",
        whole((16, 32, 512), BF16),
        (mine, other, table, slot),
        after=after,
    )


def finish_kernel(
    residual_ref, wide_ref, wide_y_ref, narrow_ref, narrow_left_ref, narrow_right_ref, delta_ref, out_ref
):
    for t in range(16):
        cols = slice(t * 512, (t + 1) * 512)
        if (t + 1) * 512 <= WIDE:
            base = wide_ref[:, cols] + wide_y_ref[:, cols].astype(F32)
        else:
            part = slice(t * 512 - WIDE, (t + 1) * 512 - WIDE)
            base = plus(narrow_ref[:, part], narrow_left_ref[:, part], narrow_right_ref[:, part])
        out_ref[:, cols] = (
            residual_ref[:, cols].astype(F32) + base + delta_ref[t].astype(F32)
        ).astype(BF16)


def local(
    attention_output,
    output_projection_weight,
    residual,
    resident_down_maps,
    resident_up_maps,
    fresh_adapter_bundle,
    fresh_slot_targets,
    request_adapter_slot,
):
    x, w = attention_output, output_projection_weight
    slot = request_adapter_slot.reshape(512, 1)
    target = fresh_slot_targets

    maps = lax.all_to_all(
        fresh_adapter_bundle.reshape(16, 256, 128), "tp", split_axis=0, concat_axis=0, tiled=True
    )
    narrow = x.shape[0] * 16 - WIDE
    narrow_away, narrow_own = product(x, w, Y_MAJOR, WIDE, narrow)
    narrow_in = send(narrow_away, 0, 0, 1)
    wide_away, wide_own = product(x, w, X_MAJOR, 0, WIDE, [narrow_away])
    wide_in = send(wide_away, 0, 0, 1)

    keep, away = chip_narrow(narrow_own, narrow_in, [wide_own])
    narrow_y = send(away, 1, 0, 0)
    here, right, left, far_right, far_left = chip_wide(wide_own, wide_in, [away])
    far_right, far_left = send(far_right, 0, 1, 0), send(far_left, 0, 3, 0)
    acc, split = shrink_resident(x, resident_down_maps, slot, target, [here])

    right, left = near(right, left, far_right, far_left, [acc])
    from_left, from_right = send(right, 0, 1, 0), send(left, 0, 3, 0)

    part = shrink_fresh(split, acc, slot, target, maps, [right])
    part = add_parts([part, send(part, 0, 0, 1)])
    table = up_table(resident_up_maps, target, maps, [part])
    rest = [send(part, 0, 1, 0), send(part, 0, 2, 0), send(part, 0, 3, 0)]

    low_here, low_right, low_left, low_far_right, low_far_left = turn_narrow(keep, narrow_y, [table])
    low_far_right, low_far_left = send(low_far_right, 0, 1, 0), send(low_far_left, 0, 3, 0)

    part = add_parts([part, *rest], [low_here])
    other = send(part, 1, 0, 0)

    low_right, low_left = near(low_right, low_left, low_far_right, low_far_left, [part])
    low_from_left, low_from_right = send(low_right, 0, 1, 0), send(low_left, 0, 3, 0)

    raised = raise_features(part, other, table, slot, [low_right])
    delta = lax.all_to_all(raised, "tp", split_axis=0, concat_axis=0, tiled=True)

    wide_keep, wide_send = turn_wide(here, from_left, from_right, [raised])
    wide_y = send(wide_send, 1, 0, 0)
    return call(
        finish_kernel,
        "finish",
        whole((32, 8192), BF16),
        (residual, wide_keep, wide_y, low_here, low_from_left, low_from_right, delta),
    )


def solution(mesh):
    return jax.shard_map(
        local,
        mesh=mesh,
        in_specs=(
            P("grp", "tp"),
            P("tp", None),
            P("tp", "grp"),
            P("tp", "grp"),
            P("grp", "tp"),
            P(("grp", "tp"), None, None),
            P("grp"),
            P("grp"),
        ),
        out_specs=P("tp", "grp"),
        check_vma=False,
    )
```

```python
import jax
import jax.numpy as jnp
from jax import lax
from jax.experimental import pallas as pl
from jax.experimental.pallas import tpu as pltpu
from jax.sharding import PartitionSpec as P

RANK = 64
SLOTS = 16
CHIPS = 8
SCALE = 0.5
F32 = jnp.float32
BF16 = jnp.bfloat16
WIDE = 4608
VMEM_LIMIT = 16 * 1024 * 1024
PRODUCT_LIMIT = 56 * 1024 * 1024
NARROW_CHUNK = 1792
WIDE_CHUNK = 1536


def place(y, x, core):
    return ((y % 2) * 4 + x % 4) * 2 + core % 2


def route(yy, xx, cc):
    return [
        (place(y, x, c), place(y + yy, x + xx, c + cc))
        for y in range(2)
        for x in range(4)
        for c in range(2)
    ]


def send(array, yy, xx, cc):
    return lax.ppermute(array, "tp", route(yy, xx, cc))


def spot():
    t = lax.axis_index("tp")
    return t // 8, lax.rem(t // 2, 4), lax.rem(t, 2)


def partner(yy, xx, cc):
    y, x, c = spot()
    return (lax.rem(y + yy, 2) * 4 + lax.rem(x + xx, 4)) * 2 + lax.rem(c + cc, 2)


def rows_at(index, size):
    return pl.ds(pl.multiple_of(index * size, size), size)


def whole(shape, dtype):
    return jax.ShapeDtypeStruct(shape, dtype)


def plus(a, *others):
    total = a.astype(F32)
    for other in others:
        total = total + other.astype(F32)
    return total


VM = pl.BlockSpec(memory_space=pltpu.VMEM)
SM = pl.BlockSpec(memory_space=pltpu.SMEM)
LATER = pl.BlockSpec(memory_space=pl.ANY)


def call(kernel, name, out_shape, args, specs=None, after=(), limit=VMEM_LIMIT, **options):
    count = len(args)

    def body(*refs):
        kernel(*refs[:count], *refs[count + len(after) :])

    return pl.pallas_call(
        body,
        in_specs=list(specs or [VM] * count) + [LATER] * len(after),
        out_shape=out_shape,
        compiler_params=pltpu.CompilerParams(vmem_limit_bytes=limit),
        cost_estimate=pl.CostEstimate(flops=1024, bytes_accessed=1024, transcendentals=0),
        name=name,
        **options,
    )(*args, *after)


X_MAJOR = [(yy, xx) for xx in range(4) for yy in range(2)]
Y_MAJOR = [(yy, xx) for yy in range(2) for xx in range(4)]


def product(x, w, order, first, width, chunk, after=()):
    chunks = width // chunk

    def kernel(x_ref, w_ref, *refs):
        away_refs = refs[:chunks]
        own_ref, rows_ref, held_ref, done_ref, sems, away_sems = refs[chunks:]

        def copy(i):
            cols = pl.ds(pl.multiple_of(first + i * chunk, 128), chunk)
            return pltpu.make_async_copy(w_ref.at[:, cols], held_ref.at[i], sems.at[i])

        def leave(i):
            return pltpu.make_async_copy(done_ref.at[i], away_refs[i], away_sems.at[i])

        for i in range(chunks):
            copy(i).start()
        for i, (yy, xx) in enumerate(order):
            for cc, top in ((1, 0), (0, 256)):
                rows_ref[top + i * 32 : top + (i + 1) * 32, :] = x_ref[
                    rows_at(partner(yy, xx, cc), 32), :
                ]
        for i in range(chunks):
            copy(i).wait()
            part = jnp.dot(rows_ref[...], held_ref[i], preferred_element_type=F32).astype(BF16)
            done_ref[i] = part[:256]
            leave(i).start()
            own_ref[:, i * chunk : (i + 1) * chunk] = part[256:]
        for i in range(chunks):
            leave(i).wait()

    return call(
        kernel,
        "product",
        [whole((256, chunk), BF16)] * chunks + [whole((256, width), BF16)],
        (x, w),
        [VM, pl.BlockSpec(memory_space=pltpu.HBM)],
        after,
        limit=PRODUCT_LIMIT,
        out_specs=[pl.BlockSpec(memory_space=pltpu.HBM)] * chunks + [VM],
        scratch_shapes=[
            pltpu.VMEM((512, 512), BF16),
            pltpu.VMEM((chunks, 512, chunk), BF16),
            pltpu.VMEM((chunks, 256, chunk), BF16),
            pltpu.SemaphoreType.DMA((chunks,)),
            pltpu.SemaphoreType.DMA((chunks,)),
        ],
    )


def chip_narrow(own, away, after=()):
    width = own.shape[1]
    step = 256

    def kernel(own_ref, *refs):
        keep_ref, send_ref = refs[len(away) :]
        for i, away_ref in enumerate(refs[: len(away)]):

            @pl.loop(0, away_ref.shape[1] // step)
            def _(j):
                cols = pl.ds(pl.multiple_of(i * away_ref.shape[1] + j * step, step), step)
                part = pl.ds(pl.multiple_of(j * step, step), step)
                total = plus(own_ref[:, cols], away_ref[:, part]).astype(BF16)
                keep_ref[:, cols] = total[:128]
                send_ref[:, cols] = total[128:]

    return call(
        kernel, "chip_narrow", [whole((128, width), BF16)] * 2, (own, *away), after=after
    )


def chip_wide(own, away, after=()):
    width = own.shape[1]
    half = width // 2
    chunk = away[0].shape[1]
    step = 256

    def kernel(own_ref, *refs):
        here_ref, right_ref, left_ref, far_right_ref, far_left_ref = refs[len(away) :]
        for first in range(0, width, step):
            cols = slice(first, first + step)
            part = first % chunk
            total = plus(
                own_ref[:, cols], refs[first // chunk][:, part : part + step]
            ).astype(BF16)
            here_ref[:, cols] = total[:64]
            right_ref[:, cols] = total[64:128]
            if first < half:
                far_right_ref[:, cols] = total[128:192]
            else:
                far_left_ref[:, first - half : first - half + step] = total[128:192]
            left_ref[:, cols] = total[192:]

    return call(
        kernel,
        "chip_wide",
        [whole((64, width), BF16)] * 3 + [whole((64, half), BF16)] * 2,
        (own, *away),
        after=after,
    )


def turn_narrow(keep, landed, after=()):
    width = keep.shape[1]
    half = width // 2

    def kernel(keep_ref, landed_ref, here_ref, right_ref, left_ref, far_right_ref, far_left_ref):
        total = plus(keep_ref[...], landed_ref[...]).astype(BF16)
        here_ref[...] = total[:32]
        right_ref[...] = total[32:64]
        left_ref[...] = total[96:]
        far_right_ref[...] = total[64:96, :half]
        far_left_ref[...] = total[64:96, half:]

    return call(
        kernel,
        "turn_narrow",
        [whole((32, width), BF16)] * 3 + [whole((32, half), BF16)] * 2,
        (keep, landed),
        after=after,
    )


def near(right, left, far_right, far_left, after=()):
    half = right.shape[1] // 2

    def kernel(right_ref, left_ref, far_right_ref, far_left_ref, to_right_ref, to_left_ref):
        to_right_ref[:, :half] = plus(right_ref[:, :half], far_right_ref[...]).astype(BF16)
        to_right_ref[:, half:] = right_ref[:, half:]
        to_left_ref[:, :half] = left_ref[:, :half]
        to_left_ref[:, half:] = plus(left_ref[:, half:], far_left_ref[...]).astype(BF16)

    return call(
        kernel, "near", [whole(right.shape, BF16)] * 2, (right, left, far_right, far_left), after=after
    )


def turn_wide(here, from_left, from_right, after=()):
    width = here.shape[1]

    def kernel(here_ref, from_left_ref, from_right_ref, keep_ref, send_ref):
        total = plus(here_ref[...], from_left_ref[...], from_right_ref[...])
        keep_ref[...] = total[:32]
        send_ref[...] = total[32:].astype(BF16)

    return call(
        kernel,
        "turn_wide",
        [whole((32, width), F32), whole((32, width), BF16)],
        (here, from_left, from_right),
        after=after,
    )


def add_parts(parts, after=()):
    def kernel(*refs):
        refs[-1][...] = plus(*[ref[...] for ref in refs[:-1]]).astype(BF16)

    return call(kernel, "add_parts", whole(parts[0].shape, BF16), parts, after=after)


def lanes(rows):
    return lax.broadcasted_iota(jnp.int32, (rows, 128), 1)


def resident_slot(slot, target_ref):
    for k in range(CHIPS):
        slot = jnp.where(slot == target_ref[k], -1, slot)
    return slot


def shrink_resident_kernel(x_ref, down_ref, slot_ref, target_ref, acc_ref, split_ref):
    x = x_ref[...]
    row = lax.broadcasted_iota(jnp.int32, (512, 512), 0)
    col = lax.broadcasted_iota(jnp.int32, (512, 512), 1)
    source = jnp.where(col < 256, 2 * col, 2 * (col - 256) + 1)
    chooser = jnp.where(row == source, 1.0, 0.0).astype(BF16)
    split_ref[...] = jnp.dot(x, chooser, preferred_element_type=F32).astype(BF16)
    slot = jnp.broadcast_to(resident_slot(slot_ref[...], target_ref), (512, 128))
    high = (lanes(512) >= RANK).astype(jnp.int32)
    acc = jnp.zeros((512, 128), F32)
    for j in range(CHIPS):
        part = jnp.dot(x, down_ref[:, j * 128 : (j + 1) * 128], preferred_element_type=F32)
        acc += jnp.where(slot == 2 * j + high, part, 0.0)
    acc_ref[...] = acc


def shrink_resident(x, down, slot, target, after=()):
    return call(
        shrink_resident_kernel,
        "shrink_resident",
        [whole((512, 128), F32), whole((512, 512), BF16)],
        (x, down, slot, target),
        [VM, VM, VM, SM],
        after,
    )


def shrink_fresh_kernel(split_ref, acc_ref, slot_ref, target_ref, maps_ref, out_ref):
    even, odd = split_ref[:, :256], split_ref[:, 256:]
    slot = jnp.broadcast_to(slot_ref[...], (512, 128))
    low = lanes(512) < RANK
    acc = acc_ref[...]
    for k in range(CHIPS):
        maps = maps_ref[2 * k]
        part = jnp.where(
            low,
            jnp.dot(even, maps, preferred_element_type=F32),
            jnp.dot(odd, maps, preferred_element_type=F32),
        )
        acc += jnp.where(slot == target_ref[k], part, 0.0)
    acc = acc + pltpu.roll(acc, RANK, 1)
    out_ref[...] = jnp.where(lanes(256) < RANK, acc[:256], acc[256:]).astype(BF16)


def shrink_fresh(split, acc, slot, target, maps, after=()):
    return call(
        shrink_fresh_kernel,
        "shrink_fresh",
        whole((256, 128), BF16),
        (split, acc, slot, target, maps),
        [VM, VM, VM, SM, VM],
        after,
    )


def up_table_kernel(up_ref, target_ref, maps_ref, table_ref):
    table_ref[...] = up_ref[...]
    row = lax.broadcasted_iota(jnp.int32, (256, 512), 0)
    col = lax.broadcasted_iota(jnp.int32, (256, 512), 1)
    to_even = jnp.where(col == 2 * row, 1.0, 0.0).astype(BF16)
    to_odd = jnp.where(col == 2 * row + 1, 1.0, 0.0).astype(BF16)
    turn = (((0,), (0,)), ((), ()))
    for k in range(CHIPS):
        maps = maps_ref[2 * k + 1]
        even = lax.dot_general(maps, to_even, turn, preferred_element_type=F32)
        odd = lax.dot_general(maps, to_odd, turn, preferred_element_type=F32)
        table_ref[rows_at(target_ref[k], RANK), :] = (even[:RANK] + odd[RANK:]).astype(BF16)


def up_table(up, target, maps, after=()):
    return call(
        up_table_kernel, "up_table", whole((1024, 512), BF16), (up, target, maps), [VM, SM, VM], after
    )


def raise_kernel(mine_ref, other_ref, table_ref, slot_ref, out_ref):
    packed = (mine_ref[...].astype(F32) + other_ref[...].astype(F32)).astype(BF16).astype(F32)
    turned = pltpu.roll(packed, RANK, 1)
    left = lanes(256) < RANK
    both = jnp.concatenate(
        [jnp.where(left, packed, turned), jnp.where(left, turned, packed)], axis=0
    )
    slot = jnp.broadcast_to(slot_ref[...], (512, 128))
    high = (lanes(512) >= RANK).astype(jnp.int32)
    raised = jnp.concatenate(
        [jnp.where(slot == 2 * j + high, both, 0.0).astype(BF16) for j in range(CHIPS)], axis=1
    )
    total = jnp.dot(raised, table_ref[...], preferred_element_type=F32)
    out_ref[...] = (SCALE * total).astype(BF16).reshape(16, 32, 512)


def raise_features(mine, other, table, slot, after=()):
    return call(
        raise_kernel,
        "raise_features",
        whole((16, 32, 512), BF16),
        (mine, other, table, slot),
        after=after,
    )


def finish_kernel(
    residual_ref, wide_ref, wide_y_ref, narrow_ref, narrow_left_ref, narrow_right_ref, delta_ref, out_ref
):
    for t in range(16):
        cols = slice(t * 512, (t + 1) * 512)
        if (t + 1) * 512 <= WIDE:
            base = wide_ref[:, cols] + wide_y_ref[:, cols].astype(F32)
        else:
            part = slice(t * 512 - WIDE, (t + 1) * 512 - WIDE)
            base = plus(narrow_ref[:, part], narrow_left_ref[:, part], narrow_right_ref[:, part])
        out_ref[:, cols] = (
            residual_ref[:, cols].astype(F32) + base + delta_ref[t].astype(F32)
        ).astype(BF16)


def local(
    attention_output,
    output_projection_weight,
    residual,
    resident_down_maps,
    resident_up_maps,
    fresh_adapter_bundle,
    fresh_slot_targets,
    request_adapter_slot,
):
    x, w = attention_output, output_projection_weight
    slot = request_adapter_slot.reshape(512, 1)
    target = fresh_slot_targets

    maps = lax.all_to_all(
        fresh_adapter_bundle.reshape(16, 256, 128), "tp", split_axis=0, concat_axis=0, tiled=True
    )
    narrow = x.shape[0] * 16 - WIDE
    *narrow_away, narrow_own = product(x, w, Y_MAJOR, WIDE, narrow, NARROW_CHUNK)
    narrow_in = [send(away, 0, 0, 1) for away in narrow_away]
    *wide_away, wide_own = product(x, w, X_MAJOR, 0, WIDE, WIDE_CHUNK, narrow_away[:1])
    wide_in = [send(away, 0, 0, 1) for away in wide_away]

    acc, split = shrink_resident(x, resident_down_maps, slot, target, [wide_own])
    part = shrink_fresh(split, acc, slot, target, maps)
    part_in = send(part, 0, 0, 1)

    keep, away = chip_narrow(narrow_own, narrow_in, [part])
    narrow_y = send(away, 1, 0, 0)
    part = add_parts([part, part_in], [away])
    rest = [send(part, 0, 1, 0), send(part, 0, 2, 0), send(part, 0, 3, 0)]
    here, right, left, far_right, far_left = chip_wide(wide_own, wide_in, [part])
    far_right, far_left = send(far_right, 0, 1, 0), send(far_left, 0, 3, 0)
    part = add_parts([part, *rest], [here])
    other = send(part, 1, 0, 0)
    table = up_table(resident_up_maps, target, maps, [part])

    right, left = near(right, left, far_right, far_left, [table])
    from_left, from_right = send(right, 0, 1, 0), send(left, 0, 3, 0)
    raised = raise_features(part, other, table, slot, [right])
    delta = lax.all_to_all(raised, "tp", split_axis=0, concat_axis=0, tiled=True)

    low_here, low_right, low_left, low_far_right, low_far_left = turn_narrow(keep, narrow_y, [raised])
    low_far_right, low_far_left = send(low_far_right, 0, 1, 0), send(low_far_left, 0, 3, 0)
    low_right, low_left = near(low_right, low_left, low_far_right, low_far_left, [low_here])
    low_from_left, low_from_right = send(low_right, 0, 1, 0), send(low_left, 0, 3, 0)

    wide_keep, wide_send = turn_wide(here, from_left, from_right, [low_right])
    wide_y = send(wide_send, 1, 0, 0)
    return call(
        finish_kernel,
        "finish",
        whole((32, 8192), BF16),
        (residual, wide_keep, wide_y, low_here, low_from_left, low_from_right, delta),
    )


def solution(mesh):
    return jax.shard_map(
        local,
        mesh=mesh,
        in_specs=(
            P("grp", "tp"),
            P("tp", None),
            P("tp", "grp"),
            P("tp", "grp"),
            P("grp", "tp"),
            P(("grp", "tp"), None, None),
            P("grp"),
            P("grp"),
        ),
        out_specs=P("tp", "grp"),
        check_vma=False,
    )
```

```python
import jax
import jax.numpy as jnp
from jax import lax
from jax.experimental import pallas as pl
from jax.experimental.pallas import tpu as pltpu
from jax.sharding import PartitionSpec as P

RANK = 64
SLOTS = 16
CHIPS = 8
SCALE = 0.5
F32 = jnp.float32
BF16 = jnp.bfloat16
WIDE = 4608
VMEM_LIMIT = 16 * 1024 * 1024
PRODUCT_LIMIT = 56 * 1024 * 1024
CHIP_LIMIT = 56 * 1024 * 1024
NARROW_CHUNK = 1792
WIDE_CHUNK = 1536


def place(y, x, core):
    return ((y % 2) * 4 + x % 4) * 2 + core % 2


def route(yy, xx, cc):
    return [
        (place(y, x, c), place(y + yy, x + xx, c + cc))
        for y in range(2)
        for x in range(4)
        for c in range(2)
    ]


def send(array, yy, xx, cc):
    return lax.ppermute(array, "tp", route(yy, xx, cc))


def trade(array, partner_of):
    pairs = [
        (place(y, x, c), place(y, partner_of(x), c))
        for y in range(2)
        for x in range(4)
        for c in range(2)
    ]
    return lax.ppermute(array, "tp", pairs)


def spot():
    t = lax.axis_index("tp")
    return t // 8, lax.rem(t // 2, 4), lax.rem(t, 2)


def partner(yy, xx, cc):
    y, x, c = spot()
    return (lax.rem(y + yy, 2) * 4 + lax.rem(x + xx, 4)) * 2 + lax.rem(c + cc, 2)


def rows_at(index, size):
    return pl.ds(pl.multiple_of(index * size, size), size)


def whole(shape, dtype):
    return jax.ShapeDtypeStruct(shape, dtype)


def plus(a, *others):
    total = a.astype(F32)
    for other in others:
        total = total + other.astype(F32)
    return total


VM = pl.BlockSpec(memory_space=pltpu.VMEM)
SM = pl.BlockSpec(memory_space=pltpu.SMEM)
LATER = pl.BlockSpec(memory_space=pl.ANY)


def call(kernel, name, out_shape, args, specs=None, after=(), limit=VMEM_LIMIT, out_specs=None, scratch_shapes=()):
    count, outs = len(args), len(out_shape)

    def body(*refs):
        results = refs[count + len(after) :]
        results[outs][...] = jnp.zeros((8, 128), F32)
        kernel(*refs[:count], *results[:outs], *results[outs + 1 :])

    return pl.pallas_call(
        body,
        in_specs=list(specs or [VM] * count) + [LATER] * len(after),
        out_specs=list(out_specs or [VM] * outs) + [VM],
        out_shape=list(out_shape) + [whole((8, 128), F32)],
        scratch_shapes=list(scratch_shapes),
        compiler_params=pltpu.CompilerParams(vmem_limit_bytes=limit),
        cost_estimate=pl.CostEstimate(flops=1024, bytes_accessed=1024, transcendentals=0),
        name=name,
    )(*args, *after)


X_MAJOR = [(yy, xx) for xx in range(4) for yy in range(2)]
Y_MAJOR = [(yy, xx) for yy in range(2) for xx in range(4)]


HBM = pl.BlockSpec(memory_space=pltpu.HBM)


def product(x, w, order, first, width, chunk, after=()):
    chunks = width // chunk

    def kernel(x_ref, w_ref, *refs):
        away_refs = refs[:chunks]
        own_ref, rows_ref, held_ref, done_ref, sems, away_sems, own_sems = refs[chunks:]

        def copy(i):
            cols = pl.ds(pl.multiple_of(first + i * chunk, 128), chunk)
            return pltpu.make_async_copy(w_ref.at[:, cols], held_ref.at[i], sems.at[i])

        def leave(i):
            return pltpu.make_async_copy(done_ref.at[i, :256], away_refs[i], away_sems.at[i])

        def stay(i):
            cols = pl.ds(i * chunk, chunk)
            return pltpu.make_async_copy(
                done_ref.at[i, 256:], own_ref.at[:, cols], own_sems.at[i]
            )

        for i in range(chunks):
            copy(i).start()
        for i, (yy, xx) in enumerate(order):
            for cc, top in ((1, 0), (0, 256)):
                rows_ref[top + i * 32 : top + (i + 1) * 32, :] = x_ref[
                    rows_at(partner(yy, xx, cc), 32), :
                ]
        for i in range(chunks):
            copy(i).wait()
            done_ref[i] = jnp.dot(
                rows_ref[...], held_ref[i], preferred_element_type=F32
            ).astype(BF16)
            leave(i).start()
            stay(i).start()
        for i in range(chunks):
            leave(i).wait()
            stay(i).wait()

    return call(
        kernel,
        "product",
        [whole((256, chunk), BF16)] * chunks + [whole((256, width), BF16)],
        (x, w),
        [VM, HBM],
        after,
        limit=PRODUCT_LIMIT,
        out_specs=[HBM] * (chunks + 1),
        scratch_shapes=[
            pltpu.VMEM((512, 512), BF16),
            pltpu.VMEM((chunks, 512, chunk), BF16),
            pltpu.VMEM((chunks, 512, chunk), BF16),
            pltpu.SemaphoreType.DMA((chunks,)),
            pltpu.SemaphoreType.DMA((chunks,)),
            pltpu.SemaphoreType.DMA((chunks,)),
        ],
    )


def chip_sum(name, own, away, blocks, split, after=()):
    chunk = away[0].shape[1]
    chunks = len(away)
    width = own.shape[1]
    half = width // 2
    step = 256
    rows = [own.shape[0] // blocks] * blocks
    size = rows[0]
    shapes = []
    for d in range(blocks):
        shapes += [(size, half)] * 2 if d == split else [(size, width)]

    def kernel(own_ref, *refs):
        away_refs, outs = refs[:chunks], refs[chunks : chunks + len(shapes)]
        held_ref, came_ref, own_sems, away_sems = refs[chunks + len(shapes) :]

        def load_own(i):
            return pltpu.make_async_copy(
                own_ref.at[:, pl.ds(i * chunk, chunk)], held_ref.at[i], own_sems.at[i]
            )

        def load_away(i):
            return pltpu.make_async_copy(away_refs[i], came_ref.at[i], away_sems.at[i])

        for i in range(chunks):
            load_own(i).start()
            load_away(i).start()
        for i in range(chunks):
            load_own(i).wait()
            load_away(i).wait()
            for part in range(0, chunk, step):
                first = i * chunk + part
                total = plus(
                    held_ref[i, :, part : part + step], came_ref[i, :, part : part + step]
                ).astype(BF16)
                place_at = 0
                for d in range(blocks):
                    piece = total[d * size : (d + 1) * size]
                    if d == split:
                        side, at = divmod(first, half)
                        outs[place_at + side][:, at : at + step] = piece
                        place_at += 2
                    else:
                        outs[place_at][:, first : first + step] = piece
                        place_at += 1

    return call(
        kernel,
        name,
        [whole(shape, BF16) for shape in shapes],
        (own, *away),
        [HBM] * (1 + chunks),
        after,
        limit=CHIP_LIMIT,
        scratch_shapes=[
            pltpu.VMEM((chunks, own.shape[0], chunk), BF16),
            pltpu.VMEM((chunks, own.shape[0], chunk), BF16),
            pltpu.SemaphoreType.DMA((chunks,)),
            pltpu.SemaphoreType.DMA((chunks,)),
        ],
    )


def turn_narrow(keep, landed, after=()):
    width = keep.shape[1]

    def kernel(keep_ref, landed_ref, *refs):
        total = plus(keep_ref[...], landed_ref[...]).astype(BF16)
        for d, ref in enumerate(refs):
            ref[...] = total[d * 32 : (d + 1) * 32]

    return call(
        kernel, "turn_narrow", [whole((32, width), BF16)] * 4, (keep, landed), after=after
    )


def near(right, left, far_right, far_left, after=()):
    half = right.shape[1] // 2

    def kernel(right_ref, left_ref, far_right_ref, far_left_ref, to_right_ref, to_left_ref):
        to_right_ref[:, :half] = plus(right_ref[:, :half], far_right_ref[...]).astype(BF16)
        to_right_ref[:, half:] = right_ref[:, half:]
        to_left_ref[:, :half] = left_ref[:, :half]
        to_left_ref[:, half:] = plus(left_ref[:, half:], far_left_ref[...]).astype(BF16)

    return call(
        kernel, "near", [whole(right.shape, BF16)] * 2, (right, left, far_right, far_left), after=after
    )


def turn_wide(here, from_left, from_right, after=()):
    width = here.shape[1]

    def kernel(here_ref, from_left_ref, from_right_ref, keep_ref, send_ref):
        total = plus(here_ref[...], from_left_ref[...], from_right_ref[...])
        keep_ref[...] = total[:32]
        send_ref[...] = total[32:].astype(BF16)

    return call(
        kernel,
        "turn_wide",
        [whole((32, width), F32), whole((32, width), BF16)],
        (here, from_left, from_right),
        after=after,
    )


def add_parts(parts, after=(), dtype=BF16):
    def kernel(*refs):
        refs[-1][...] = plus(*[ref[...] for ref in refs[:-1]]).astype(dtype)

    return call(kernel, "add_parts", [whole(parts[0].shape, dtype)], parts, after=after)


def lanes(rows):
    return lax.broadcasted_iota(jnp.int32, (rows, 128), 1)


def resident_slot(slot, target_ref):
    for k in range(CHIPS):
        slot = jnp.where(slot == target_ref[k], -1, slot)
    return slot


def shrink_kernel(x_ref, down_ref, slot_ref, target_ref, maps_ref, out_ref):
    x = x_ref[...]
    row = lax.broadcasted_iota(jnp.int32, (512, 512), 0)
    col = lax.broadcasted_iota(jnp.int32, (512, 512), 1)
    source = jnp.where(col < 256, 2 * col, 2 * (col - 256) + 1)
    chooser = jnp.where(row == source, 1.0, 0.0).astype(BF16)
    split = jnp.dot(x, chooser, preferred_element_type=F32).astype(BF16)
    even, odd = split[:, :256], split[:, 256:]
    slot = jnp.broadcast_to(slot_ref[...], (512, 128))
    kept = resident_slot(slot, target_ref)
    high = (lanes(512) >= RANK).astype(jnp.int32)
    acc = jnp.zeros((512, 128), F32)
    for k in range(CHIPS):
        part = jnp.dot(x, down_ref[:, k * 128 : (k + 1) * 128], preferred_element_type=F32)
        acc += jnp.where(kept == 2 * k + high, part, 0.0)
        maps = maps_ref[2 * k]
        part = jnp.where(
            high == 0,
            jnp.dot(even, maps, preferred_element_type=F32),
            jnp.dot(odd, maps, preferred_element_type=F32),
        )
        acc += jnp.where(slot == target_ref[k], part, 0.0)
    acc = acc + pltpu.roll(acc, RANK, 1)
    out_ref[...] = jnp.where(lanes(256) < RANK, acc[:256], acc[256:]).astype(BF16)


def shrink_part(x, down, slot, target, maps, after=()):
    return call(
        shrink_kernel,
        "shrink_part",
        [whole((256, 128), BF16)],
        (x, down, slot, target, maps),
        [VM, VM, VM, SM, VM],
        after,
    )


def up_table_kernel(up_ref, target_ref, maps_ref, table_ref):
    table_ref[...] = up_ref[...]
    row = lax.broadcasted_iota(jnp.int32, (256, 512), 0)
    col = lax.broadcasted_iota(jnp.int32, (256, 512), 1)
    to_even = jnp.where(col == 2 * row, 1.0, 0.0).astype(BF16)
    to_odd = jnp.where(col == 2 * row + 1, 1.0, 0.0).astype(BF16)
    turn = (((0,), (0,)), ((), ()))
    for k in range(CHIPS):
        maps = maps_ref[2 * k + 1]
        even = lax.dot_general(maps, to_even, turn, preferred_element_type=F32)
        odd = lax.dot_general(maps, to_odd, turn, preferred_element_type=F32)
        table_ref[rows_at(target_ref[k], RANK), :] = (even[:RANK] + odd[RANK:]).astype(BF16)


def up_table(up, target, maps, after=()):
    return call(
        up_table_kernel, "up_table", [whole((1024, 512), BF16)], (up, target, maps), [VM, SM, VM], after
    )


def raise_kernel(mine_ref, other_ref, table_ref, slot_ref, out_ref):
    packed = (mine_ref[...].astype(F32) + other_ref[...].astype(F32)).astype(BF16).astype(F32)
    turned = pltpu.roll(packed, RANK, 1)
    left = lanes(256) < RANK
    both = jnp.concatenate(
        [jnp.where(left, packed, turned), jnp.where(left, turned, packed)], axis=0
    )
    slot = jnp.broadcast_to(slot_ref[...], (512, 128))
    high = (lanes(512) >= RANK).astype(jnp.int32)
    raised = jnp.concatenate(
        [jnp.where(slot == 2 * j + high, both, 0.0).astype(BF16) for j in range(CHIPS)], axis=1
    )
    total = jnp.dot(raised, table_ref[...], preferred_element_type=F32)
    out_ref[...] = (SCALE * total).astype(BF16).reshape(16, 32, 512)


def raise_features(mine, other, table, slot, after=()):
    return call(
        raise_kernel,
        "raise_features",
        [whole((16, 32, 512), BF16)],
        (mine, other, table, slot),
        after=after,
    )


def finish_kernel(
    residual_ref, wide_ref, wide_y_ref, narrow_ref, delta_ref, out_ref
):
    for t in range(16):
        cols = slice(t * 512, (t + 1) * 512)
        if (t + 1) * 512 <= WIDE:
            base = wide_ref[:, cols] + wide_y_ref[:, cols].astype(F32)
        else:
            part = slice(t * 512 - WIDE, (t + 1) * 512 - WIDE)
            base = narrow_ref[:, part]
        out_ref[:, cols] = (
            residual_ref[:, cols].astype(F32) + base + delta_ref[t].astype(F32)
        ).astype(BF16)


def local(
    attention_output,
    output_projection_weight,
    residual,
    resident_down_maps,
    resident_up_maps,
    fresh_adapter_bundle,
    fresh_slot_targets,
    request_adapter_slot,
):
    x, w = attention_output, output_projection_weight
    slot = request_adapter_slot.reshape(512, 1)
    target = fresh_slot_targets

    maps = lax.all_to_all(
        fresh_adapter_bundle.reshape(16, 256, 128), "tp", split_axis=0, concat_axis=0, tiled=True
    )
    narrow = x.shape[0] * 16 - WIDE
    *narrow_away, narrow_own, mark = product(x, w, Y_MAJOR, WIDE, narrow, NARROW_CHUNK)
    narrow_in = [send(away, 0, 0, 1) for away in narrow_away]
    *wide_away, wide_own, mark = product(x, w, X_MAJOR, 0, WIDE, WIDE_CHUNK, [mark])
    wide_in = [send(away, 0, 0, 1) for away in wide_away]

    part, mark = shrink_part(x, resident_down_maps, slot, target, maps, [mark])
    part_in = send(part, 0, 0, 1)

    keep, away, mark = chip_sum("chip_narrow", narrow_own, narrow_in, 2, None, [mark])
    narrow_y = send(away, 1, 0, 0)
    here, right, far_right, far_left, left, mark = chip_sum(
        "chip_wide", wide_own, wide_in, 4, 2, [mark]
    )
    far_right, far_left = send(far_right, 0, 1, 0), send(far_left, 0, 3, 0)
    part, mark = add_parts([part, part_in], [mark])
    part_in = trade(part, lambda x: x ^ 1)
    part, mark = add_parts([part, part_in], [mark])
    part_in = trade(part, lambda x: 3 - x)
    part, mark = add_parts([part, part_in], [mark])
    other = send(part, 1, 0, 0)

    right, left, mark = near(right, left, far_right, far_left, [mark])
    from_left, from_right = send(right, 0, 1, 0), send(left, 0, 3, 0)
    table, mark = up_table(resident_up_maps, target, maps, [mark])
    *low, mark = turn_narrow(keep, narrow_y, [mark])
    low_in = [send(low[d], 0, d, 0) for d in (1, 2, 3)]
    raised, mark = raise_features(part, other, table, slot, [mark])
    delta = lax.all_to_all(raised, "tp", split_axis=0, concat_axis=0, tiled=True)

    narrow_sum, mark = add_parts([low[0], *low_in], [mark], F32)
    wide_keep, wide_send, mark = turn_wide(here, from_left, from_right, [mark])
    wide_y = send(wide_send, 1, 0, 0)
    hidden, _ = call(
        finish_kernel,
        "finish",
        [whole((32, 8192), BF16)],
        (residual, wide_keep, wide_y, narrow_sum, delta),
    )
    return hidden


def solution(mesh):
    return jax.shard_map(
        local,
        mesh=mesh,
        in_specs=(
            P("grp", "tp"),
            P("tp", None),
            P("tp", "grp"),
            P("tp", "grp"),
            P("grp", "tp"),
            P(("grp", "tp"), None, None),
            P("grp"),
            P("grp"),
        ),
        out_specs=P("tp", "grp"),
        check_vma=False,
    )
```

```python
import jax
import jax.numpy as jnp
from jax import lax
from jax.experimental import pallas as pl
from jax.experimental.pallas import tpu as pltpu
from jax.sharding import PartitionSpec as P

RANK = 64
SLOTS = 16
CHIPS = 8
SCALE = 0.5
F32 = jnp.float32
BF16 = jnp.bfloat16
WIDE = 4608
VMEM_LIMIT = 16 * 1024 * 1024
PRODUCT_LIMIT = 56 * 1024 * 1024
CHIP_LIMIT = 48 * 1024 * 1024
NARROW_CHUNK = 1792
WIDE_CHUNK = 1536


def place(y, x, core):
    return ((y % 2) * 4 + x % 4) * 2 + core % 2


def route(yy, xx, cc):
    return [
        (place(y, x, c), place(y + yy, x + xx, c + cc))
        for y in range(2)
        for x in range(4)
        for c in range(2)
    ]


def send(array, yy, xx, cc):
    return lax.ppermute(array, "tp", route(yy, xx, cc))


def trade(array, partner_of):
    pairs = [
        (place(y, x, c), place(y, partner_of(x), c))
        for y in range(2)
        for x in range(4)
        for c in range(2)
    ]
    return lax.ppermute(array, "tp", pairs)


def spot():
    t = lax.axis_index("tp")
    return t // 8, lax.rem(t // 2, 4), lax.rem(t, 2)


def partner(yy, xx, cc):
    y, x, c = spot()
    return (lax.rem(y + yy, 2) * 4 + lax.rem(x + xx, 4)) * 2 + lax.rem(c + cc, 2)


def rows_at(index, size):
    return pl.ds(pl.multiple_of(index * size, size), size)


def whole(shape, dtype):
    return jax.ShapeDtypeStruct(shape, dtype)


def plus(a, *others):
    total = a.astype(F32)
    for other in others:
        total = total + other.astype(F32)
    return total


VM = pl.BlockSpec(memory_space=pltpu.VMEM)
SM = pl.BlockSpec(memory_space=pltpu.SMEM)
LATER = pl.BlockSpec(memory_space=pl.ANY)


def call(kernel, name, out_shape, args, specs=None, after=(), limit=VMEM_LIMIT, out_specs=None, scratch_shapes=()):
    count, outs = len(args), len(out_shape)

    def body(*refs):
        results = refs[count + len(after) :]
        results[outs][...] = jnp.zeros((8, 128), F32)
        kernel(*refs[:count], *results[:outs], *results[outs + 1 :])

    return pl.pallas_call(
        body,
        in_specs=list(specs or [VM] * count) + [LATER] * len(after),
        out_specs=list(out_specs or [VM] * outs) + [VM],
        out_shape=list(out_shape) + [whole((8, 128), F32)],
        scratch_shapes=list(scratch_shapes),
        compiler_params=pltpu.CompilerParams(vmem_limit_bytes=limit),
        cost_estimate=pl.CostEstimate(flops=1024, bytes_accessed=1024, transcendentals=0),
        name=name,
    )(*args, *after)


X_MAJOR = [(yy, xx) for xx in range(4) for yy in range(2)]
Y_MAJOR = [(yy, xx) for yy in range(2) for xx in range(4)]


HBM = pl.BlockSpec(memory_space=pltpu.HBM)


def product(x, w, order, first, width, chunk, after=()):
    chunks = width // chunk
    sub = chunk // 2
    subs = 2 * chunks

    def kernel(x_ref, w_ref, *refs):
        away_refs = refs[:chunks]
        own_ref, rows_ref, held_ref, done_ref, sems, away_sems, own_sems = refs[chunks:]

        def copy(i):
            cols = pl.ds(pl.multiple_of(first + i * sub, 128), sub)
            return pltpu.make_async_copy(w_ref.at[:, cols], held_ref.at[i], sems.at[i])

        def leave(i):
            return pltpu.make_async_copy(
                done_ref.at[i, :256],
                away_refs[i // 2].at[:, pl.ds(i % 2 * sub, sub)],
                away_sems.at[i],
            )

        def stay(i):
            return pltpu.make_async_copy(
                done_ref.at[i, 256:], own_ref.at[:, pl.ds(i * sub, sub)], own_sems.at[i]
            )

        for i in range(subs):
            copy(i).start()
        for i, (yy, xx) in enumerate(order):
            for cc, top in ((1, 0), (0, 256)):
                rows_ref[top + i * 32 : top + (i + 1) * 32, :] = x_ref[
                    rows_at(partner(yy, xx, cc), 32), :
                ]
        for i in range(subs):
            copy(i).wait()
            done_ref[i] = jnp.dot(
                rows_ref[...], held_ref[i], preferred_element_type=F32
            ).astype(BF16)
            leave(i).start()
            stay(i).start()
        for i in range(subs):
            leave(i).wait()
            stay(i).wait()

    return call(
        kernel,
        "product",
        [whole((256, chunk), BF16)] * chunks + [whole((256, width), BF16)],
        (x, w),
        [VM, HBM],
        after,
        limit=PRODUCT_LIMIT,
        out_specs=[HBM] * (chunks + 1),
        scratch_shapes=[
            pltpu.VMEM((512, 512), BF16),
            pltpu.VMEM((subs, 512, sub), BF16),
            pltpu.VMEM((subs, 512, sub), BF16),
            pltpu.SemaphoreType.DMA((subs,)),
            pltpu.SemaphoreType.DMA((subs,)),
            pltpu.SemaphoreType.DMA((subs,)),
        ],
    )


def chip_sum(name, own, away, blocks, split, after=()):
    chunk = away[0].shape[1]
    sub = chunk // 2
    subs = 2 * len(away)
    width = own.shape[1]
    half = width // 2
    step = 128
    size = own.shape[0] // blocks
    shapes = []
    for d in range(blocks):
        shapes += [(size, half)] * 2 if d == split else [(size, width)]

    def kernel(own_ref, *refs):
        away_refs, outs = refs[: len(away)], refs[len(away) : len(away) + len(shapes)]
        held_ref, came_ref, own_sems, away_sems = refs[len(away) + len(shapes) :]

        def load_own(i):
            return pltpu.make_async_copy(
                own_ref.at[:, pl.ds(i * sub, sub)], held_ref.at[i], own_sems.at[i]
            )

        def load_away(i):
            return pltpu.make_async_copy(
                away_refs[i // 2].at[:, pl.ds(i % 2 * sub, sub)], came_ref.at[i], away_sems.at[i]
            )

        for i in range(subs):
            load_own(i).start()
            load_away(i).start()
        for i in range(subs):
            load_own(i).wait()
            load_away(i).wait()
            for part in range(0, sub, step):
                first = i * sub + part
                total = plus(
                    held_ref[i, :, part : part + step], came_ref[i, :, part : part + step]
                ).astype(BF16)
                place_at = 0
                for d in range(blocks):
                    piece = total[d * size : (d + 1) * size]
                    if d == split:
                        side, at = divmod(first, half)
                        outs[place_at + side][:, at : at + step] = piece
                        place_at += 2
                    else:
                        outs[place_at][:, first : first + step] = piece
                        place_at += 1

    return call(
        kernel,
        name,
        [whole(shape, BF16) for shape in shapes],
        (own, *away),
        [HBM] * (1 + len(away)),
        after,
        limit=CHIP_LIMIT,
        scratch_shapes=[
            pltpu.VMEM((subs, own.shape[0], sub), BF16),
            pltpu.VMEM((subs, own.shape[0], sub), BF16),
            pltpu.SemaphoreType.DMA((subs,)),
            pltpu.SemaphoreType.DMA((subs,)),
        ],
    )


def turn_narrow(keep, landed, after=()):
    width = keep.shape[1]

    def kernel(keep_ref, landed_ref, *refs):
        total = plus(keep_ref[...], landed_ref[...]).astype(BF16)
        for d, ref in enumerate(refs):
            ref[...] = total[d * 32 : (d + 1) * 32]

    return call(
        kernel, "turn_narrow", [whole((32, width), BF16)] * 4, (keep, landed), after=after
    )


def near(right, left, far_right, far_left, after=()):
    half = right.shape[1] // 2

    def kernel(right_ref, left_ref, far_right_ref, far_left_ref, to_right_ref, to_left_ref):
        to_right_ref[:, :half] = plus(right_ref[:, :half], far_right_ref[...]).astype(BF16)
        to_right_ref[:, half:] = right_ref[:, half:]
        to_left_ref[:, :half] = left_ref[:, :half]
        to_left_ref[:, half:] = plus(left_ref[:, half:], far_left_ref[...]).astype(BF16)

    return call(
        kernel, "near", [whole(right.shape, BF16)] * 2, (right, left, far_right, far_left), after=after
    )


def turn_wide(here, from_left, from_right, after=()):
    width = here.shape[1]

    def kernel(here_ref, from_left_ref, from_right_ref, keep_ref, send_ref):
        total = plus(here_ref[...], from_left_ref[...], from_right_ref[...])
        keep_ref[...] = total[:32]
        send_ref[...] = total[32:].astype(BF16)

    return call(
        kernel,
        "turn_wide",
        [whole((32, width), F32), whole((32, width), BF16)],
        (here, from_left, from_right),
        after=after,
    )


def add_parts(parts, after=(), dtype=BF16):
    def kernel(*refs):
        refs[-1][...] = plus(*[ref[...] for ref in refs[:-1]]).astype(dtype)

    return call(kernel, "add_parts", [whole(parts[0].shape, dtype)], parts, after=after)


def lanes(rows):
    return lax.broadcasted_iota(jnp.int32, (rows, 128), 1)


def resident_slot(slot, target_ref):
    for k in range(CHIPS):
        slot = jnp.where(slot == target_ref[k], -1, slot)
    return slot


def shrink_kernel(x_ref, down_ref, slot_ref, target_ref, maps_ref, out_ref):
    x = x_ref[...]
    row = lax.broadcasted_iota(jnp.int32, (512, 512), 0)
    col = lax.broadcasted_iota(jnp.int32, (512, 512), 1)
    source = jnp.where(col < 256, 2 * col, 2 * (col - 256) + 1)
    chooser = jnp.where(row == source, 1.0, 0.0).astype(BF16)
    split = jnp.dot(x, chooser, preferred_element_type=F32).astype(BF16)
    even, odd = split[:, :256], split[:, 256:]
    slot = jnp.broadcast_to(slot_ref[...], (512, 128))
    kept = resident_slot(slot, target_ref)
    high = (lanes(512) >= RANK).astype(jnp.int32)
    acc = jnp.zeros((512, 128), F32)
    for k in range(CHIPS):
        part = jnp.dot(x, down_ref[:, k * 128 : (k + 1) * 128], preferred_element_type=F32)
        acc += jnp.where(kept == 2 * k + high, part, 0.0)
        maps = maps_ref[2 * k]
        part = jnp.where(
            high == 0,
            jnp.dot(even, maps, preferred_element_type=F32),
            jnp.dot(odd, maps, preferred_element_type=F32),
        )
        acc += jnp.where(slot == target_ref[k], part, 0.0)
    acc = acc + pltpu.roll(acc, RANK, 1)
    out_ref[...] = jnp.where(lanes(256) < RANK, acc[:256], acc[256:]).astype(BF16)


def shrink_part(x, down, slot, target, maps, after=()):
    return call(
        shrink_kernel,
        "shrink_part",
        [whole((256, 128), BF16)],
        (x, down, slot, target, maps),
        [VM, VM, VM, SM, VM],
        after,
    )


def up_table_kernel(up_ref, target_ref, maps_ref, table_ref):
    table_ref[...] = up_ref[...]
    row = lax.broadcasted_iota(jnp.int32, (256, 512), 0)
    col = lax.broadcasted_iota(jnp.int32, (256, 512), 1)
    to_even = jnp.where(col == 2 * row, 1.0, 0.0).astype(BF16)
    to_odd = jnp.where(col == 2 * row + 1, 1.0, 0.0).astype(BF16)
    turn = (((0,), (0,)), ((), ()))
    for k in range(CHIPS):
        maps = maps_ref[2 * k + 1]
        even = lax.dot_general(maps, to_even, turn, preferred_element_type=F32)
        odd = lax.dot_general(maps, to_odd, turn, preferred_element_type=F32)
        table_ref[rows_at(target_ref[k], RANK), :] = (even[:RANK] + odd[RANK:]).astype(BF16)


def up_table(up, target, maps, after=()):
    return call(
        up_table_kernel, "up_table", [whole((1024, 512), BF16)], (up, target, maps), [VM, SM, VM], after
    )


def raise_kernel(mine_ref, other_ref, table_ref, slot_ref, out_ref):
    packed = (mine_ref[...].astype(F32) + other_ref[...].astype(F32)).astype(BF16).astype(F32)
    turned = pltpu.roll(packed, RANK, 1)
    left = lanes(256) < RANK
    both = jnp.concatenate(
        [jnp.where(left, packed, turned), jnp.where(left, turned, packed)], axis=0
    )
    slot = jnp.broadcast_to(slot_ref[...], (512, 128))
    high = (lanes(512) >= RANK).astype(jnp.int32)
    raised = jnp.concatenate(
        [jnp.where(slot == 2 * j + high, both, 0.0).astype(BF16) for j in range(CHIPS)], axis=1
    )
    total = jnp.dot(raised, table_ref[...], preferred_element_type=F32)
    out_ref[...] = (SCALE * total).astype(BF16).reshape(16, 32, 512)


def raise_features(mine, other, table, slot, after=()):
    return call(
        raise_kernel,
        "raise_features",
        [whole((16, 32, 512), BF16)],
        (mine, other, table, slot),
        after=after,
    )


def finish_kernel(
    residual_ref, wide_ref, wide_y_ref, narrow_ref, delta_ref, out_ref
):
    for t in range(16):
        cols = slice(t * 512, (t + 1) * 512)
        if (t + 1) * 512 <= WIDE:
            base = wide_ref[:, cols] + wide_y_ref[:, cols].astype(F32)
        else:
            part = slice(t * 512 - WIDE, (t + 1) * 512 - WIDE)
            base = narrow_ref[:, part]
        out_ref[:, cols] = (
            residual_ref[:, cols].astype(F32) + base + delta_ref[t].astype(F32)
        ).astype(BF16)


def local(
    attention_output,
    output_projection_weight,
    residual,
    resident_down_maps,
    resident_up_maps,
    fresh_adapter_bundle,
    fresh_slot_targets,
    request_adapter_slot,
):
    x, w = attention_output, output_projection_weight
    slot = request_adapter_slot.reshape(512, 1)
    target = fresh_slot_targets

    maps = lax.all_to_all(
        fresh_adapter_bundle.reshape(16, 256, 128), "tp", split_axis=0, concat_axis=0, tiled=True
    )
    narrow = x.shape[0] * 16 - WIDE
    *narrow_away, narrow_own, mark = product(x, w, Y_MAJOR, WIDE, narrow, NARROW_CHUNK, [slot])
    narrow_in = [send(away, 0, 0, 1) for away in narrow_away]
    *wide_away, wide_own, mark = product(x, w, X_MAJOR, 0, WIDE, WIDE_CHUNK, [mark])
    wide_in = [send(away, 0, 0, 1) for away in wide_away]

    keep, away, mark = chip_sum(
        "chip_narrow", narrow_own, narrow_in, 2, None, [mark, maps]
    )
    narrow_y = send(away, 1, 0, 0)
    here, right, far_right, far_left, left, mark = chip_sum(
        "chip_wide", wide_own, wide_in, 4, 2, [away]
    )
    far_right, far_left = send(far_right, 0, 1, 0), send(far_left, 0, 3, 0)

    part, mark = shrink_part(x, resident_down_maps, slot, target, maps, [mark])
    part_in = send(part, 0, 0, 1)
    part, mark = add_parts([part, part_in], [mark])
    part_in = trade(part, lambda x: x ^ 1)
    part, mark = add_parts([part, part_in], [mark])
    part_in = trade(part, lambda x: 3 - x)

    right, left, mark = near(right, left, far_right, far_left, [mark])
    from_left, from_right = send(right, 0, 1, 0), send(left, 0, 3, 0)
    part, mark = add_parts([part, part_in], [mark])
    other = send(part, 1, 0, 0)
    table, mark = up_table(resident_up_maps, target, maps, [mark])
    *low, mark = turn_narrow(keep, narrow_y, [mark])
    low_in = [send(low[d], 0, d, 0) for d in (1, 2, 3)]
    raised, mark = raise_features(part, other, table, slot, [mark])
    delta = lax.all_to_all(raised, "tp", split_axis=0, concat_axis=0, tiled=True)

    narrow_sum, mark = add_parts([low[0], *low_in], [mark], F32)
    wide_keep, wide_send, mark = turn_wide(here, from_left, from_right, [mark])
    wide_y = send(wide_send, 1, 0, 0)
    hidden, _ = call(
        finish_kernel,
        "finish",
        [whole((32, 8192), BF16)],
        (residual, wide_keep, wide_y, narrow_sum, delta),
    )
    return hidden


def solution(mesh):
    return jax.shard_map(
        local,
        mesh=mesh,
        in_specs=(
            P("grp", "tp"),
            P("tp", None),
            P("tp", "grp"),
            P("tp", "grp"),
            P("grp", "tp"),
            P(("grp", "tp"), None, None),
            P("grp"),
            P("grp"),
        ),
        out_specs=P("tp", "grp"),
        check_vma=False,
    )
```

```python
import jax
import jax.numpy as jnp
from jax import lax
from jax.experimental import pallas as pl
from jax.experimental.pallas import tpu as pltpu
from jax.sharding import PartitionSpec as P

RANK = 64
SLOTS = 16
CHIPS = 8
SCALE = 0.5
F32 = jnp.float32
BF16 = jnp.bfloat16
WIDE = 4608
CUT = 2560
VMEM_LIMIT = 16 * 1024 * 1024
PRODUCT_LIMIT = 56 * 1024 * 1024
CHIP_LIMIT = 48 * 1024 * 1024
NARROW_CHUNK = 1792
WIDE_CHUNK = 1536


def place(y, x, core):
    return ((y % 2) * 4 + x % 4) * 2 + core % 2


def route(yy, xx, cc):
    return [
        (place(y, x, c), place(y + yy, x + xx, c + cc))
        for y in range(2)
        for x in range(4)
        for c in range(2)
    ]


def send(array, yy, xx, cc):
    return lax.ppermute(array, "tp", route(yy, xx, cc))


def trade(array, partner_of):
    pairs = [
        (place(y, x, c), place(y, partner_of(x), c))
        for y in range(2)
        for x in range(4)
        for c in range(2)
    ]
    return lax.ppermute(array, "tp", pairs)


def spot():
    t = lax.axis_index("tp")
    return t // 8, lax.rem(t // 2, 4), lax.rem(t, 2)


def partner(yy, xx, cc):
    y, x, c = spot()
    return (lax.rem(y + yy, 2) * 4 + lax.rem(x + xx, 4)) * 2 + lax.rem(c + cc, 2)


def rows_at(index, size):
    return pl.ds(pl.multiple_of(index * size, size), size)


def whole(shape, dtype):
    return jax.ShapeDtypeStruct(shape, dtype)


def plus(a, *others):
    total = a.astype(F32)
    for other in others:
        total = total + other.astype(F32)
    return total


VM = pl.BlockSpec(memory_space=pltpu.VMEM)
SM = pl.BlockSpec(memory_space=pltpu.SMEM)
LATER = pl.BlockSpec(memory_space=pl.ANY)


def call(kernel, name, out_shape, args, specs=None, after=(), limit=VMEM_LIMIT, out_specs=None, scratch_shapes=()):
    count, outs = len(args), len(out_shape)

    def body(*refs):
        results = refs[count + len(after) :]
        results[outs][...] = jnp.zeros((8, 128), F32)
        kernel(*refs[:count], *results[:outs], *results[outs + 1 :])

    return pl.pallas_call(
        body,
        in_specs=list(specs or [VM] * count) + [LATER] * len(after),
        out_specs=list(out_specs or [VM] * outs) + [VM],
        out_shape=list(out_shape) + [whole((8, 128), F32)],
        scratch_shapes=list(scratch_shapes),
        compiler_params=pltpu.CompilerParams(vmem_limit_bytes=limit),
        cost_estimate=pl.CostEstimate(flops=1024, bytes_accessed=1024, transcendentals=0),
        name=name,
    )(*args, *after)


X_MAJOR = [(yy, xx) for xx in range(4) for yy in range(2)]
Y_MAJOR = [(yy, xx) for yy in range(2) for xx in range(4)]


HBM = pl.BlockSpec(memory_space=pltpu.HBM)


def product(x, w, order, first, width, chunk, after=()):
    chunks = width // chunk
    sub = chunk // 2
    subs = 2 * chunks

    def kernel(x_ref, w_ref, *refs):
        away_refs = refs[:chunks]
        own_ref, rows_ref, held_ref, done_ref, sems, away_sems, own_sems = refs[chunks:]

        def copy(i):
            cols = pl.ds(pl.multiple_of(first + i * sub, 128), sub)
            return pltpu.make_async_copy(w_ref.at[:, cols], held_ref.at[i], sems.at[i])

        def leave(i):
            return pltpu.make_async_copy(
                done_ref.at[i, :256],
                away_refs[i // 2].at[:, pl.ds(i % 2 * sub, sub)],
                away_sems.at[i],
            )

        def stay(i):
            return pltpu.make_async_copy(
                done_ref.at[i, 256:], own_ref.at[:, pl.ds(i * sub, sub)], own_sems.at[i]
            )

        for i in range(subs):
            copy(i).start()
        for i, (yy, xx) in enumerate(order):
            for cc, top in ((1, 0), (0, 256)):
                rows_ref[top + i * 32 : top + (i + 1) * 32, :] = x_ref[
                    rows_at(partner(yy, xx, cc), 32), :
                ]
        for i in range(subs):
            copy(i).wait()
            done_ref[i] = jnp.dot(
                rows_ref[...], held_ref[i], preferred_element_type=F32
            ).astype(BF16)
            leave(i).start()
            stay(i).start()
        for i in range(subs):
            leave(i).wait()
            stay(i).wait()

    return call(
        kernel,
        "product",
        [whole((256, chunk), BF16)] * chunks + [whole((256, width), BF16)],
        (x, w),
        [VM, HBM],
        after,
        limit=PRODUCT_LIMIT,
        out_specs=[HBM] * (chunks + 1),
        scratch_shapes=[
            pltpu.VMEM((512, 512), BF16),
            pltpu.VMEM((subs, 512, sub), BF16),
            pltpu.VMEM((subs, 512, sub), BF16),
            pltpu.SemaphoreType.DMA((subs,)),
            pltpu.SemaphoreType.DMA((subs,)),
            pltpu.SemaphoreType.DMA((subs,)),
        ],
    )


def chip_sum(name, own, away, blocks, split, after=()):
    chunk = away[0].shape[1]
    sub = chunk // 2
    subs = 2 * len(away)
    width = own.shape[1]
    half = width // 2
    step = 128
    size = own.shape[0] // blocks
    shapes = []
    for d in range(blocks):
        shapes += [(size, half)] * 2 if d == split else [(size, width)]

    def kernel(own_ref, *refs):
        away_refs, outs = refs[: len(away)], refs[len(away) : len(away) + len(shapes)]
        held_ref, came_ref, own_sems, away_sems = refs[len(away) + len(shapes) :]

        def load_own(i):
            return pltpu.make_async_copy(
                own_ref.at[:, pl.ds(i * sub, sub)], held_ref.at[i], own_sems.at[i]
            )

        def load_away(i):
            return pltpu.make_async_copy(
                away_refs[i // 2].at[:, pl.ds(i % 2 * sub, sub)], came_ref.at[i], away_sems.at[i]
            )

        for i in range(subs):
            load_own(i).start()
            load_away(i).start()
        for i in range(subs):
            load_own(i).wait()
            load_away(i).wait()
            for part in range(0, sub, step):
                first = i * sub + part
                total = plus(
                    held_ref[i, :, part : part + step], came_ref[i, :, part : part + step]
                ).astype(BF16)
                place_at = 0
                for d in range(blocks):
                    piece = total[d * size : (d + 1) * size]
                    if d == split:
                        side, at = divmod(first, half)
                        outs[place_at + side][:, at : at + step] = piece
                        place_at += 2
                    else:
                        outs[place_at][:, first : first + step] = piece
                        place_at += 1

    return call(
        kernel,
        name,
        [whole(shape, BF16) for shape in shapes],
        (own, *away),
        [HBM] * (1 + len(away)),
        after,
        limit=CHIP_LIMIT,
        scratch_shapes=[
            pltpu.VMEM((subs, own.shape[0], sub), BF16),
            pltpu.VMEM((subs, own.shape[0], sub), BF16),
            pltpu.SemaphoreType.DMA((subs,)),
            pltpu.SemaphoreType.DMA((subs,)),
        ],
    )


def turn_narrow(keep, landed, after=()):
    width = keep.shape[1]

    def kernel(keep_ref, landed_ref, *refs):
        total = plus(keep_ref[...], landed_ref[...]).astype(BF16)
        for d, ref in enumerate(refs):
            ref[...] = total[d * 32 : (d + 1) * 32]

    return call(
        kernel, "turn_narrow", [whole((32, width), BF16)] * 4, (keep, landed), after=after
    )


def near(right, left, far_right, far_left, after=()):
    half = right.shape[1] // 2

    def kernel(right_ref, left_ref, far_right_ref, far_left_ref, to_right_ref, to_left_ref):
        to_right_ref[:, :half] = plus(right_ref[:, :half], far_right_ref[...]).astype(BF16)
        to_right_ref[:, half:] = right_ref[:, half:]
        to_left_ref[:, :half] = left_ref[:, :half]
        to_left_ref[:, half:] = plus(left_ref[:, half:], far_left_ref[...]).astype(BF16)

    return call(
        kernel, "near", [whole(right.shape, BF16)] * 2, (right, left, far_right, far_left), after=after
    )


def turn_wide(here, from_left, from_right, after=()):
    width = here.shape[1]

    def kernel(here_ref, from_left_ref, from_right_ref, keep_ref, send_ref, rest_ref):
        total = plus(here_ref[...], from_left_ref[...], from_right_ref[...])
        keep_ref[...] = total[:32]
        send_ref[...] = total[32:, :CUT].astype(BF16)
        rest_ref[...] = total[32:, CUT:].astype(BF16)

    return call(
        kernel,
        "turn_wide",
        [whole((32, width), F32), whole((32, CUT), BF16), whole((32, width - CUT), BF16)],
        (here, from_left, from_right),
        after=after,
    )


def add_parts(parts, after=(), dtype=BF16):
    def kernel(*refs):
        refs[-1][...] = plus(*[ref[...] for ref in refs[:-1]]).astype(dtype)

    return call(kernel, "add_parts", [whole(parts[0].shape, dtype)], parts, after=after)


def lanes(rows):
    return lax.broadcasted_iota(jnp.int32, (rows, 128), 1)


def slot_columns(slot_ref):
    row = slot_ref[...].astype(F32)
    return jnp.broadcast_to(row, (128, 512)).T.astype(jnp.int32)


def resident_slot(slot, target_ref):
    for k in range(CHIPS):
        slot = jnp.where(slot == target_ref[k], -1, slot)
    return slot


def shrink_kernel(x_ref, down_ref, slot_ref, target_ref, maps_ref, out_ref):
    x = x_ref[...]
    row = lax.broadcasted_iota(jnp.int32, (512, 512), 0)
    col = lax.broadcasted_iota(jnp.int32, (512, 512), 1)
    source = jnp.where(col < 256, 2 * col, 2 * (col - 256) + 1)
    chooser = jnp.where(row == source, 1.0, 0.0).astype(BF16)
    split = jnp.dot(x, chooser, preferred_element_type=F32).astype(BF16)
    even, odd = split[:, :256], split[:, 256:]
    slot = slot_columns(slot_ref)
    kept = resident_slot(slot, target_ref)
    high = (lanes(512) >= RANK).astype(jnp.int32)
    acc = jnp.zeros((512, 128), F32)
    for k in range(CHIPS):
        part = jnp.dot(x, down_ref[:, k * 128 : (k + 1) * 128], preferred_element_type=F32)
        acc += jnp.where(kept == 2 * k + high, part, 0.0)
        maps = maps_ref[2 * k]
        part = jnp.where(
            high == 0,
            jnp.dot(even, maps, preferred_element_type=F32),
            jnp.dot(odd, maps, preferred_element_type=F32),
        )
        acc += jnp.where(slot == target_ref[k], part, 0.0)
    acc = acc + pltpu.roll(acc, RANK, 1)
    out_ref[...] = jnp.where(lanes(256) < RANK, acc[:256], acc[256:]).astype(BF16)


def shrink_part(x, down, slot, target, maps, after=()):
    return call(
        shrink_kernel,
        "shrink_part",
        [whole((256, 128), BF16)],
        (x, down, slot, target, maps),
        [VM, VM, VM, SM, VM],
        after,
    )


def up_table_kernel(up_ref, target_ref, maps_ref, table_ref):
    table_ref[...] = up_ref[...]
    row = lax.broadcasted_iota(jnp.int32, (256, 512), 0)
    col = lax.broadcasted_iota(jnp.int32, (256, 512), 1)
    to_even = jnp.where(col == 2 * row, 1.0, 0.0).astype(BF16)
    to_odd = jnp.where(col == 2 * row + 1, 1.0, 0.0).astype(BF16)
    turn = (((0,), (0,)), ((), ()))
    for k in range(CHIPS):
        maps = maps_ref[2 * k + 1]
        even = lax.dot_general(maps, to_even, turn, preferred_element_type=F32)
        odd = lax.dot_general(maps, to_odd, turn, preferred_element_type=F32)
        table_ref[rows_at(target_ref[k], RANK), :] = (even[:RANK] + odd[RANK:]).astype(BF16)


def up_table(up, target, maps, after=()):
    return call(
        up_table_kernel, "up_table", [whole((1024, 512), BF16)], (up, target, maps), [VM, SM, VM], after
    )


def raise_kernel(mine_ref, other_ref, table_ref, slot_ref, out_ref):
    packed = (mine_ref[...].astype(F32) + other_ref[...].astype(F32)).astype(BF16).astype(F32)
    turned = pltpu.roll(packed, RANK, 1)
    left = lanes(256) < RANK
    both = jnp.concatenate(
        [jnp.where(left, packed, turned), jnp.where(left, turned, packed)], axis=0
    )
    slot = slot_columns(slot_ref)
    high = (lanes(512) >= RANK).astype(jnp.int32)
    raised = jnp.concatenate(
        [jnp.where(slot == 2 * j + high, both, 0.0).astype(BF16) for j in range(CHIPS)], axis=1
    )
    total = jnp.dot(raised, table_ref[...], preferred_element_type=F32)
    out_ref[...] = (SCALE * total).astype(BF16).reshape(16, 32, 512)


def raise_features(mine, other, table, slot, after=()):
    return call(
        raise_kernel,
        "raise_features",
        [whole((16, 32, 512), BF16)],
        (mine, other, table, slot),
        after=after,
    )


def finish_kernel(
    residual_ref, wide_ref, wide_y_ref, rest_y_ref, narrow_ref, delta_ref, out_ref
):
    for t in range(16):
        cols = slice(t * 512, (t + 1) * 512)
        if (t + 1) * 512 <= WIDE:
            if (t + 1) * 512 <= CUT:
                other = wide_y_ref[:, cols]
            else:
                other = rest_y_ref[:, t * 512 - CUT : (t + 1) * 512 - CUT]
            base = wide_ref[:, cols] + other.astype(F32)
        else:
            part = slice(t * 512 - WIDE, (t + 1) * 512 - WIDE)
            base = narrow_ref[:, part]
        out_ref[:, cols] = (
            residual_ref[:, cols].astype(F32) + base + delta_ref[t].astype(F32)
        ).astype(BF16)


def local(
    attention_output,
    output_projection_weight,
    residual,
    resident_down_maps,
    resident_up_maps,
    fresh_adapter_bundle,
    fresh_slot_targets,
    request_adapter_slot,
):
    x, w = attention_output, output_projection_weight
    slot = request_adapter_slot.reshape(1, 512)
    target = fresh_slot_targets

    maps = lax.all_to_all(
        fresh_adapter_bundle.reshape(16, 256, 128), "tp", split_axis=0, concat_axis=0, tiled=True
    )
    narrow = x.shape[0] * 16 - WIDE
    *narrow_away, narrow_own, mark = product(x, w, Y_MAJOR, WIDE, narrow, NARROW_CHUNK)
    narrow_in = [send(away, 0, 0, 1) for away in narrow_away]
    *wide_away, wide_own, mark = product(x, w, X_MAJOR, 0, WIDE, WIDE_CHUNK, [mark])
    wide_in = [send(away, 0, 0, 1) for away in wide_away]

    keep, away, mark = chip_sum(
        "chip_narrow", narrow_own, narrow_in, 2, None, [mark, maps]
    )
    narrow_y = send(away, 1, 0, 0)
    here, right, far_right, far_left, left, mark = chip_sum(
        "chip_wide", wide_own, wide_in, 4, 2, [away]
    )
    far_right, far_left = send(far_right, 0, 1, 0), send(far_left, 0, 3, 0)

    part, mark = shrink_part(x, resident_down_maps, slot, target, maps, [mark])
    part_in = send(part, 0, 0, 1)
    part, mark = add_parts([part, part_in], [mark])
    part_in = trade(part, lambda x: x ^ 1)
    part, mark = add_parts([part, part_in], [mark])
    part_in = trade(part, lambda x: 3 - x)
    part, mark = add_parts([part, part_in], [mark])
    other = send(part, 1, 0, 0)

    right, left, mark = near(right, left, far_right, far_left, [mark])
    from_left, from_right = send(right, 0, 1, 0), send(left, 0, 3, 0)
    table, mark = up_table(resident_up_maps, target, maps, [mark])
    *low, mark = turn_narrow(keep, narrow_y, [mark])
    low_in = [send(low[d], 0, d, 0) for d in (1, 2, 3)]
    raised, mark = raise_features(part, other, table, slot, [mark])
    delta = lax.all_to_all(raised, "tp", split_axis=0, concat_axis=0, tiled=True)

    wide_keep, wide_send, wide_rest, mark = turn_wide(here, from_left, from_right, [mark])
    wide_y = send(wide_send, 1, 0, 0)
    rest_y = send(wide_rest, 1, 0, 0)
    narrow_sum, mark = add_parts([low[0], *low_in], [mark], F32)
    hidden, _ = call(
        finish_kernel,
        "finish",
        [whole((32, 8192), BF16)],
        (residual, wide_keep, wide_y, rest_y, narrow_sum, delta),
    )
    return hidden


def solution(mesh):
    return jax.shard_map(
        local,
        mesh=mesh,
        in_specs=(
            P("grp", "tp"),
            P("tp", None),
            P("tp", "grp"),
            P("tp", "grp"),
            P("grp", "tp"),
            P(("grp", "tp"), None, None),
            P("grp"),
            P("grp"),
        ),
        out_specs=P("tp", "grp"),
        check_vma=False,
    )
```

```python
import jax
import jax.numpy as jnp
from jax import lax
from jax.experimental import pallas as pl
from jax.experimental.pallas import tpu as pltpu
from jax.sharding import PartitionSpec as P

RANK = 64
SLOTS = 16
CHIPS = 8
SCALE = 0.5
F32 = jnp.float32
BF16 = jnp.bfloat16
WIDE = 4608
CUT = 2560
VMEM_LIMIT = 16 * 1024 * 1024
PRODUCT_LIMIT = 56 * 1024 * 1024
CHIP_LIMIT = 48 * 1024 * 1024
NARROW_CHUNK = 1792
WIDE_CHUNK = 1536


def place(y, x, core):
    return ((y % 2) * 4 + x % 4) * 2 + core % 2


def route(yy, xx, cc):
    return [
        (place(y, x, c), place(y + yy, x + xx, c + cc))
        for y in range(2)
        for x in range(4)
        for c in range(2)
    ]


def send(array, yy, xx, cc):
    return lax.ppermute(array, "tp", route(yy, xx, cc))


def trade(array, partner_of):
    pairs = [
        (place(y, x, c), place(y, partner_of(x), c))
        for y in range(2)
        for x in range(4)
        for c in range(2)
    ]
    return lax.ppermute(array, "tp", pairs)


def spot():
    t = lax.axis_index("tp")
    return t // 8, lax.rem(t // 2, 4), lax.rem(t, 2)


def partner(yy, xx, cc):
    y, x, c = spot()
    return (lax.rem(y + yy, 2) * 4 + lax.rem(x + xx, 4)) * 2 + lax.rem(c + cc, 2)


def rows_at(index, size):
    return pl.ds(pl.multiple_of(index * size, size), size)


def whole(shape, dtype):
    return jax.ShapeDtypeStruct(shape, dtype)


def plus(a, *others):
    total = a.astype(F32)
    for other in others:
        total = total + other.astype(F32)
    return total


VM = pl.BlockSpec(memory_space=pltpu.VMEM)
SM = pl.BlockSpec(memory_space=pltpu.SMEM)
LATER = pl.BlockSpec(memory_space=pl.ANY)


def call(kernel, name, out_shape, args, specs=None, after=(), limit=VMEM_LIMIT, out_specs=None, scratch_shapes=()):
    count, outs = len(args), len(out_shape)

    def body(*refs):
        results = refs[count + len(after) :]
        results[outs][...] = jnp.zeros((8, 128), F32)
        kernel(*refs[:count], *results[:outs], *results[outs + 1 :])

    return pl.pallas_call(
        body,
        in_specs=list(specs or [VM] * count) + [LATER] * len(after),
        out_specs=list(out_specs or [VM] * outs) + [VM],
        out_shape=list(out_shape) + [whole((8, 128), F32)],
        scratch_shapes=list(scratch_shapes),
        compiler_params=pltpu.CompilerParams(vmem_limit_bytes=limit),
        cost_estimate=pl.CostEstimate(flops=1024, bytes_accessed=1024, transcendentals=0),
        name=name,
    )(*args, *after)


X_MAJOR = [(yy, xx) for xx in range(4) for yy in range(2)]
Y_MAJOR = [(yy, xx) for yy in range(2) for xx in range(4)]


HBM = pl.BlockSpec(memory_space=pltpu.HBM)


def product(x, w, order, first, width, chunk, after=()):
    chunks = width // chunk
    sub = chunk // 2
    subs = 2 * chunks

    def kernel(x_ref, w_ref, *refs):
        away_refs = refs[:chunks]
        own_ref, rows_ref, held_ref, done_ref, sems, away_sems, own_sems = refs[chunks:]

        def copy(i):
            cols = pl.ds(pl.multiple_of(first + i * sub, 128), sub)
            return pltpu.make_async_copy(w_ref.at[:, cols], held_ref.at[i], sems.at[i])

        def leave(i):
            return pltpu.make_async_copy(
                done_ref.at[i, :256],
                away_refs[i // 2].at[:, pl.ds(i % 2 * sub, sub)],
                away_sems.at[i],
            )

        def stay(i):
            return pltpu.make_async_copy(
                done_ref.at[i, 256:], own_ref.at[:, pl.ds(i * sub, sub)], own_sems.at[i]
            )

        for i in range(subs):
            copy(i).start()
        for i, (yy, xx) in enumerate(order):
            for cc, top in ((1, 0), (0, 256)):
                rows_ref[top + i * 32 : top + (i + 1) * 32, :] = x_ref[
                    rows_at(partner(yy, xx, cc), 32), :
                ]
        for i in range(subs):
            copy(i).wait()
            done_ref[i] = jnp.dot(
                rows_ref[...], held_ref[i], preferred_element_type=F32
            ).astype(BF16)
            leave(i).start()
            stay(i).start()
        for i in range(subs):
            leave(i).wait()
            stay(i).wait()

    return call(
        kernel,
        "product",
        [whole((256, chunk), BF16)] * chunks + [whole((256, width), BF16)],
        (x, w),
        [VM, HBM],
        after,
        limit=PRODUCT_LIMIT,
        out_specs=[HBM] * (chunks + 1),
        scratch_shapes=[
            pltpu.VMEM((512, 512), BF16),
            pltpu.VMEM((subs, 512, sub), BF16),
            pltpu.VMEM((subs, 512, sub), BF16),
            pltpu.SemaphoreType.DMA((subs,)),
            pltpu.SemaphoreType.DMA((subs,)),
            pltpu.SemaphoreType.DMA((subs,)),
        ],
    )


def chip_sum(name, own, away, blocks, split, after=()):
    chunk = away[0].shape[1]
    sub = chunk // 2
    subs = 2 * len(away)
    width = own.shape[1]
    half = width // 2
    step = 128
    size = own.shape[0] // blocks
    shapes = []
    for d in range(blocks):
        shapes += [(size, half)] * 2 if d == split else [(size, width)]

    def kernel(own_ref, *refs):
        away_refs, outs = refs[: len(away)], refs[len(away) : len(away) + len(shapes)]
        held_ref, came_ref, own_sems, away_sems = refs[len(away) + len(shapes) :]

        def load_own(i):
            return pltpu.make_async_copy(
                own_ref.at[:, pl.ds(i * sub, sub)], held_ref.at[i], own_sems.at[i]
            )

        def load_away(i):
            return pltpu.make_async_copy(
                away_refs[i // 2].at[:, pl.ds(i % 2 * sub, sub)], came_ref.at[i], away_sems.at[i]
            )

        for i in range(subs):
            load_own(i).start()
            load_away(i).start()
        for i in range(subs):
            load_own(i).wait()
            load_away(i).wait()
            for part in range(0, sub, step):
                first = i * sub + part
                total = plus(
                    held_ref[i, :, part : part + step], came_ref[i, :, part : part + step]
                ).astype(BF16)
                place_at = 0
                for d in range(blocks):
                    piece = total[d * size : (d + 1) * size]
                    if d == split:
                        side, at = divmod(first, half)
                        outs[place_at + side][:, at : at + step] = piece
                        place_at += 2
                    else:
                        outs[place_at][:, first : first + step] = piece
                        place_at += 1

    return call(
        kernel,
        name,
        [whole(shape, BF16) for shape in shapes],
        (own, *away),
        [HBM] * (1 + len(away)),
        after,
        limit=CHIP_LIMIT,
        scratch_shapes=[
            pltpu.VMEM((subs, own.shape[0], sub), BF16),
            pltpu.VMEM((subs, own.shape[0], sub), BF16),
            pltpu.SemaphoreType.DMA((subs,)),
            pltpu.SemaphoreType.DMA((subs,)),
        ],
    )


def turn_narrow(keep, landed, after=()):
    width = keep.shape[1]

    def kernel(keep_ref, landed_ref, *refs):
        total = plus(keep_ref[...], landed_ref[...]).astype(BF16)
        for d, ref in enumerate(refs):
            ref[...] = total[d * 32 : (d + 1) * 32]

    return call(
        kernel, "turn_narrow", [whole((32, width), BF16)] * 4, (keep, landed), after=after
    )


def near(right, left, far_right, far_left, after=()):
    half = right.shape[1] // 2

    def kernel(right_ref, left_ref, far_right_ref, far_left_ref, to_right_ref, to_left_ref):
        to_right_ref[:, :half] = plus(right_ref[:, :half], far_right_ref[...]).astype(BF16)
        to_right_ref[:, half:] = right_ref[:, half:]
        to_left_ref[:, :half] = left_ref[:, :half]
        to_left_ref[:, half:] = plus(left_ref[:, half:], far_left_ref[...]).astype(BF16)

    return call(
        kernel, "near", [whole(right.shape, BF16)] * 2, (right, left, far_right, far_left), after=after
    )


def turn_wide(here, from_left, from_right, after=()):
    width = here.shape[1]

    def kernel(here_ref, from_left_ref, from_right_ref, keep_ref, send_ref, rest_ref):
        total = plus(here_ref[...], from_left_ref[...], from_right_ref[...])
        keep_ref[...] = total[:32]
        send_ref[...] = total[32:, :CUT].astype(BF16)
        rest_ref[...] = total[32:, CUT:].astype(BF16)

    return call(
        kernel,
        "turn_wide",
        [whole((32, width), F32), whole((32, CUT), BF16), whole((32, width - CUT), BF16)],
        (here, from_left, from_right),
        after=after,
    )


def add_parts(parts, after=(), dtype=BF16):
    def kernel(*refs):
        refs[-1][...] = plus(*[ref[...] for ref in refs[:-1]]).astype(dtype)

    return call(kernel, "add_parts", [whole(parts[0].shape, dtype)], parts, after=after)


def lanes(rows):
    return lax.broadcasted_iota(jnp.int32, (rows, 128), 1)


def slot_columns(slot_ref):
    row = slot_ref[...].astype(F32)
    return jnp.broadcast_to(row, (128, 512)).T.astype(jnp.int32)


def resident_slot(slot, target_ref):
    for k in range(CHIPS):
        slot = jnp.where(slot == target_ref[k], -1, slot)
    return slot


def shrink_kernel(x_ref, down_ref, slot_ref, target_ref, maps_ref, out_ref):
    x = x_ref[...]
    row = lax.broadcasted_iota(jnp.int32, (512, 512), 0)
    col = lax.broadcasted_iota(jnp.int32, (512, 512), 1)
    source = jnp.where(col < 256, 2 * col, 2 * (col - 256) + 1)
    chooser = jnp.where(row == source, 1.0, 0.0).astype(BF16)
    split = jnp.dot(x, chooser, preferred_element_type=F32).astype(BF16)
    even, odd = split[:, :256], split[:, 256:]
    slot = slot_columns(slot_ref)
    kept = resident_slot(slot, target_ref)
    high = (lanes(512) >= RANK).astype(jnp.int32)
    acc = jnp.zeros((512, 128), F32)
    for k in range(0, CHIPS, 2):
        resident = jnp.dot(
            x, down_ref[:, k * 128 : (k + 2) * 128], preferred_element_type=F32
        )
        maps = jnp.concatenate([maps_ref[2 * k], maps_ref[2 * k + 2]], axis=1)
        of_even = jnp.dot(even, maps, preferred_element_type=F32)
        of_odd = jnp.dot(odd, maps, preferred_element_type=F32)
        for i in range(2):
            cols = slice(i * 128, (i + 1) * 128)
            acc += jnp.where(kept == 2 * (k + i) + high, resident[:, cols], 0.0)
            part = jnp.where(high == 0, of_even[:, cols], of_odd[:, cols])
            acc += jnp.where(slot == target_ref[k + i], part, 0.0)
    acc = acc + pltpu.roll(acc, RANK, 1)
    out_ref[...] = jnp.where(lanes(256) < RANK, acc[:256], acc[256:]).astype(BF16)


def shrink_part(x, down, slot, target, maps, after=()):
    return call(
        shrink_kernel,
        "shrink_part",
        [whole((256, 128), BF16)],
        (x, down, slot, target, maps),
        [VM, VM, VM, SM, VM],
        after,
    )


def up_table_kernel(up_ref, target_ref, maps_ref, table_ref):
    table_ref[...] = up_ref[...]
    row = lax.broadcasted_iota(jnp.int32, (256, 512), 0)
    col = lax.broadcasted_iota(jnp.int32, (256, 512), 1)
    to_even = jnp.where(col == 2 * row, 1.0, 0.0).astype(BF16)
    to_odd = jnp.where(col == 2 * row + 1, 1.0, 0.0).astype(BF16)
    turn = (((0,), (0,)), ((), ()))
    for k in range(CHIPS):
        maps = maps_ref[2 * k + 1]
        even = lax.dot_general(maps, to_even, turn, preferred_element_type=F32)
        odd = lax.dot_general(maps, to_odd, turn, preferred_element_type=F32)
        table_ref[rows_at(target_ref[k], RANK), :] = (even[:RANK] + odd[RANK:]).astype(BF16)


def up_table(up, target, maps, after=()):
    return call(
        up_table_kernel, "up_table", [whole((1024, 512), BF16)], (up, target, maps), [VM, SM, VM], after
    )


def raise_kernel(mine_ref, other_ref, table_ref, slot_ref, out_ref):
    packed = (mine_ref[...].astype(F32) + other_ref[...].astype(F32)).astype(BF16).astype(F32)
    turned = pltpu.roll(packed, RANK, 1)
    left = lanes(256) < RANK
    both = jnp.concatenate(
        [jnp.where(left, packed, turned), jnp.where(left, turned, packed)], axis=0
    )
    slot = slot_columns(slot_ref)
    high = (lanes(512) >= RANK).astype(jnp.int32)
    raised = jnp.concatenate(
        [jnp.where(slot == 2 * j + high, both, 0.0).astype(BF16) for j in range(CHIPS)], axis=1
    )
    total = jnp.dot(raised, table_ref[...], preferred_element_type=F32)
    out_ref[...] = (SCALE * total).astype(BF16).reshape(16, 32, 512)


def raise_features(mine, other, table, slot, after=()):
    return call(
        raise_kernel,
        "raise_features",
        [whole((16, 32, 512), BF16)],
        (mine, other, table, slot),
        after=after,
    )


def finish_kernel(
    residual_ref, wide_ref, wide_y_ref, rest_y_ref, narrow_ref, delta_ref, out_ref
):
    for t in range(16):
        cols = slice(t * 512, (t + 1) * 512)
        if (t + 1) * 512 <= WIDE:
            if (t + 1) * 512 <= CUT:
                other = wide_y_ref[:, cols]
            else:
                other = rest_y_ref[:, t * 512 - CUT : (t + 1) * 512 - CUT]
            base = wide_ref[:, cols] + other.astype(F32)
        else:
            part = slice(t * 512 - WIDE, (t + 1) * 512 - WIDE)
            base = narrow_ref[:, part]
        out_ref[:, cols] = (
            residual_ref[:, cols].astype(F32) + base + delta_ref[t].astype(F32)
        ).astype(BF16)


def local(
    attention_output,
    output_projection_weight,
    residual,
    resident_down_maps,
    resident_up_maps,
    fresh_adapter_bundle,
    fresh_slot_targets,
    request_adapter_slot,
):
    x, w = attention_output, output_projection_weight
    slot = request_adapter_slot.reshape(1, 512)
    target = fresh_slot_targets

    maps = lax.all_to_all(
        fresh_adapter_bundle.reshape(16, 256, 128), "tp", split_axis=0, concat_axis=0, tiled=True
    )
    narrow = x.shape[0] * 16 - WIDE
    *narrow_away, narrow_own, mark = product(x, w, Y_MAJOR, WIDE, narrow, NARROW_CHUNK)
    narrow_in = [send(away, 0, 0, 1) for away in narrow_away]
    *wide_away, wide_own, mark = product(x, w, X_MAJOR, 0, WIDE, WIDE_CHUNK, [mark])
    wide_in = [send(away, 0, 0, 1) for away in wide_away]

    keep, away, mark = chip_sum(
        "chip_narrow", narrow_own, narrow_in, 2, None, [maps]
    )
    narrow_y = send(away, 1, 0, 0)
    here, right, far_right, far_left, left, mark = chip_sum(
        "chip_wide", wide_own, wide_in, 4, 2, [away]
    )
    far_right, far_left = send(far_right, 0, 1, 0), send(far_left, 0, 3, 0)

    part, mark = shrink_part(x, resident_down_maps, slot, target, maps, [mark])
    part_in = send(part, 0, 0, 1)
    part, mark = add_parts([part, part_in], [mark])
    part_in = trade(part, lambda x: x ^ 1)
    part, mark = add_parts([part, part_in], [mark])
    part_in = trade(part, lambda x: 3 - x)
    part, mark = add_parts([part, part_in], [mark])
    other = send(part, 1, 0, 0)

    right, left, mark = near(right, left, far_right, far_left, [mark])
    from_left, from_right = send(right, 0, 1, 0), send(left, 0, 3, 0)
    table, mark = up_table(resident_up_maps, target, maps, [mark])
    *low, mark = turn_narrow(keep, narrow_y, [mark])
    low_in = [send(low[d], 0, d, 0) for d in (1, 2, 3)]
    raised, mark = raise_features(part, other, table, slot, [mark])
    delta = lax.all_to_all(raised, "tp", split_axis=0, concat_axis=0, tiled=True)

    wide_keep, wide_send, wide_rest, mark = turn_wide(here, from_left, from_right, [mark])
    wide_y = send(wide_send, 1, 0, 0)
    rest_y = send(wide_rest, 1, 0, 0)
    narrow_sum, mark = add_parts([low[0], *low_in], [mark], F32)
    hidden, _ = call(
        finish_kernel,
        "finish",
        [whole((32, 8192), BF16)],
        (residual, wide_keep, wide_y, rest_y, narrow_sum, delta),
    )
    return hidden


def solution(mesh):
    return jax.shard_map(
        local,
        mesh=mesh,
        in_specs=(
            P("grp", "tp"),
            P("tp", None),
            P("tp", "grp"),
            P("tp", "grp"),
            P("grp", "tp"),
            P(("grp", "tp"), None, None),
            P("grp"),
            P("grp"),
        ),
        out_specs=P("tp", "grp"),
        check_vma=False,
    )
```

```python
import jax
import jax.numpy as jnp
from jax import lax
from jax.experimental import pallas as pl
from jax.experimental.pallas import tpu as pltpu
from jax.sharding import PartitionSpec as P

RANK = 64
SLOTS = 16
CHIPS = 8
SCALE = 0.5
F32 = jnp.float32
BF16 = jnp.bfloat16
WIDE = 4608
CUT = 2560
VMEM_LIMIT = 16 * 1024 * 1024
PRODUCT_LIMIT = 56 * 1024 * 1024
CHIP_LIMIT = 48 * 1024 * 1024
NARROW_CHUNK = 1792
WIDE_CHUNK = 1536


def place(y, x, core):
    return ((y % 2) * 4 + x % 4) * 2 + core % 2


def route(yy, xx, cc):
    return [
        (place(y, x, c), place(y + yy, x + xx, c + cc))
        for y in range(2)
        for x in range(4)
        for c in range(2)
    ]


def send(array, yy, xx, cc):
    return lax.ppermute(array, "tp", route(yy, xx, cc))


def trade(array, partner_of):
    pairs = [
        (place(y, x, c), place(y, partner_of(x), c))
        for y in range(2)
        for x in range(4)
        for c in range(2)
    ]
    return lax.ppermute(array, "tp", pairs)


def spot():
    t = lax.axis_index("tp")
    return t // 8, lax.rem(t // 2, 4), lax.rem(t, 2)


def partner(yy, xx, cc):
    y, x, c = spot()
    return (lax.rem(y + yy, 2) * 4 + lax.rem(x + xx, 4)) * 2 + lax.rem(c + cc, 2)


def rows_at(index, size):
    return pl.ds(pl.multiple_of(index * size, size), size)


def whole(shape, dtype):
    return jax.ShapeDtypeStruct(shape, dtype)


def plus(a, *others):
    total = a.astype(F32)
    for other in others:
        total = total + other.astype(F32)
    return total


VM = pl.BlockSpec(memory_space=pltpu.VMEM)
SM = pl.BlockSpec(memory_space=pltpu.SMEM)
LATER = pl.BlockSpec(memory_space=pl.ANY)


def call(kernel, name, out_shape, args, specs=None, after=(), limit=VMEM_LIMIT, out_specs=None, scratch_shapes=()):
    count, outs = len(args), len(out_shape)

    def body(*refs):
        results = refs[count + len(after) :]
        results[outs][...] = jnp.zeros((8, 128), F32)
        kernel(*refs[:count], *results[:outs], *results[outs + 1 :])

    return pl.pallas_call(
        body,
        in_specs=list(specs or [VM] * count) + [LATER] * len(after),
        out_specs=list(out_specs or [VM] * outs) + [VM],
        out_shape=list(out_shape) + [whole((8, 128), F32)],
        scratch_shapes=list(scratch_shapes),
        compiler_params=pltpu.CompilerParams(vmem_limit_bytes=limit),
        cost_estimate=pl.CostEstimate(flops=1024, bytes_accessed=1024, transcendentals=0),
        name=name,
    )(*args, *after)


X_MAJOR = [(yy, xx) for xx in range(4) for yy in range(2)]
Y_MAJOR = [(yy, xx) for yy in range(2) for xx in range(4)]


HBM = pl.BlockSpec(memory_space=pltpu.HBM)


def product(x, w, order, first, width, chunk, after=()):
    chunks = width // chunk
    sub = chunk // 2
    subs = 2 * chunks

    def kernel(x_ref, w_ref, *refs):
        away_refs = refs[:chunks]
        own_ref, rows_ref, held_ref, done_ref, sems, away_sems, own_sems = refs[chunks:]

        def copy(i):
            cols = pl.ds(pl.multiple_of(first + i * sub, 128), sub)
            return pltpu.make_async_copy(w_ref.at[:, cols], held_ref.at[i], sems.at[i])

        def leave(i):
            return pltpu.make_async_copy(
                done_ref.at[i, :256],
                away_refs[i // 2].at[:, pl.ds(i % 2 * sub, sub)],
                away_sems.at[i],
            )

        def stay(i):
            return pltpu.make_async_copy(
                done_ref.at[i, 256:], own_ref.at[:, pl.ds(i * sub, sub)], own_sems.at[i]
            )

        for i in range(subs):
            copy(i).start()
        for i, (yy, xx) in enumerate(order):
            for cc, top in ((1, 0), (0, 256)):
                rows_ref[top + i * 32 : top + (i + 1) * 32, :] = x_ref[
                    rows_at(partner(yy, xx, cc), 32), :
                ]
        for i in range(subs):
            copy(i).wait()
            done_ref[i] = jnp.dot(
                rows_ref[...], held_ref[i], preferred_element_type=F32
            ).astype(BF16)
            leave(i).start()
            stay(i).start()
        for i in range(subs):
            leave(i).wait()
            stay(i).wait()

    return call(
        kernel,
        "product",
        [whole((256, chunk), BF16)] * chunks + [whole((256, width), BF16)],
        (x, w),
        [VM, HBM],
        after,
        limit=PRODUCT_LIMIT,
        out_specs=[HBM] * (chunks + 1),
        scratch_shapes=[
            pltpu.VMEM((512, 512), BF16),
            pltpu.VMEM((subs, 512, sub), BF16),
            pltpu.VMEM((subs, 512, sub), BF16),
            pltpu.SemaphoreType.DMA((subs,)),
            pltpu.SemaphoreType.DMA((subs,)),
            pltpu.SemaphoreType.DMA((subs,)),
        ],
    )


def chip_sum(name, own, away, blocks, split, after=()):
    chunk = away[0].shape[1]
    sub = chunk // 2
    subs = 2 * len(away)
    width = own.shape[1]
    half = width // 2
    step = 128
    size = own.shape[0] // blocks
    shapes = []
    for d in range(blocks):
        shapes += [(size, half)] * 2 if d == split else [(size, width)]

    def kernel(own_ref, *refs):
        away_refs, outs = refs[: len(away)], refs[len(away) : len(away) + len(shapes)]
        held_ref, came_ref, own_sems, away_sems = refs[len(away) + len(shapes) :]

        def load_own(i):
            return pltpu.make_async_copy(
                own_ref.at[:, pl.ds(i * sub, sub)], held_ref.at[i], own_sems.at[i]
            )

        def load_away(i):
            return pltpu.make_async_copy(
                away_refs[i // 2].at[:, pl.ds(i % 2 * sub, sub)], came_ref.at[i], away_sems.at[i]
            )

        for i in range(subs):
            load_own(i).start()
            load_away(i).start()
        for i in range(subs):
            load_own(i).wait()
            load_away(i).wait()
            for part in range(0, sub, step):
                first = i * sub + part
                total = plus(
                    held_ref[i, :, part : part + step], came_ref[i, :, part : part + step]
                ).astype(BF16)
                place_at = 0
                for d in range(blocks):
                    piece = total[d * size : (d + 1) * size]
                    if d == split:
                        side, at = divmod(first, half)
                        outs[place_at + side][:, at : at + step] = piece
                        place_at += 2
                    else:
                        outs[place_at][:, first : first + step] = piece
                        place_at += 1

    return call(
        kernel,
        name,
        [whole(shape, BF16) for shape in shapes],
        (own, *away),
        [HBM] * (1 + len(away)),
        after,
        limit=CHIP_LIMIT,
        scratch_shapes=[
            pltpu.VMEM((subs, own.shape[0], sub), BF16),
            pltpu.VMEM((subs, own.shape[0], sub), BF16),
            pltpu.SemaphoreType.DMA((subs,)),
            pltpu.SemaphoreType.DMA((subs,)),
        ],
    )


def turn_narrow(keep, landed, after=()):
    width = keep.shape[1]

    def kernel(keep_ref, landed_ref, *refs):
        total = plus(keep_ref[...], landed_ref[...]).astype(BF16)
        for d, ref in enumerate(refs):
            ref[...] = total[d * 32 : (d + 1) * 32]

    return call(
        kernel, "turn_narrow", [whole((32, width), BF16)] * 4, (keep, landed), after=after
    )


def near_rest(right, left, after=()):
    half = right.shape[1] // 2

    def kernel(right_ref, left_ref, to_right_ref, to_left_ref):
        to_right_ref[...] = right_ref[:, half:]
        to_left_ref[...] = left_ref[:, :half]

    return call(
        kernel, "near_rest", [whole((64, half), BF16)] * 2, (right, left), after=after
    )


def near(right, left, far_right, far_left, after=()):
    half = right.shape[1] // 2

    def kernel(right_ref, left_ref, far_right_ref, far_left_ref, to_right_ref, to_left_ref):
        to_right_ref[...] = plus(right_ref[:, :half], far_right_ref[...]).astype(BF16)
        to_left_ref[...] = plus(left_ref[:, half:], far_left_ref[...]).astype(BF16)

    return call(
        kernel,
        "near",
        [whole((64, half), BF16)] * 2,
        (right, left, far_right, far_left),
        after=after,
    )


def turn_wide(here, from_left, from_right, after=()):
    width = here.shape[1]
    half = width // 2

    def kernel(here_ref, *refs):
        left_near, left_rest, right_near, right_rest, keep_ref, send_ref, rest_ref = refs
        low = plus(here_ref[:, :half], left_near[...], right_rest[...])
        high = plus(here_ref[:, half:], left_rest[...], right_near[...])
        keep_ref[:, :half] = low[:32]
        keep_ref[:, half:] = high[:32]
        send_ref[:, :half] = low[32:].astype(BF16)
        send_ref[:, half:] = high[32:, : CUT - half].astype(BF16)
        rest_ref[...] = high[32:, CUT - half :].astype(BF16)

    return call(
        kernel,
        "turn_wide",
        [whole((32, width), F32), whole((32, CUT), BF16), whole((32, width - CUT), BF16)],
        (here, *from_left, *from_right),
        after=after,
    )


def add_parts(parts, after=(), dtype=BF16):
    def kernel(*refs):
        refs[-1][...] = plus(*[ref[...] for ref in refs[:-1]]).astype(dtype)

    return call(kernel, "add_parts", [whole(parts[0].shape, dtype)], parts, after=after)


def lanes(rows):
    return lax.broadcasted_iota(jnp.int32, (rows, 128), 1)


def slot_columns(slot_ref):
    row = slot_ref[...].astype(F32)
    return jnp.broadcast_to(row, (128, 512)).T.astype(jnp.int32)


def resident_slot(slot, target_ref):
    for k in range(CHIPS):
        slot = jnp.where(slot == target_ref[k], -1, slot)
    return slot


def shrink_kernel(x_ref, down_ref, slot_ref, target_ref, maps_ref, out_ref):
    x = x_ref[...]
    row = lax.broadcasted_iota(jnp.int32, (512, 512), 0)
    col = lax.broadcasted_iota(jnp.int32, (512, 512), 1)
    source = jnp.where(col < 256, 2 * col, 2 * (col - 256) + 1)
    chooser = jnp.where(row == source, 1.0, 0.0).astype(BF16)
    split = jnp.dot(x, chooser, preferred_element_type=F32).astype(BF16)
    even, odd = split[:, :256], split[:, 256:]
    slot = slot_columns(slot_ref)
    kept = resident_slot(slot, target_ref)
    high = (lanes(512) >= RANK).astype(jnp.int32)
    acc = jnp.zeros((512, 128), F32)
    for k in range(0, CHIPS, 2):
        resident = jnp.dot(
            x, down_ref[:, k * 128 : (k + 2) * 128], preferred_element_type=F32
        )
        maps = jnp.concatenate([maps_ref[2 * k], maps_ref[2 * k + 2]], axis=1)
        of_even = jnp.dot(even, maps, preferred_element_type=F32)
        of_odd = jnp.dot(odd, maps, preferred_element_type=F32)
        for i in range(2):
            cols = slice(i * 128, (i + 1) * 128)
            acc += jnp.where(kept == 2 * (k + i) + high, resident[:, cols], 0.0)
            part = jnp.where(high == 0, of_even[:, cols], of_odd[:, cols])
            acc += jnp.where(slot == target_ref[k + i], part, 0.0)
    acc = acc + pltpu.roll(acc, RANK, 1)
    out_ref[...] = jnp.where(lanes(256) < RANK, acc[:256], acc[256:]).astype(BF16)


def shrink_part(x, down, slot, target, maps, after=()):
    return call(
        shrink_kernel,
        "shrink_part",
        [whole((256, 128), BF16)],
        (x, down, slot, target, maps),
        [VM, VM, VM, SM, VM],
        after,
    )


def up_table_kernel(up_ref, target_ref, maps_ref, table_ref):
    table_ref[...] = up_ref[...]
    row = lax.broadcasted_iota(jnp.int32, (256, 512), 0)
    col = lax.broadcasted_iota(jnp.int32, (256, 512), 1)
    to_even = jnp.where(col == 2 * row, 1.0, 0.0).astype(BF16)
    to_odd = jnp.where(col == 2 * row + 1, 1.0, 0.0).astype(BF16)
    turn = (((0,), (0,)), ((), ()))
    for k in range(CHIPS):
        maps = maps_ref[2 * k + 1]
        even = lax.dot_general(maps, to_even, turn, preferred_element_type=F32)
        odd = lax.dot_general(maps, to_odd, turn, preferred_element_type=F32)
        table_ref[rows_at(target_ref[k], RANK), :] = (even[:RANK] + odd[RANK:]).astype(BF16)


def up_table(up, target, maps, after=()):
    return call(
        up_table_kernel, "up_table", [whole((1024, 512), BF16)], (up, target, maps), [VM, SM, VM], after
    )


def raise_kernel(mine_ref, other_ref, table_ref, slot_ref, out_ref):
    packed = (mine_ref[...].astype(F32) + other_ref[...].astype(F32)).astype(BF16).astype(F32)
    turned = pltpu.roll(packed, RANK, 1)
    left = lanes(256) < RANK
    both = jnp.concatenate(
        [jnp.where(left, packed, turned), jnp.where(left, turned, packed)], axis=0
    )
    slot = slot_columns(slot_ref)
    high = (lanes(512) >= RANK).astype(jnp.int32)
    raised = jnp.concatenate(
        [jnp.where(slot == 2 * j + high, both, 0.0).astype(BF16) for j in range(CHIPS)], axis=1
    )
    total = jnp.dot(raised, table_ref[...], preferred_element_type=F32)
    out_ref[...] = (SCALE * total).astype(BF16).reshape(16, 32, 512)


def raise_features(mine, other, table, slot, after=()):
    return call(
        raise_kernel,
        "raise_features",
        [whole((16, 32, 512), BF16)],
        (mine, other, table, slot),
        after=after,
    )


def finish_kernel(
    residual_ref, wide_ref, wide_y_ref, rest_y_ref, narrow_ref, delta_ref, out_ref
):
    for t in range(16):
        cols = slice(t * 512, (t + 1) * 512)
        if (t + 1) * 512 <= WIDE:
            if (t + 1) * 512 <= CUT:
                other = wide_y_ref[:, cols]
            else:
                other = rest_y_ref[:, t * 512 - CUT : (t + 1) * 512 - CUT]
            base = wide_ref[:, cols] + other.astype(F32)
        else:
            part = slice(t * 512 - WIDE, (t + 1) * 512 - WIDE)
            base = narrow_ref[:, part]
        out_ref[:, cols] = (
            residual_ref[:, cols].astype(F32) + base + delta_ref[t].astype(F32)
        ).astype(BF16)


def local(
    attention_output,
    output_projection_weight,
    residual,
    resident_down_maps,
    resident_up_maps,
    fresh_adapter_bundle,
    fresh_slot_targets,
    request_adapter_slot,
):
    x, w = attention_output, output_projection_weight
    slot = request_adapter_slot.reshape(1, 512)
    target = fresh_slot_targets

    maps = lax.all_to_all(
        fresh_adapter_bundle.reshape(16, 256, 128), "tp", split_axis=0, concat_axis=0, tiled=True
    )
    narrow = x.shape[0] * 16 - WIDE
    *narrow_away, narrow_own, mark = product(x, w, Y_MAJOR, WIDE, narrow, NARROW_CHUNK)
    narrow_in = [send(away, 0, 0, 1) for away in narrow_away]
    *wide_away, wide_own, mark = product(x, w, X_MAJOR, 0, WIDE, WIDE_CHUNK, [mark])
    wide_in = [send(away, 0, 0, 1) for away in wide_away]

    keep, away, mark = chip_sum(
        "chip_narrow", narrow_own, narrow_in, 2, None, [maps]
    )
    narrow_y = send(away, 1, 0, 0)
    here, right, far_right, far_left, left, mark = chip_sum(
        "chip_wide", wide_own, wide_in, 4, 2, [away]
    )
    far_right, far_left = send(far_right, 0, 1, 0), send(far_left, 0, 3, 0)

    part, mark = shrink_part(x, resident_down_maps, slot, target, maps, [mark])
    part_in = send(part, 0, 0, 1)
    part, mark = add_parts([part, part_in], [mark])
    part_in = trade(part, lambda x: x ^ 1)
    near_right, near_left, mark = near(right, left, far_right, far_left, [mark])
    part, mark = add_parts([part, part_in], [mark])
    part_in = trade(part, lambda x: 3 - x)
    rest_right, rest_left, mark = near_rest(right, left, [mark])
    rest_right, rest_left = send(rest_right, 0, 1, 0), send(rest_left, 0, 3, 0)
    part, mark = add_parts([part, part_in], [mark])
    other = send(part, 1, 0, 0)

    near_right, near_left = send(near_right, 0, 1, 0), send(near_left, 0, 3, 0)
    table, mark = up_table(resident_up_maps, target, maps, [mark])
    *low, mark = turn_narrow(keep, narrow_y, [mark])
    low_in = [send(low[d], 0, d, 0) for d in (1, 2, 3)]
    wide_keep, wide_send, wide_rest, mark = turn_wide(
        here, (near_right, rest_right), (near_left, rest_left), [mark]
    )
    raised, mark = raise_features(part, other, table, slot, [mark])
    delta = lax.all_to_all(raised, "tp", split_axis=0, concat_axis=0, tiled=True)
    wide_y = send(wide_send, 1, 0, 0)
    rest_y = send(wide_rest, 1, 0, 0)
    narrow_sum, mark = add_parts([low[0], *low_in], [mark], F32)
    hidden, _ = call(
        finish_kernel,
        "finish",
        [whole((32, 8192), BF16)],
        (residual, wide_keep, wide_y, rest_y, narrow_sum, delta),
    )
    return hidden


def solution(mesh):
    return jax.shard_map(
        local,
        mesh=mesh,
        in_specs=(
            P("grp", "tp"),
            P("tp", None),
            P("tp", "grp"),
            P("tp", "grp"),
            P("grp", "tp"),
            P(("grp", "tp"), None, None),
            P("grp"),
            P("grp"),
        ),
        out_specs=P("tp", "grp"),
        check_vma=False,
    )
```

```python
import jax
import jax.numpy as jnp
from jax import lax
from jax.experimental import pallas as pl
from jax.experimental.pallas import tpu as pltpu
from jax.sharding import PartitionSpec as P

RANK = 64
SLOTS = 16
CHIPS = 8
SCALE = 0.5
F32 = jnp.float32
BF16 = jnp.bfloat16
WIDE = 4608
CUT = 2560
VMEM_LIMIT = 16 * 1024 * 1024
PRODUCT_LIMIT = 56 * 1024 * 1024
CHIP_LIMIT = 48 * 1024 * 1024
NARROW_CHUNK = 1792
WIDE_CHUNK = 1536


def place(y, x, core):
    return ((y % 2) * 4 + x % 4) * 2 + core % 2


def route(yy, xx, cc):
    return [
        (place(y, x, c), place(y + yy, x + xx, c + cc))
        for y in range(2)
        for x in range(4)
        for c in range(2)
    ]


def send(array, yy, xx, cc):
    return lax.ppermute(array, "tp", route(yy, xx, cc))


def trade(array, partner_of):
    pairs = [
        (place(y, x, c), place(y, partner_of(x), c))
        for y in range(2)
        for x in range(4)
        for c in range(2)
    ]
    return lax.ppermute(array, "tp", pairs)


def spot():
    t = lax.axis_index("tp")
    return t // 8, lax.rem(t // 2, 4), lax.rem(t, 2)


def partner(yy, xx, cc):
    y, x, c = spot()
    return (lax.rem(y + yy, 2) * 4 + lax.rem(x + xx, 4)) * 2 + lax.rem(c + cc, 2)


def rows_at(index, size):
    return pl.ds(pl.multiple_of(index * size, size), size)


def whole(shape, dtype):
    return jax.ShapeDtypeStruct(shape, dtype)


def plus(a, *others):
    total = a.astype(F32)
    for other in others:
        total = total + other.astype(F32)
    return total


VM = pl.BlockSpec(memory_space=pltpu.VMEM)
SM = pl.BlockSpec(memory_space=pltpu.SMEM)
LATER = pl.BlockSpec(memory_space=pl.ANY)


def call(kernel, name, out_shape, args, specs=None, after=(), limit=VMEM_LIMIT, out_specs=None, scratch_shapes=()):
    count, outs = len(args), len(out_shape)

    def body(*refs):
        results = refs[count + len(after) :]
        results[outs][...] = jnp.zeros((8, 128), F32)
        kernel(*refs[:count], *results[:outs], *results[outs + 1 :])

    return pl.pallas_call(
        body,
        in_specs=list(specs or [VM] * count) + [LATER] * len(after),
        out_specs=list(out_specs or [VM] * outs) + [VM],
        out_shape=list(out_shape) + [whole((8, 128), F32)],
        scratch_shapes=list(scratch_shapes),
        compiler_params=pltpu.CompilerParams(vmem_limit_bytes=limit),
        cost_estimate=pl.CostEstimate(flops=1024, bytes_accessed=1024, transcendentals=0),
        name=name,
    )(*args, *after)


X_MAJOR = [(yy, xx) for xx in range(4) for yy in range(2)]
Y_MAJOR = [(yy, xx) for yy in range(2) for xx in range(4)]


HBM = pl.BlockSpec(memory_space=pltpu.HBM)


def product(x, w, order, first, width, chunk, after=()):
    chunks = width // chunk
    sub = chunk // 2
    subs = 2 * chunks

    def kernel(x_ref, w_ref, *refs):
        away_refs = refs[:chunks]
        own_ref, rows_ref, held_ref, done_ref, sems, away_sems, own_sems = refs[chunks:]

        def copy(i):
            cols = pl.ds(pl.multiple_of(first + i * sub, 128), sub)
            return pltpu.make_async_copy(w_ref.at[:, cols], held_ref.at[i], sems.at[i])

        def leave(i):
            return pltpu.make_async_copy(
                done_ref.at[i, :256],
                away_refs[i // 2].at[:, pl.ds(i % 2 * sub, sub)],
                away_sems.at[i],
            )

        def stay(i):
            return pltpu.make_async_copy(
                done_ref.at[i, 256:], own_ref.at[:, pl.ds(i * sub, sub)], own_sems.at[i]
            )

        for i in range(subs):
            copy(i).start()
        for i, (yy, xx) in enumerate(order):
            for cc, top in ((1, 0), (0, 256)):
                rows_ref[top + i * 32 : top + (i + 1) * 32, :] = x_ref[
                    rows_at(partner(yy, xx, cc), 32), :
                ]
        for i in range(subs):
            copy(i).wait()
            done_ref[i] = jnp.dot(
                rows_ref[...], held_ref[i], preferred_element_type=F32
            ).astype(BF16)
            leave(i).start()
            stay(i).start()
        for i in range(subs):
            leave(i).wait()
            stay(i).wait()

    return call(
        kernel,
        "product",
        [whole((256, chunk), BF16)] * chunks + [whole((256, width), BF16)],
        (x, w),
        [VM, HBM],
        after,
        limit=PRODUCT_LIMIT,
        out_specs=[HBM] * (chunks + 1),
        scratch_shapes=[
            pltpu.VMEM((512, 512), BF16),
            pltpu.VMEM((subs, 512, sub), BF16),
            pltpu.VMEM((subs, 512, sub), BF16),
            pltpu.SemaphoreType.DMA((subs,)),
            pltpu.SemaphoreType.DMA((subs,)),
            pltpu.SemaphoreType.DMA((subs,)),
        ],
    )


def chip_sum(name, own, away, blocks, split, after=()):
    chunk = away[0].shape[1]
    sub = chunk // 2
    subs = 2 * len(away)
    width = own.shape[1]
    half = width // 2
    step = 128
    size = own.shape[0] // blocks
    shapes = []
    for d in range(blocks):
        shapes += [(size, half)] * 2 if d == split else [(size, width)]

    def kernel(own_ref, *refs):
        away_refs, outs = refs[: len(away)], refs[len(away) : len(away) + len(shapes)]
        held_ref, came_ref, own_sems, away_sems = refs[len(away) + len(shapes) :]

        def load_own(i):
            return pltpu.make_async_copy(
                own_ref.at[:, pl.ds(i * sub, sub)], held_ref.at[i], own_sems.at[i]
            )

        def load_away(i):
            return pltpu.make_async_copy(
                away_refs[i // 2].at[:, pl.ds(i % 2 * sub, sub)], came_ref.at[i], away_sems.at[i]
            )

        for i in range(subs):
            load_own(i).start()
            load_away(i).start()
        for i in range(subs):
            load_own(i).wait()
            load_away(i).wait()
            for part in range(0, sub, step):
                first = i * sub + part
                total = plus(
                    held_ref[i, :, part : part + step], came_ref[i, :, part : part + step]
                ).astype(BF16)
                place_at = 0
                for d in range(blocks):
                    piece = total[d * size : (d + 1) * size]
                    if d == split:
                        side, at = divmod(first, half)
                        outs[place_at + side][:, at : at + step] = piece
                        place_at += 2
                    else:
                        outs[place_at][:, first : first + step] = piece
                        place_at += 1

    return call(
        kernel,
        name,
        [whole(shape, BF16) for shape in shapes],
        (own, *away),
        [HBM] * (1 + len(away)),
        after,
        limit=CHIP_LIMIT,
        scratch_shapes=[
            pltpu.VMEM((subs, own.shape[0], sub), BF16),
            pltpu.VMEM((subs, own.shape[0], sub), BF16),
            pltpu.SemaphoreType.DMA((subs,)),
            pltpu.SemaphoreType.DMA((subs,)),
        ],
    )


def turn_narrow(keep, landed, after=()):
    width = keep.shape[1]

    def kernel(keep_ref, landed_ref, *refs):
        total = plus(keep_ref[...], landed_ref[...]).astype(BF16)
        for d, ref in enumerate(refs):
            ref[...] = total[d * 32 : (d + 1) * 32]

    return call(
        kernel, "turn_narrow", [whole((32, width), BF16)] * 4, (keep, landed), after=after
    )


def near_rest(right, left, after=()):
    half = right.shape[1] // 2

    def kernel(right_ref, left_ref, to_right_ref, to_left_ref):
        to_right_ref[...] = right_ref[:, half:]
        to_left_ref[...] = left_ref[:, :half]

    return call(
        kernel, "near_rest", [whole((64, half), BF16)] * 2, (right, left), after=after
    )


def near(right, left, far_right, far_left, after=()):
    half = right.shape[1] // 2

    def kernel(right_ref, left_ref, far_right_ref, far_left_ref, to_right_ref, to_left_ref):
        to_right_ref[...] = plus(right_ref[:, :half], far_right_ref[...]).astype(BF16)
        to_left_ref[...] = plus(left_ref[:, half:], far_left_ref[...]).astype(BF16)

    return call(
        kernel,
        "near",
        [whole((64, half), BF16)] * 2,
        (right, left, far_right, far_left),
        after=after,
    )


def turn_wide(here, from_left, from_right, after=()):
    width = here.shape[1]
    half = width // 2

    def kernel(here_ref, *refs):
        left_near, left_rest, right_near, right_rest, keep_ref, send_ref, rest_ref = refs
        low = plus(here_ref[:, :half], left_near[...], right_rest[...])
        high = plus(here_ref[:, half:], left_rest[...], right_near[...])
        keep_ref[:, :half] = low[:32]
        keep_ref[:, half:] = high[:32]
        send_ref[:, :half] = low[32:].astype(BF16)
        send_ref[:, half:] = high[32:, : CUT - half].astype(BF16)
        rest_ref[...] = high[32:, CUT - half :].astype(BF16)

    return call(
        kernel,
        "turn_wide",
        [whole((32, width), F32), whole((32, CUT), BF16), whole((32, width - CUT), BF16)],
        (here, *from_left, *from_right),
        after=after,
    )


def add_parts(parts, after=(), dtype=BF16):
    def kernel(*refs):
        refs[-1][...] = plus(*[ref[...] for ref in refs[:-1]]).astype(dtype)

    return call(kernel, "add_parts", [whole(parts[0].shape, dtype)], parts, after=after)


def lanes(rows):
    return lax.broadcasted_iota(jnp.int32, (rows, 128), 1)


def slot_columns(slot_ref):
    row = slot_ref[...].astype(F32)
    return jnp.broadcast_to(row, (128, 512)).T.astype(jnp.int32)


def resident_slot(slot, target_ref):
    for k in range(CHIPS):
        slot = jnp.where(slot == target_ref[k], -1, slot)
    return slot


def shrink_kernel(x_ref, down_ref, slot_ref, target_ref, maps_ref, out_ref):
    x = x_ref[...]
    row = lax.broadcasted_iota(jnp.int32, (512, 512), 0)
    col = lax.broadcasted_iota(jnp.int32, (512, 512), 1)
    source = jnp.where(col < 256, 2 * col, 2 * (col - 256) + 1)
    chooser = jnp.where(row == source, 1.0, 0.0).astype(BF16)
    split = jnp.dot(x, chooser, preferred_element_type=F32).astype(BF16)
    even, odd = split[:, :256], split[:, 256:]
    slot = slot_columns(slot_ref)
    kept = resident_slot(slot, target_ref)
    high = (lanes(512) >= RANK).astype(jnp.int32)
    acc = jnp.zeros((512, 128), F32)
    for k in range(0, CHIPS, 2):
        resident = jnp.dot(
            x, down_ref[:, k * 128 : (k + 2) * 128], preferred_element_type=F32
        )
        maps = jnp.concatenate([maps_ref[2 * k], maps_ref[2 * k + 2]], axis=1)
        of_even = jnp.dot(even, maps, preferred_element_type=F32)
        of_odd = jnp.dot(odd, maps, preferred_element_type=F32)
        for i in range(2):
            cols = slice(i * 128, (i + 1) * 128)
            acc += jnp.where(kept == 2 * (k + i) + high, resident[:, cols], 0.0)
            part = jnp.where(high == 0, of_even[:, cols], of_odd[:, cols])
            acc += jnp.where(slot == target_ref[k + i], part, 0.0)
    acc = acc + pltpu.roll(acc, RANK, 1)
    out_ref[...] = jnp.where(lanes(256) < RANK, acc[:256], acc[256:]).astype(BF16)


def shrink_part(x, down, slot, target, maps, after=()):
    return call(
        shrink_kernel,
        "shrink_part",
        [whole((256, 128), BF16)],
        (x, down, slot, target, maps),
        [VM, VM, VM, SM, VM],
        after,
    )


def up_table_kernel(up_ref, target_ref, maps_ref, table_ref):
    table_ref[...] = up_ref[...]
    row = lax.broadcasted_iota(jnp.int32, (256, 512), 0)
    col = lax.broadcasted_iota(jnp.int32, (256, 512), 1)
    to_even = jnp.where(col == 2 * row, 1.0, 0.0).astype(BF16)
    to_odd = jnp.where(col == 2 * row + 1, 1.0, 0.0).astype(BF16)
    turn = (((0,), (0,)), ((), ()))
    for k in range(CHIPS):
        maps = maps_ref[2 * k + 1]
        even = lax.dot_general(maps, to_even, turn, preferred_element_type=F32)
        odd = lax.dot_general(maps, to_odd, turn, preferred_element_type=F32)
        table_ref[rows_at(target_ref[k], RANK), :] = (even[:RANK] + odd[RANK:]).astype(BF16)


def up_table(up, target, maps, after=()):
    return call(
        up_table_kernel, "up_table", [whole((1024, 512), BF16)], (up, target, maps), [VM, SM, VM], after
    )


def raise_kernel(mine_ref, other_ref, table_ref, slot_ref, out_ref):
    packed = (mine_ref[...].astype(F32) + other_ref[...].astype(F32)).astype(BF16).astype(F32)
    turned = pltpu.roll(packed, RANK, 1)
    left = lanes(256) < RANK
    both = jnp.concatenate(
        [jnp.where(left, packed, turned), jnp.where(left, turned, packed)], axis=0
    )
    slot = slot_columns(slot_ref)
    high = (lanes(512) >= RANK).astype(jnp.int32)
    raised = jnp.concatenate(
        [jnp.where(slot == 2 * j + high, both, 0.0).astype(BF16) for j in range(CHIPS)], axis=1
    )
    total = jnp.dot(raised, table_ref[...], preferred_element_type=F32)
    out_ref[...] = (SCALE * total).astype(BF16).reshape(16, 32, 512)


def raise_features(mine, other, table, slot, after=()):
    return call(
        raise_kernel,
        "raise_features",
        [whole((16, 32, 512), BF16)],
        (mine, other, table, slot),
        after=after,
    )


def finish_kernel(
    residual_ref, wide_ref, wide_y_ref, rest_y_ref, narrow_ref, delta_ref, out_ref
):
    for t in range(16):
        cols = slice(t * 512, (t + 1) * 512)
        if (t + 1) * 512 <= WIDE:
            if (t + 1) * 512 <= CUT:
                other = wide_y_ref[:, cols]
            else:
                other = rest_y_ref[:, t * 512 - CUT : (t + 1) * 512 - CUT]
            base = wide_ref[:, cols] + other.astype(F32)
        else:
            part = slice(t * 512 - WIDE, (t + 1) * 512 - WIDE)
            base = narrow_ref[:, part]
        out_ref[:, cols] = (
            residual_ref[:, cols].astype(F32) + base + delta_ref[t].astype(F32)
        ).astype(BF16)


def local(
    attention_output,
    output_projection_weight,
    residual,
    resident_down_maps,
    resident_up_maps,
    fresh_adapter_bundle,
    fresh_slot_targets,
    request_adapter_slot,
):
    x, w = attention_output, output_projection_weight
    slot = request_adapter_slot.reshape(1, 512)
    target = fresh_slot_targets

    maps = lax.all_to_all(
        fresh_adapter_bundle.reshape(16, 256, 128), "tp", split_axis=0, concat_axis=0, tiled=True
    )
    narrow = x.shape[0] * 16 - WIDE
    *narrow_away, narrow_own, mark = product(x, w, Y_MAJOR, WIDE, narrow, NARROW_CHUNK)
    narrow_in = [send(away, 0, 0, 1) for away in narrow_away]
    *wide_away, wide_own, mark = product(x, w, X_MAJOR, 0, WIDE, WIDE_CHUNK, [mark])
    wide_in = [send(away, 0, 0, 1) for away in wide_away]

    keep, away, mark = chip_sum(
        "chip_narrow", narrow_own, narrow_in, 2, None, [maps]
    )
    narrow_y = send(away, 1, 0, 0)
    here, right, far_right, far_left, left, mark = chip_sum(
        "chip_wide", wide_own, wide_in, 4, 2, [away]
    )
    far_right, far_left = send(far_right, 0, 1, 0), send(far_left, 0, 3, 0)

    part, mark = shrink_part(x, resident_down_maps, slot, target, maps, [mark])
    part_in = send(part, 0, 0, 1)
    part, mark = add_parts([part, part_in], [mark])
    part_in = trade(part, lambda x: x ^ 1)
    near_right, near_left, mark = near(right, left, far_right, far_left, [mark])
    part, mark = add_parts([part, part_in], [mark])
    part_in = trade(part, lambda x: 3 - x)
    rest_right, rest_left, mark = near_rest(right, left, [mark])
    rest_right, rest_left = send(rest_right, 0, 1, 0), send(rest_left, 0, 3, 0)
    part, mark = add_parts([part, part_in], [mark])
    other = send(part, 1, 0, 0)

    near_right, near_left = send(near_right, 0, 1, 0), send(near_left, 0, 3, 0)
    table, mark = up_table(resident_up_maps, target, maps, [mark])
    raised, mark = raise_features(part, other, table, slot, [mark])
    *low, mark = turn_narrow(keep, narrow_y, [mark])
    low_in = [send(low[d], 0, d, 0) for d in (1, 2, 3)]
    wide_keep, wide_send, wide_rest, mark = turn_wide(
        here, (near_right, rest_right), (near_left, rest_left), [mark]
    )
    delta = lax.all_to_all(raised, "tp", split_axis=0, concat_axis=0, tiled=True)
    wide_y = send(wide_send, 1, 0, 0)
    rest_y = send(wide_rest, 1, 0, 0)
    narrow_sum, mark = add_parts([low[0], *low_in], [mark], F32)
    hidden, _ = call(
        finish_kernel,
        "finish",
        [whole((32, 8192), BF16)],
        (residual, wide_keep, wide_y, rest_y, narrow_sum, delta),
    )
    return hidden


def solution(mesh):
    return jax.shard_map(
        local,
        mesh=mesh,
        in_specs=(
            P("grp", "tp"),
            P("tp", None),
            P("tp", "grp"),
            P("tp", "grp"),
            P("grp", "tp"),
            P(("grp", "tp"), None, None),
            P("grp"),
            P("grp"),
        ),
        out_specs=P("tp", "grp"),
        check_vma=False,
    )
```

```python
import jax
import jax.numpy as jnp
from jax import lax
from jax.experimental import pallas as pl
from jax.experimental.pallas import tpu as pltpu
from jax.sharding import PartitionSpec as P

RANK = 64
SLOTS = 16
CHIPS = 8
SCALE = 0.5
F32 = jnp.float32
BF16 = jnp.bfloat16
WIDE = 4608
CUT = 2560
VMEM_LIMIT = 16 * 1024 * 1024
PRODUCT_LIMIT = 56 * 1024 * 1024
CHIP_LIMIT = 48 * 1024 * 1024
NARROW_CHUNK = 1792
WIDE_CHUNK = 1536


def place(y, x, core):
    return ((y % 2) * 4 + x % 4) * 2 + core % 2


def route(yy, xx, cc):
    return [
        (place(y, x, c), place(y + yy, x + xx, c + cc))
        for y in range(2)
        for x in range(4)
        for c in range(2)
    ]


def send(array, yy, xx, cc):
    return lax.ppermute(array, "tp", route(yy, xx, cc))


def trade(array, partner_of):
    pairs = [
        (place(y, x, c), place(y, partner_of(x), c))
        for y in range(2)
        for x in range(4)
        for c in range(2)
    ]
    return lax.ppermute(array, "tp", pairs)


def spot():
    t = lax.axis_index("tp")
    return t // 8, lax.rem(t // 2, 4), lax.rem(t, 2)


def partner(yy, xx, cc):
    y, x, c = spot()
    return (lax.rem(y + yy, 2) * 4 + lax.rem(x + xx, 4)) * 2 + lax.rem(c + cc, 2)


def rows_at(index, size):
    return pl.ds(pl.multiple_of(index * size, size), size)


def whole(shape, dtype):
    return jax.ShapeDtypeStruct(shape, dtype)


def plus(a, *others):
    total = a.astype(F32)
    for other in others:
        total = total + other.astype(F32)
    return total


VM = pl.BlockSpec(memory_space=pltpu.VMEM)
SM = pl.BlockSpec(memory_space=pltpu.SMEM)
LATER = pl.BlockSpec(memory_space=pl.ANY)


def call(kernel, name, out_shape, args, specs=None, after=(), limit=VMEM_LIMIT, out_specs=None, scratch_shapes=()):
    count, outs = len(args), len(out_shape)

    def body(*refs):
        results = refs[count + len(after) :]
        results[outs][...] = jnp.zeros((8, 128), F32)
        kernel(*refs[:count], *results[:outs], *results[outs + 1 :])

    return pl.pallas_call(
        body,
        in_specs=list(specs or [VM] * count) + [LATER] * len(after),
        out_specs=list(out_specs or [VM] * outs) + [VM],
        out_shape=list(out_shape) + [whole((8, 128), F32)],
        scratch_shapes=list(scratch_shapes),
        compiler_params=pltpu.CompilerParams(vmem_limit_bytes=limit),
        cost_estimate=pl.CostEstimate(flops=1024, bytes_accessed=1024, transcendentals=0),
        name=name,
    )(*args, *after)


X_MAJOR = [(yy, xx) for xx in range(4) for yy in range(2)]
Y_MAJOR = [(yy, xx) for yy in range(2) for xx in range(4)]


HBM = pl.BlockSpec(memory_space=pltpu.HBM)


def product(x, w, order, first, width, chunk, after=()):
    chunks = width // chunk
    sub = chunk // 2
    subs = 2 * chunks

    def kernel(x_ref, w_ref, *refs):
        away_refs = refs[:chunks]
        own_ref, rows_ref, held_ref, done_ref, sems, away_sems, own_sems = refs[chunks:]

        def copy(i):
            cols = pl.ds(pl.multiple_of(first + i * sub, 128), sub)
            return pltpu.make_async_copy(w_ref.at[:, cols], held_ref.at[i], sems.at[i])

        def leave(i):
            return pltpu.make_async_copy(
                done_ref.at[i, :256],
                away_refs[i // 2].at[:, pl.ds(i % 2 * sub, sub)],
                away_sems.at[i],
            )

        def stay(i):
            return pltpu.make_async_copy(
                done_ref.at[i, 256:], own_ref.at[:, pl.ds(i * sub, sub)], own_sems.at[i]
            )

        for i in range(subs):
            copy(i).start()
        for i, (yy, xx) in enumerate(order):
            for cc, top in ((1, 0), (0, 256)):
                rows_ref[top + i * 32 : top + (i + 1) * 32, :] = x_ref[
                    rows_at(partner(yy, xx, cc), 32), :
                ]
        for i in range(subs):
            copy(i).wait()
            done_ref[i] = jnp.dot(
                rows_ref[...], held_ref[i], preferred_element_type=F32
            ).astype(BF16)
            leave(i).start()
            stay(i).start()
        for i in range(subs):
            leave(i).wait()
            stay(i).wait()

    return call(
        kernel,
        "product",
        [whole((256, chunk), BF16)] * chunks + [whole((256, width), BF16)],
        (x, w),
        [VM, HBM],
        after,
        limit=PRODUCT_LIMIT,
        out_specs=[HBM] * (chunks + 1),
        scratch_shapes=[
            pltpu.VMEM((512, 512), BF16),
            pltpu.VMEM((subs, 512, sub), BF16),
            pltpu.VMEM((subs, 512, sub), BF16),
            pltpu.SemaphoreType.DMA((subs,)),
            pltpu.SemaphoreType.DMA((subs,)),
            pltpu.SemaphoreType.DMA((subs,)),
        ],
    )


def chip_sum(name, own, away, blocks, split, after=()):
    chunk = away[0].shape[1]
    sub = chunk // 2
    subs = 2 * len(away)
    width = own.shape[1]
    half = width // 2
    step = 128
    size = own.shape[0] // blocks
    shapes = []
    for d in range(blocks):
        shapes += [(size, half)] * 2 if d == split else [(size, width)]

    def kernel(own_ref, *refs):
        away_refs, outs = refs[: len(away)], refs[len(away) : len(away) + len(shapes)]
        held_ref, came_ref, own_sems, away_sems = refs[len(away) + len(shapes) :]

        def load_own(i):
            return pltpu.make_async_copy(
                own_ref.at[:, pl.ds(i * sub, sub)], held_ref.at[i], own_sems.at[i]
            )

        def load_away(i):
            return pltpu.make_async_copy(
                away_refs[i // 2].at[:, pl.ds(i % 2 * sub, sub)], came_ref.at[i], away_sems.at[i]
            )

        for i in range(subs):
            load_own(i).start()
            load_away(i).start()
        for i in range(subs):
            load_own(i).wait()
            load_away(i).wait()
            for part in range(0, sub, step):
                first = i * sub + part
                total = plus(
                    held_ref[i, :, part : part + step], came_ref[i, :, part : part + step]
                ).astype(BF16)
                place_at = 0
                for d in range(blocks):
                    piece = total[d * size : (d + 1) * size]
                    if d == split:
                        side, at = divmod(first, half)
                        outs[place_at + side][:, at : at + step] = piece
                        place_at += 2
                    else:
                        outs[place_at][:, first : first + step] = piece
                        place_at += 1

    return call(
        kernel,
        name,
        [whole(shape, BF16) for shape in shapes],
        (own, *away),
        [HBM] * (1 + len(away)),
        after,
        limit=CHIP_LIMIT,
        scratch_shapes=[
            pltpu.VMEM((subs, own.shape[0], sub), BF16),
            pltpu.VMEM((subs, own.shape[0], sub), BF16),
            pltpu.SemaphoreType.DMA((subs,)),
            pltpu.SemaphoreType.DMA((subs,)),
        ],
    )


def turn_narrow(keep, landed, after=()):
    width = keep.shape[1]

    def kernel(keep_ref, landed_ref, *refs):
        total = plus(keep_ref[...], landed_ref[...]).astype(BF16)
        for d, ref in enumerate(refs):
            ref[...] = total[d * 32 : (d + 1) * 32]

    return call(
        kernel, "turn_narrow", [whole((32, width), BF16)] * 4, (keep, landed), after=after
    )


def near(right, left, far_right, far_left, after=()):
    half = right.shape[1] // 2

    def kernel(right_ref, left_ref, far_right_ref, far_left_ref, to_right_ref, to_left_ref):
        to_right_ref[:, :half] = plus(right_ref[:, :half], far_right_ref[...]).astype(BF16)
        to_right_ref[:, half:] = right_ref[:, half:]
        to_left_ref[:, :half] = left_ref[:, :half]
        to_left_ref[:, half:] = plus(left_ref[:, half:], far_left_ref[...]).astype(BF16)

    return call(
        kernel, "near", [whole(right.shape, BF16)] * 2, (right, left, far_right, far_left), after=after
    )


def turn_wide(here, from_left, from_right, after=()):
    width = here.shape[1]

    def kernel(here_ref, from_left_ref, from_right_ref, keep_ref, send_ref, rest_ref):
        total = plus(here_ref[...], from_left_ref[...], from_right_ref[...])
        keep_ref[...] = total[:32]
        send_ref[...] = total[32:, :CUT].astype(BF16)
        rest_ref[...] = total[32:, CUT:].astype(BF16)

    return call(
        kernel,
        "turn_wide",
        [whole((32, width), F32), whole((32, CUT), BF16), whole((32, width - CUT), BF16)],
        (here, from_left, from_right),
        after=after,
    )


def add_parts(parts, after=(), dtype=BF16):
    def kernel(*refs):
        refs[-1][...] = plus(*[ref[...] for ref in refs[:-1]]).astype(dtype)

    return call(kernel, "add_parts", [whole(parts[0].shape, dtype)], parts, after=after)


def lanes(rows):
    return lax.broadcasted_iota(jnp.int32, (rows, 128), 1)


def slot_columns(slot_ref):
    row = slot_ref[...].astype(F32)
    return jnp.broadcast_to(row, (128, 512)).T.astype(jnp.int32)


def resident_slot(slot, target_ref):
    for k in range(CHIPS):
        slot = jnp.where(slot == target_ref[k], -1, slot)
    return slot


def shrink_kernel(x_ref, down_ref, slot_ref, target_ref, maps_ref, out_ref):
    x = x_ref[...]
    row = lax.broadcasted_iota(jnp.int32, (512, 512), 0)
    col = lax.broadcasted_iota(jnp.int32, (512, 512), 1)
    source = jnp.where(col < 256, 2 * col, 2 * (col - 256) + 1)
    chooser = jnp.where(row == source, 1.0, 0.0).astype(BF16)
    split = jnp.dot(x, chooser, preferred_element_type=F32).astype(BF16)
    even, odd = split[:, :256], split[:, 256:]
    slot = slot_columns(slot_ref)
    kept = resident_slot(slot, target_ref)
    high = (lanes(512) >= RANK).astype(jnp.int32)
    acc = jnp.zeros((512, 128), F32)
    for k in range(0, CHIPS, 2):
        resident = jnp.dot(
            x, down_ref[:, k * 128 : (k + 2) * 128], preferred_element_type=F32
        )
        maps = jnp.concatenate([maps_ref[2 * k], maps_ref[2 * k + 2]], axis=1)
        of_even = jnp.dot(even, maps, preferred_element_type=F32)
        of_odd = jnp.dot(odd, maps, preferred_element_type=F32)
        for i in range(2):
            cols = slice(i * 128, (i + 1) * 128)
            acc += jnp.where(kept == 2 * (k + i) + high, resident[:, cols], 0.0)
            part = jnp.where(high == 0, of_even[:, cols], of_odd[:, cols])
            acc += jnp.where(slot == target_ref[k + i], part, 0.0)
    acc = acc + pltpu.roll(acc, RANK, 1)
    out_ref[...] = jnp.where(lanes(256) < RANK, acc[:256], acc[256:]).astype(BF16)


def shrink_part(x, down, slot, target, maps, after=()):
    return call(
        shrink_kernel,
        "shrink_part",
        [whole((256, 128), BF16)],
        (x, down, slot, target, maps),
        [VM, VM, VM, SM, VM],
        after,
    )


def up_table_kernel(up_ref, target_ref, maps_ref, table_ref):
    table_ref[...] = up_ref[...]
    row = lax.broadcasted_iota(jnp.int32, (256, 512), 0)
    col = lax.broadcasted_iota(jnp.int32, (256, 512), 1)
    to_even = jnp.where(col == 2 * row, 1.0, 0.0).astype(BF16)
    to_odd = jnp.where(col == 2 * row + 1, 1.0, 0.0).astype(BF16)
    turn = (((0,), (0,)), ((), ()))
    for k in range(CHIPS):
        maps = maps_ref[2 * k + 1]
        even = lax.dot_general(maps, to_even, turn, preferred_element_type=F32)
        odd = lax.dot_general(maps, to_odd, turn, preferred_element_type=F32)
        table_ref[rows_at(target_ref[k], RANK), :] = (even[:RANK] + odd[RANK:]).astype(BF16)


def up_table(up, target, maps, after=()):
    return call(
        up_table_kernel, "up_table", [whole((1024, 512), BF16)], (up, target, maps), [VM, SM, VM], after
    )


def raise_kernel(mine_ref, other_ref, table_ref, slot_ref, out_ref):
    packed = (mine_ref[...].astype(F32) + other_ref[...].astype(F32)).astype(BF16).astype(F32)
    turned = pltpu.roll(packed, RANK, 1)
    left = lanes(256) < RANK
    both = jnp.concatenate(
        [jnp.where(left, packed, turned), jnp.where(left, turned, packed)], axis=0
    )
    slot = slot_columns(slot_ref)
    high = (lanes(512) >= RANK).astype(jnp.int32)
    raised = jnp.concatenate(
        [jnp.where(slot == 2 * j + high, both, 0.0).astype(BF16) for j in range(CHIPS)], axis=1
    )
    total = jnp.dot(raised, table_ref[...], preferred_element_type=F32)
    out_ref[...] = (SCALE * total).astype(BF16).reshape(16, 32, 512)


def raise_features(mine, other, table, slot, after=()):
    return call(
        raise_kernel,
        "raise_features",
        [whole((16, 32, 512), BF16)],
        (mine, other, table, slot),
        after=after,
    )


def finish_kernel(
    residual_ref, wide_ref, wide_y_ref, rest_y_ref, low_ref, narrow_ref, delta_ref, out_ref
):
    for t in range(16):
        cols = slice(t * 512, (t + 1) * 512)
        if (t + 1) * 512 <= WIDE:
            if (t + 1) * 512 <= CUT:
                other = wide_y_ref[:, cols]
            else:
                other = rest_y_ref[:, t * 512 - CUT : (t + 1) * 512 - CUT]
            base = wide_ref[:, cols] + other.astype(F32)
        else:
            part = slice(t * 512 - WIDE, (t + 1) * 512 - WIDE)
            base = plus(low_ref[:, part], narrow_ref[:, part])
        out_ref[:, cols] = (
            residual_ref[:, cols].astype(F32) + base + delta_ref[t].astype(F32)
        ).astype(BF16)


def local(
    attention_output,
    output_projection_weight,
    residual,
    resident_down_maps,
    resident_up_maps,
    fresh_adapter_bundle,
    fresh_slot_targets,
    request_adapter_slot,
):
    x, w = attention_output, output_projection_weight
    slot = request_adapter_slot.reshape(1, 512)
    target = fresh_slot_targets

    maps = lax.all_to_all(
        fresh_adapter_bundle.reshape(16, 256, 128), "tp", split_axis=0, concat_axis=0, tiled=True
    )
    narrow = x.shape[0] * 16 - WIDE
    *narrow_away, narrow_own, mark = product(x, w, Y_MAJOR, WIDE, narrow, NARROW_CHUNK)
    narrow_in = [send(away, 0, 0, 1) for away in narrow_away]
    *wide_away, wide_own, mark = product(x, w, X_MAJOR, 0, WIDE, WIDE_CHUNK, [mark])
    wide_in = [send(away, 0, 0, 1) for away in wide_away]

    keep, away, mark = chip_sum(
        "chip_narrow", narrow_own, narrow_in, 2, None, [maps]
    )
    narrow_y = send(away, 1, 0, 0)
    here, right, far_right, far_left, left, mark = chip_sum(
        "chip_wide", wide_own, wide_in, 4, 2, [away]
    )
    far_right, far_left = send(far_right, 0, 1, 0), send(far_left, 0, 3, 0)

    part, mark = shrink_part(x, resident_down_maps, slot, target, maps, [mark])
    part_in = send(part, 0, 0, 1)
    part, mark = add_parts([part, part_in], [mark])
    part_in = trade(part, lambda x: x ^ 1)
    part, mark = add_parts([part, part_in], [mark])
    part_in = trade(part, lambda x: 3 - x)
    part, mark = add_parts([part, part_in], [mark])
    other = send(part, 1, 0, 0)

    right, left, mark = near(right, left, far_right, far_left, [mark])
    from_left, from_right = send(right, 0, 1, 0), send(left, 0, 3, 0)
    table, mark = up_table(resident_up_maps, target, maps, [mark])
    *low, mark = turn_narrow(keep, narrow_y, [mark])
    low_in = [send(low[d], 0, d, 0) for d in (2, 1, 3)]
    raised, mark = raise_features(part, other, table, slot, [mark])
    delta = lax.all_to_all(raised, "tp", split_axis=0, concat_axis=0, tiled=True)

    wide_keep, wide_send, wide_rest, mark = turn_wide(here, from_left, from_right, [mark])
    wide_y = send(wide_send, 1, 0, 0)
    rest_y = send(wide_rest, 1, 0, 0)
    narrow_sum, mark = add_parts(low_in, [mark], F32)
    hidden, _ = call(
        finish_kernel,
        "finish",
        [whole((32, 8192), BF16)],
        (residual, wide_keep, wide_y, rest_y, low[0], narrow_sum, delta),
    )
    return hidden


def solution(mesh):
    return jax.shard_map(
        local,
        mesh=mesh,
        in_specs=(
            P("grp", "tp"),
            P("tp", None),
            P("tp", "grp"),
            P("tp", "grp"),
            P("grp", "tp"),
            P(("grp", "tp"), None, None),
            P("grp"),
            P("grp"),
        ),
        out_specs=P("tp", "grp"),
        check_vma=False,
    )
```

```python
import jax
import jax.numpy as jnp
from jax import lax
from jax.experimental import pallas as pl
from jax.experimental.pallas import tpu as pltpu
from jax.sharding import PartitionSpec as P

RANK = 64
SLOTS = 16
CHIPS = 8
SCALE = 0.5
F32 = jnp.float32
BF16 = jnp.bfloat16
WIDE = 4608
CUT = 2560
VMEM_LIMIT = 16 * 1024 * 1024
PRODUCT_LIMIT = 56 * 1024 * 1024
CHIP_LIMIT = 48 * 1024 * 1024
NARROW_CHUNK = 1792
WIDE_CHUNK = 1536


def place(y, x, core):
    return ((y % 2) * 4 + x % 4) * 2 + core % 2


def route(yy, xx, cc):
    return [
        (place(y, x, c), place(y + yy, x + xx, c + cc))
        for y in range(2)
        for x in range(4)
        for c in range(2)
    ]


def send(array, yy, xx, cc):
    return lax.ppermute(array, "tp", route(yy, xx, cc))


def trade(array, partner_of):
    pairs = [
        (place(y, x, c), place(y, partner_of(x), c))
        for y in range(2)
        for x in range(4)
        for c in range(2)
    ]
    return lax.ppermute(array, "tp", pairs)


def spot():
    t = lax.axis_index("tp")
    return t // 8, lax.rem(t // 2, 4), lax.rem(t, 2)


def partner(yy, xx, cc):
    y, x, c = spot()
    return (lax.rem(y + yy, 2) * 4 + lax.rem(x + xx, 4)) * 2 + lax.rem(c + cc, 2)


def rows_at(index, size):
    return pl.ds(pl.multiple_of(index * size, size), size)


def whole(shape, dtype):
    return jax.ShapeDtypeStruct(shape, dtype)


def plus(a, *others):
    total = a.astype(F32)
    for other in others:
        total = total + other.astype(F32)
    return total


VM = pl.BlockSpec(memory_space=pltpu.VMEM)
SM = pl.BlockSpec(memory_space=pltpu.SMEM)
LATER = pl.BlockSpec(memory_space=pl.ANY)


def call(kernel, name, out_shape, args, specs=None, after=(), limit=VMEM_LIMIT, out_specs=None, scratch_shapes=()):
    count, outs = len(args), len(out_shape)

    def body(*refs):
        results = refs[count + len(after) :]
        results[outs][...] = jnp.zeros((8, 128), F32)
        kernel(*refs[:count], *results[:outs], *results[outs + 1 :])

    return pl.pallas_call(
        body,
        in_specs=list(specs or [VM] * count) + [LATER] * len(after),
        out_specs=list(out_specs or [VM] * outs) + [VM],
        out_shape=list(out_shape) + [whole((8, 128), F32)],
        scratch_shapes=list(scratch_shapes),
        compiler_params=pltpu.CompilerParams(vmem_limit_bytes=limit),
        cost_estimate=pl.CostEstimate(flops=1024, bytes_accessed=1024, transcendentals=0),
        name=name,
    )(*args, *after)


X_MAJOR = [(yy, xx) for xx in range(4) for yy in range(2)]
Y_MAJOR = [(yy, xx) for yy in range(2) for xx in range(4)]


HBM = pl.BlockSpec(memory_space=pltpu.HBM)


def product(x, w, order, first, width, chunk, after=()):
    chunks = width // chunk
    sub = chunk // 2
    subs = 2 * chunks

    def kernel(x_ref, w_ref, *refs):
        away_refs = refs[:chunks]
        own_ref, rows_ref, held_ref, done_ref, sems, away_sems, own_sems = refs[chunks:]

        def copy(i):
            cols = pl.ds(pl.multiple_of(first + i * sub, 128), sub)
            return pltpu.make_async_copy(w_ref.at[:, cols], held_ref.at[i], sems.at[i])

        def leave(i):
            return pltpu.make_async_copy(
                done_ref.at[i, :256],
                away_refs[i // 2].at[:, pl.ds(i % 2 * sub, sub)],
                away_sems.at[i],
            )

        def stay(i):
            return pltpu.make_async_copy(
                done_ref.at[i, 256:], own_ref.at[:, pl.ds(i * sub, sub)], own_sems.at[i]
            )

        for i in range(subs):
            copy(i).start()
        for i, (yy, xx) in enumerate(order):
            for cc, top in ((1, 0), (0, 256)):
                rows_ref[top + i * 32 : top + (i + 1) * 32, :] = x_ref[
                    rows_at(partner(yy, xx, cc), 32), :
                ]
        for i in range(subs):
            copy(i).wait()
            done_ref[i] = jnp.dot(
                rows_ref[...], held_ref[i], preferred_element_type=F32
            ).astype(BF16)
            leave(i).start()
            stay(i).start()
        for i in range(subs):
            leave(i).wait()
            stay(i).wait()

    return call(
        kernel,
        "product",
        [whole((256, chunk), BF16)] * chunks + [whole((256, width), BF16)],
        (x, w),
        [VM, HBM],
        after,
        limit=PRODUCT_LIMIT,
        out_specs=[HBM] * (chunks + 1),
        scratch_shapes=[
            pltpu.VMEM((512, 512), BF16),
            pltpu.VMEM((subs, 512, sub), BF16),
            pltpu.VMEM((subs, 512, sub), BF16),
            pltpu.SemaphoreType.DMA((subs,)),
            pltpu.SemaphoreType.DMA((subs,)),
            pltpu.SemaphoreType.DMA((subs,)),
        ],
    )


def chip_sum(name, own, away, blocks, split, after=()):
    chunk = away[0].shape[1]
    sub = chunk // 2
    subs = 2 * len(away)
    width = own.shape[1]
    half = width // 2
    step = 128
    size = own.shape[0] // blocks
    shapes = []
    for d in range(blocks):
        shapes += [(size, half)] * 2 if d == split else [(size, width)]

    def kernel(own_ref, *refs):
        away_refs, outs = refs[: len(away)], refs[len(away) : len(away) + len(shapes)]
        held_ref, came_ref, own_sems, away_sems = refs[len(away) + len(shapes) :]

        def load_own(i):
            return pltpu.make_async_copy(
                own_ref.at[:, pl.ds(i * sub, sub)], held_ref.at[i], own_sems.at[i]
            )

        def load_away(i):
            return pltpu.make_async_copy(
                away_refs[i // 2].at[:, pl.ds(i % 2 * sub, sub)], came_ref.at[i], away_sems.at[i]
            )

        for i in range(subs):
            load_own(i).start()
            load_away(i).start()
        for i in range(subs):
            load_own(i).wait()
            load_away(i).wait()
            for part in range(0, sub, step):
                first = i * sub + part
                total = plus(
                    held_ref[i, :, part : part + step], came_ref[i, :, part : part + step]
                ).astype(BF16)
                place_at = 0
                for d in range(blocks):
                    piece = total[d * size : (d + 1) * size]
                    if d == split:
                        side, at = divmod(first, half)
                        outs[place_at + side][:, at : at + step] = piece
                        place_at += 2
                    else:
                        outs[place_at][:, first : first + step] = piece
                        place_at += 1

    return call(
        kernel,
        name,
        [whole(shape, BF16) for shape in shapes],
        (own, *away),
        [HBM] * (1 + len(away)),
        after,
        limit=CHIP_LIMIT,
        scratch_shapes=[
            pltpu.VMEM((subs, own.shape[0], sub), BF16),
            pltpu.VMEM((subs, own.shape[0], sub), BF16),
            pltpu.SemaphoreType.DMA((subs,)),
            pltpu.SemaphoreType.DMA((subs,)),
        ],
    )


def turn_narrow(keep, landed, after=()):
    width = keep.shape[1]

    def kernel(keep_ref, landed_ref, *refs):
        total = plus(keep_ref[...], landed_ref[...]).astype(BF16)
        for d, ref in enumerate(refs):
            ref[...] = total[d * 32 : (d + 1) * 32]

    return call(
        kernel, "turn_narrow", [whole((32, width), BF16)] * 4, (keep, landed), after=after
    )


def near(right, left, far_right, far_left, after=()):
    half = right.shape[1] // 2

    def kernel(right_ref, left_ref, far_right_ref, far_left_ref, to_right_ref, to_left_ref):
        to_right_ref[:, :half] = plus(right_ref[:, :half], far_right_ref[...]).astype(BF16)
        to_right_ref[:, half:] = right_ref[:, half:]
        to_left_ref[:, :half] = left_ref[:, :half]
        to_left_ref[:, half:] = plus(left_ref[:, half:], far_left_ref[...]).astype(BF16)

    return call(
        kernel, "near", [whole(right.shape, BF16)] * 2, (right, left, far_right, far_left), after=after
    )


def turn_wide(here, from_left, from_right, after=()):
    width = here.shape[1]

    def kernel(here_ref, from_left_ref, from_right_ref, keep_ref, send_ref, rest_ref):
        total = plus(here_ref[...], from_left_ref[...], from_right_ref[...])
        keep_ref[...] = total[:32]
        send_ref[...] = total[32:, :CUT].astype(BF16)
        rest_ref[...] = total[32:, CUT:].astype(BF16)

    return call(
        kernel,
        "turn_wide",
        [whole((32, width), F32), whole((32, CUT), BF16), whole((32, width - CUT), BF16)],
        (here, from_left, from_right),
        after=after,
    )


def add_parts(parts, after=(), dtype=BF16):
    def kernel(*refs):
        refs[-1][...] = plus(*[ref[...] for ref in refs[:-1]]).astype(dtype)

    return call(kernel, "add_parts", [whole(parts[0].shape, dtype)], parts, after=after)


def lanes(rows):
    return lax.broadcasted_iota(jnp.int32, (rows, 128), 1)


def slot_columns(slot_ref):
    row = slot_ref[...].astype(F32)
    return jnp.broadcast_to(row, (128, 512)).T.astype(jnp.int32)


def resident_slot(slot, target_ref):
    for k in range(CHIPS):
        slot = jnp.where(slot == target_ref[k], -1, slot)
    return slot


def shrink_kernel(x_ref, down_ref, slot_ref, target_ref, maps_ref, out_ref):
    x = x_ref[...]
    row = lax.broadcasted_iota(jnp.int32, (512, 512), 0)
    col = lax.broadcasted_iota(jnp.int32, (512, 512), 1)
    source = jnp.where(col < 256, 2 * col, 2 * (col - 256) + 1)
    chooser = jnp.where(row == source, 1.0, 0.0).astype(BF16)
    split = jnp.dot(x, chooser, preferred_element_type=F32).astype(BF16)
    even, odd = split[:, :256], split[:, 256:]
    slot = slot_columns(slot_ref)
    kept = resident_slot(slot, target_ref)
    high = (lanes(512) >= RANK).astype(jnp.int32)
    acc = jnp.zeros((512, 128), F32)
    for k in range(0, CHIPS, 2):
        resident = jnp.dot(
            x, down_ref[:, k * 128 : (k + 2) * 128], preferred_element_type=F32
        )
        maps = jnp.concatenate([maps_ref[2 * k], maps_ref[2 * k + 2]], axis=1)
        of_even = jnp.dot(even, maps, preferred_element_type=F32)
        of_odd = jnp.dot(odd, maps, preferred_element_type=F32)
        for i in range(2):
            cols = slice(i * 128, (i + 1) * 128)
            acc += jnp.where(kept == 2 * (k + i) + high, resident[:, cols], 0.0)
            part = jnp.where(high == 0, of_even[:, cols], of_odd[:, cols])
            acc += jnp.where(slot == target_ref[k + i], part, 0.0)
    acc = acc + pltpu.roll(acc, RANK, 1)
    out_ref[...] = jnp.where(lanes(256) < RANK, acc[:256], acc[256:]).astype(BF16)


def shrink_part(x, down, slot, target, maps, after=()):
    return call(
        shrink_kernel,
        "shrink_part",
        [whole((256, 128), BF16)],
        (x, down, slot, target, maps),
        [VM, VM, VM, SM, VM],
        after,
    )


def up_table_kernel(up_ref, target_ref, maps_ref, table_ref):
    table_ref[...] = up_ref[...]
    row = lax.broadcasted_iota(jnp.int32, (256, 512), 0)
    col = lax.broadcasted_iota(jnp.int32, (256, 512), 1)
    to_even = jnp.where(col == 2 * row, 1.0, 0.0).astype(BF16)
    to_odd = jnp.where(col == 2 * row + 1, 1.0, 0.0).astype(BF16)
    turn = (((0,), (0,)), ((), ()))
    for k in range(CHIPS):
        maps = maps_ref[2 * k + 1]
        even = lax.dot_general(maps, to_even, turn, preferred_element_type=F32)
        odd = lax.dot_general(maps, to_odd, turn, preferred_element_type=F32)
        table_ref[rows_at(target_ref[k], RANK), :] = (even[:RANK] + odd[RANK:]).astype(BF16)


def up_table(up, target, maps, after=()):
    return call(
        up_table_kernel, "up_table", [whole((1024, 512), BF16)], (up, target, maps), [VM, SM, VM], after
    )


def raise_kernel(mine_ref, other_ref, table_ref, slot_ref, out_ref):
    packed = (mine_ref[...].astype(F32) + other_ref[...].astype(F32)).astype(BF16).astype(F32)
    turned = pltpu.roll(packed, RANK, 1)
    left = lanes(256) < RANK
    both = jnp.concatenate(
        [jnp.where(left, packed, turned), jnp.where(left, turned, packed)], axis=0
    )
    slot = slot_columns(slot_ref)
    high = (lanes(512) >= RANK).astype(jnp.int32)
    raised = jnp.concatenate(
        [jnp.where(slot == 2 * j + high, both, 0.0).astype(BF16) for j in range(CHIPS)], axis=1
    )
    total = jnp.dot(raised, table_ref[...], preferred_element_type=F32)
    out_ref[...] = (SCALE * total).astype(BF16).reshape(16, 32, 512)


def raise_features(mine, other, table, slot, after=()):
    return call(
        raise_kernel,
        "raise_features",
        [whole((16, 32, 512), BF16)],
        (mine, other, table, slot),
        after=after,
    )


def finish_kernel(
    residual_ref, wide_ref, wide_y_ref, rest_y_ref, low_ref, narrow_ref, delta_ref, out_ref
):
    for t in range(16):
        cols = slice(t * 512, (t + 1) * 512)
        if (t + 1) * 512 <= WIDE:
            if (t + 1) * 512 <= CUT:
                other = wide_y_ref[:, cols]
            else:
                other = rest_y_ref[:, t * 512 - CUT : (t + 1) * 512 - CUT]
            base = wide_ref[:, cols] + other.astype(F32)
        else:
            part = slice(t * 512 - WIDE, (t + 1) * 512 - WIDE)
            base = plus(low_ref[:, part], narrow_ref[:, part])
        out_ref[:, cols] = (
            residual_ref[:, cols].astype(F32) + base + delta_ref[t].astype(F32)
        ).astype(BF16)


def local(
    attention_output,
    output_projection_weight,
    residual,
    resident_down_maps,
    resident_up_maps,
    fresh_adapter_bundle,
    fresh_slot_targets,
    request_adapter_slot,
):
    x, w = attention_output, output_projection_weight
    slot = request_adapter_slot.reshape(1, 512)
    target = fresh_slot_targets

    maps = lax.all_to_all(
        fresh_adapter_bundle.reshape(16, 256, 128), "tp", split_axis=0, concat_axis=0, tiled=True
    )
    narrow = x.shape[0] * 16 - WIDE
    *narrow_away, narrow_own, mark = product(x, w, Y_MAJOR, WIDE, narrow, NARROW_CHUNK)
    narrow_in = [send(away, 0, 0, 1) for away in narrow_away]
    *wide_away, wide_own, mark = product(x, w, X_MAJOR, 0, WIDE, WIDE_CHUNK, [mark])
    wide_in = [send(away, 0, 0, 1) for away in wide_away]

    keep, away, mark = chip_sum(
        "chip_narrow", narrow_own, narrow_in, 2, None, [maps]
    )
    narrow_y = send(away, 1, 0, 0)
    here, right, far_right, far_left, left, mark = chip_sum(
        "chip_wide", wide_own, wide_in, 4, 2, [away]
    )
    far_right, far_left = send(far_right, 0, 1, 0), send(far_left, 0, 3, 0)

    part, mark = shrink_part(x, resident_down_maps, slot, target, maps, [mark])
    part_in = send(part, 0, 0, 1)
    part, mark = add_parts([part, part_in], [mark])
    part_in = trade(part, lambda x: x ^ 1)
    part, mark = add_parts([part, part_in], [mark])
    part_in = trade(part, lambda x: 3 - x)
    part, mark = add_parts([part, part_in], [mark])
    other = send(part, 1, 0, 0)

    right, left, mark = near(right, left, far_right, far_left, [mark])
    from_left, from_right = send(right, 0, 1, 0), send(left, 0, 3, 0)
    table, mark = up_table(resident_up_maps, target, maps, [mark])
    raised, mark = raise_features(part, other, table, slot, [mark])
    *low, mark = turn_narrow(keep, narrow_y, [mark])
    low_in = [send(low[d], 0, d, 0) for d in (2, 1, 3)]
    delta = lax.all_to_all(raised, "tp", split_axis=0, concat_axis=0, tiled=True)

    wide_keep, wide_send, wide_rest, mark = turn_wide(here, from_left, from_right, [mark])
    wide_y = send(wide_send, 1, 0, 0)
    rest_y = send(wide_rest, 1, 0, 0)
    narrow_sum, mark = add_parts(low_in, [mark], F32)
    hidden, _ = call(
        finish_kernel,
        "finish",
        [whole((32, 8192), BF16)],
        (residual, wide_keep, wide_y, rest_y, low[0], narrow_sum, delta),
    )
    return hidden


def solution(mesh):
    return jax.shard_map(
        local,
        mesh=mesh,
        in_specs=(
            P("grp", "tp"),
            P("tp", None),
            P("tp", "grp"),
            P("tp", "grp"),
            P("grp", "tp"),
            P(("grp", "tp"), None, None),
            P("grp"),
            P("grp"),
        ),
        out_specs=P("tp", "grp"),
        check_vma=False,
    )
```
